128 devices in a mesh: dev: 128 (over y, z, x, core).
Axes of the slice: x: 4, y: 4, z: 4, core: 2. Of those that a mesh axis runs over, the one named last changes fastest.
Arguments:
- params: float32 [59, 524288], P(None, 'dev'), may hold values from -40 to 40, as said below
- moment_one: float32 [59, 524288], P(None, 'dev'), may hold values from -3 to 3
- moment_two: float32 [59, 524288], P(None, 'dev'), may hold values from 0.01 to 1
- visible: int32 [2048, 512], P('dev'), may hold values from -1 to 524287, as said below
- counts: int32 [2048, 4], P('dev'), may hold values from 0 to 128, as said below
- tile_pos: int32 [2048], P('dev'), may hold values from 0 to 2047, as said below
- target: bfloat16 [2048, 3, 256], P('dev'), may hold values from 0 to 1
Outputs:
- tile_loss: float32 [2048], P('dev')
- new_params: float32 [59, 524288], P(None, 'dev')
- new_moment_one: float32 [59, 524288], P(None, 'dev')
- new_moment_two: float32 [59, 524288], P(None, 'dev')
The draws below stay inside these ranges and needn't reach their ends.
Inputs may be any that keep to these rules, and one draw needn't show every extreme that they name: `visible`: row r holds the ids of the Gaussians that tile r composites, in compositing order; slot j is live when j % 128 < counts[r, j // 128], and a dead slot holds -1. Gaussian i is owned by device i // 4096. Among the live slots of the rows of one device at most 64 distinct ids belong to one owner, and on every device some owner has exactly 64. `counts`: the live slots of a row come first: block 0 holds 128, every block before a row's last live block holds 128 and every block after it 0. A permutation: rendered tile r is the screen tile in column tile_pos[r] % 64 and row tile_pos[r] // 64 of tiles. `params`: row 2 lies between 3 and 30.
All inputs are finite; a program needn't handle non-finite values.
Results may differ from the reference program's by a relative error of at most 0.0003.
Values sent between devices are 32-bit elements; how exact they have to be, the bound alone decides.
No kernel may reach another device: no remote copies, remote signals or barrier semaphores. Data moves between devices by JAX's collectives and lax.ppermute only.
A program may use at most 192 MiB of HBM per device.

```python
import math
import jax
import jax.numpy as jnp
from jax import lax

PARAMS = 59
G_DEV = 4096
TILE_DEV = 16
BLOCKS = 4
TILES_X = 64
ADAM_STEP = 1000
TILES = 2048
GAUSS = 524288
CAP = 64
N_DEV = 128


def layout(key):
    subkeys = jax.random.split(key, 6)
    tile_pos = jax.random.permutation(subkeys[0], TILES).astype(jnp.int32)
    level_dev = jax.random.randint(subkeys[1], (N_DEV, 1), 1, BLOCKS + 1, dtype=jnp.int32)
    extra_len = jax.random.randint(subkeys[2], (N_DEV, TILE_DEV), 0, 1 << 20, dtype=jnp.int32)
    lengths = 128 + extra_len % (128 * (level_dev - 1) + 1)
    take_count = jax.random.randint(subkeys[3], (N_DEV, N_DEV), 1, CAP + 1, dtype=jnp.int32)
    busiest = jax.random.randint(subkeys[4], (N_DEV, 1), 0, N_DEV, dtype=jnp.int32)
    start_at = jax.random.randint(subkeys[5], (N_DEV, N_DEV), 0, G_DEV, dtype=jnp.int32)
    owner_col = jnp.arange(N_DEV, dtype=jnp.int32)[None, :]
    take_count = jnp.where(owner_col == busiest, CAP, take_count)
    rank_owner = (busiest + owner_col) % N_DEV
    take_sorted = jnp.take_along_axis(take_count, rank_owner, axis=1)
    start_sorted = jnp.take_along_axis(start_at, rank_owner, axis=1)
    within = jnp.arange(CAP, dtype=jnp.int32)
    ids_all = rank_owner[:, :, None] * G_DEV + (start_sorted[:, :, None] + within[None, None, :] * (G_DEV // CAP)) % G_DEV
    live_all = within[None, None, :] < take_sorted[:, :, None]
    ids_all = ids_all.reshape(N_DEV, N_DEV * CAP)
    live_all = live_all.reshape(N_DEV, N_DEV * CAP).astype(jnp.int32)
    packing = jnp.argsort(1 - live_all, axis=1, stable=True)
    working = jnp.take_along_axis(ids_all, packing, axis=1)
    set_size = jnp.sum(live_all, axis=1)
    slot_index = jnp.arange(BLOCKS * 128, dtype=jnp.int32)
    offsets = jnp.cumsum(lengths, axis=1) - lengths
    counter = offsets[:, :, None] + slot_index[None, None, :]
    pick_index = (counter % set_size[:, None, None]).reshape(N_DEV, TILE_DEV * BLOCKS * 128)
    visible = jnp.take_along_axis(working, pick_index, axis=1).reshape(N_DEV, TILE_DEV, BLOCKS * 128)
    visible = jnp.where(slot_index[None, None, :] < lengths[:, :, None], visible, -1).reshape(TILES, BLOCKS * 128)
    counts = jnp.clip(lengths[:, :, None] - 128 * jnp.arange(BLOCKS, dtype=jnp.int32)[None, None, :], 0, 128)
    return (tile_pos, visible.astype(jnp.int32), counts.reshape(TILES, BLOCKS).astype(jnp.int32))


def draw_tile_pos(key, part):
    tile_pos, visible, counts = layout(key)
    return tile_pos


def draw_visible(key, part):
    tile_pos, visible, counts = layout(key)
    return visible


def draw_counts(key, part):
    tile_pos, visible, counts = layout(key)
    return counts


def draw_params(key, part):
    tile_pos, visible, counts = layout(key)
    key = jax.random.fold_in(key, 11)
    subkeys = jax.random.split(key, 9)
    row_index = jnp.broadcast_to(jnp.arange(TILES, dtype=jnp.int32)[:, None], visible.shape)
    segment = jnp.where(visible >= 0, visible, GAUSS).reshape(-1)
    home_row = jax.ops.segment_min(row_index.reshape(-1), segment, num_segments=GAUSS + 1)[:GAUSS]
    spare_row = jax.random.randint(subkeys[0], (GAUSS,), 0, TILES, dtype=jnp.int32)
    home_row = jnp.where((home_row >= 0) & (home_row < TILES), home_row, spare_row)
    screen_tile = tile_pos[home_row]
    screen_width = TILES_X * 16.0
    screen_height = TILES // TILES_X * 16.0
    focal = 1.2 * screen_width
    centre_x = (screen_tile % TILES_X).astype(jnp.float32) * 16.0 + 8.0 + jax.random.uniform(subkeys[1], (GAUSS,), jnp.float32, -8.0, 8.0)
    centre_y = (screen_tile // TILES_X).astype(jnp.float32) * 16.0 + 8.0 + jax.random.uniform(subkeys[2], (GAUSS,), jnp.float32, -8.0, 8.0)
    depths = jnp.exp(jax.random.uniform(subkeys[3], (GAUSS,), jnp.float32, jnp.log(3.0), jnp.log(30.0)))
    mean_x = (centre_x - 0.5 * screen_width) * depths / focal
    mean_y = (centre_y - 0.5 * screen_height) * depths / focal
    size_px = jnp.exp(jax.random.uniform(subkeys[4], (GAUSS,), jnp.float32, jnp.log(2.0), jnp.log(8.0)))
    log_scales = jnp.log(size_px * depths / focal)[None, :] + 0.3 * jax.random.normal(subkeys[5], (3, GAUSS), jnp.float32)
    quats = jnp.clip(jax.random.normal(subkeys[6], (4, GAUSS), jnp.float32), -4.0, 4.0)
    row_scale = jnp.where(jnp.arange(48) < 3, 1.0, 0.25).astype(jnp.float32)[:, None]
    logits = jax.random.uniform(subkeys[7], (1, GAUSS), jnp.float32, -6.5, -3.0)
    colour_rows = row_scale * jnp.clip(jax.random.normal(subkeys[8], (48, GAUSS), jnp.float32), -4.0, 4.0)
    return jnp.concatenate([mean_x[None], mean_y[None], depths[None], log_scales, quats, logits, colour_rows], axis=0).astype(jnp.float32)


def level_of(own_key, shape, cuts, smallest, top_value):
    gain, own = 1.0, jax.random.fold_in(own_key, 6)
    for dim, parts in cuts:
        draws = jnp.exp(jax.random.uniform(jax.random.fold_in(own, dim), (parts,), jnp.float32, smallest / len(cuts), top_value / len(cuts)))
        gain = gain * jnp.repeat(draws, shape[dim] // parts).reshape([-1 if axis == dim else 1 for axis in range(len(shape))])
    return gain


def centred(own_key, dims, width, most, cuts=(), kind=jnp.bfloat16):
    factor_of = level_of(own_key, dims, cuts, -0.22, 0.18) if cuts else 1.0
    result = jax.random.normal(own_key, dims, jnp.float32) * width * factor_of
    return jnp.minimum(jnp.maximum(result, -most), most).astype(kind)


def setup_inputs(seed: int = 0) -> dict:
    seeds = jax.random.split(jax.random.key(seed), 8)
    return {
        "params": draw_params(jax.random.fold_in(seeds[7], 71), 0),
        "moment_one": centred(seeds[1], (PARAMS, GAUSS), 0.5, 3.0, ((1, 128),), jnp.float32),
        "moment_two": jnp.clip(jnp.exp(math.log(1.0) - 4.6051702 * jax.random.uniform(seeds[2], (PARAMS, GAUSS), jnp.float32) ** level_of(seeds[2], (PARAMS, GAUSS), ((1, 128),), -0.2, 0.2)), 0.01, 1.0),
        "visible": draw_visible(jax.random.fold_in(seeds[7], 71), 0),
        "counts": draw_counts(jax.random.fold_in(seeds[7], 71), 0),
        "tile_pos": draw_tile_pos(jax.random.fold_in(seeds[7], 71), 0),
        "target": jnp.clip(1.0 * jax.random.uniform(seeds[6], (TILES, 3, 256), jnp.float32) ** level_of(seeds[6], (TILES, 3, 256), ((0, 128),), -0.2, 0.2), 0.0, 1.0).astype(jnp.bfloat16),
    }


SH_ZERO = 0.28209479177387814
SH_ONE = 0.4886025119029199
SH_TWO = (1.0925484305920792, -1.0925484305920792, 0.31539156525252005, -1.0925484305920792, 0.5462742152960396)
SH_THREE = (-0.5900435899266435, 2.890611442640554, -0.4570457994644658, 0.3731763325901154, -0.4570457994644658, 1.445305721320277, -0.5900435899266435)
BETA_ONE = 0.9
BETA_TWO = 0.999
ADAM_EPS = 1e-15

def harmonics(dir_x, dir_y, dir_z):
    sq_x = dir_x * dir_x
    sq_y = dir_y * dir_y
    sq_z = dir_z * dir_z
    return [SH_ZERO * jnp.ones_like(dir_x), -SH_ONE * dir_y, SH_ONE * dir_z, -SH_ONE * dir_x, SH_TWO[0] * dir_x * dir_y, SH_TWO[1] * dir_y * dir_z, SH_TWO[2] * (2.0 * sq_z - sq_x - sq_y), SH_TWO[3] * dir_x * dir_z, SH_TWO[4] * (sq_x - sq_y), SH_THREE[0] * dir_y * (3.0 * sq_x - sq_y), SH_THREE[1] * dir_x * dir_y * dir_z, SH_THREE[2] * dir_y * (4.0 * sq_z - sq_x - sq_y), SH_THREE[3] * dir_z * (2.0 * sq_z - 3.0 * sq_x - 3.0 * sq_y), SH_THREE[4] * dir_x * (4.0 * sq_z - sq_x - sq_y), SH_THREE[5] * dir_z * (sq_x - sq_y), SH_THREE[6] * dir_x * (sq_x - 3.0 * sq_y)]

def project(param_rows, screen_width, screen_height):
    mean_x, mean_y, depths = (param_rows[0], param_rows[1], param_rows[2])
    scale_x = jnp.exp(param_rows[3])
    scale_y = jnp.exp(param_rows[4])
    scale_z = jnp.exp(param_rows[5])
    quat_len = jnp.maximum(jnp.sqrt(param_rows[6] ** 2 + param_rows[7] ** 2 + param_rows[8] ** 2 + param_rows[9] ** 2), 0.5)
    quat_w = param_rows[6] / quat_len
    quat_x = param_rows[7] / quat_len
    quat_y = param_rows[8] / quat_len
    quat_z = param_rows[9] / quat_len
    rot_xx = 1.0 - 2.0 * (quat_y * quat_y + quat_z * quat_z)
    rot_xy = 2.0 * (quat_x * quat_y - quat_w * quat_z)
    rot_xz = 2.0 * (quat_x * quat_z + quat_w * quat_y)
    rot_yx = 2.0 * (quat_x * quat_y + quat_w * quat_z)
    rot_yy = 1.0 - 2.0 * (quat_x * quat_x + quat_z * quat_z)
    rot_yz = 2.0 * (quat_y * quat_z - quat_w * quat_x)
    rot_zx = 2.0 * (quat_x * quat_z - quat_w * quat_y)
    rot_zy = 2.0 * (quat_y * quat_z + quat_w * quat_x)
    rot_zz = 1.0 - 2.0 * (quat_x * quat_x + quat_y * quat_y)
    m_xx, m_xy, m_xz = (rot_xx * scale_x, rot_xy * scale_y, rot_xz * scale_z)
    m_yx, m_yy, m_yz = (rot_yx * scale_x, rot_yy * scale_y, rot_yz * scale_z)
    m_zx, m_zy, m_zz = (rot_zx * scale_x, rot_zy * scale_y, rot_zz * scale_z)
    cov_xx = m_xx * m_xx + m_xy * m_xy + m_xz * m_xz
    cov_xy = m_xx * m_yx + m_xy * m_yy + m_xz * m_yz
    cov_xz = m_xx * m_zx + m_xy * m_zy + m_xz * m_zz
    cov_yy = m_yx * m_yx + m_yy * m_yy + m_yz * m_yz
    cov_yz = m_yx * m_zx + m_yy * m_zy + m_yz * m_zz
    cov_zz = m_zx * m_zx + m_zy * m_zy + m_zz * m_zz
    focal = 1.2 * screen_width
    inverse = 1.0 / depths
    jac_xx = focal * inverse
    jac_xz = -focal * mean_x * inverse * inverse
    jac_yy = focal * inverse
    jac_yz = -focal * mean_y * inverse * inverse
    plane_a = jac_xx * jac_xx * cov_xx + 2.0 * jac_xx * jac_xz * cov_xz + jac_xz * jac_xz * cov_zz + 0.3
    plane_b = jac_xx * jac_yy * cov_xy + jac_xx * jac_yz * cov_xz + jac_xz * jac_yy * cov_yz + jac_xz * jac_yz * cov_zz
    plane_c = jac_yy * jac_yy * cov_yy + 2.0 * jac_yy * jac_yz * cov_yz + jac_yz * jac_yz * cov_zz + 0.3
    determ = plane_a * plane_c - plane_b * plane_b
    screen_u = focal * mean_x * inverse + 0.5 * screen_width
    screen_v = focal * mean_y * inverse + 0.5 * screen_height
    distance = jnp.sqrt(mean_x * mean_x + mean_y * mean_y + depths * depths)
    basis = harmonics(mean_x / distance, mean_y / distance, depths / distance)
    colours = []
    for channel in range(3):
        total = 0.5 + basis[0] * param_rows[11 + channel]
        for degree in range(1, 16):
            total = total + basis[degree] * param_rows[11 + 3 * degree + channel]
        colours.append(total)
    return jnp.stack([screen_u, screen_v, plane_c / determ, -plane_b / determ, plane_a / determ, jax.nn.sigmoid(param_rows[10]), colours[0], colours[1], colours[2]])

def pixel_coords(tile_pos):
    offset = jnp.arange(256, dtype=jnp.int32)
    pix_x = (tile_pos % TILES_X)[:, None] * 16 + (offset % 16)[None, :]
    pix_y = (tile_pos // TILES_X)[:, None] * 16 + (offset // 16)[None, :]
    return (pix_x.astype(jnp.float32), pix_y.astype(jnp.float32))

def opacities(features, slot_live, pix_x, pix_y):
    delta_x = pix_x[:, :, None] - features[0][:, None, :]
    delta_y = pix_y[:, :, None] - features[1][:, None, :]
    exponent = 0.5 * (features[2][:, None, :] * delta_x * delta_x + features[4][:, None, :] * delta_y * delta_y) + features[3][:, None, :] * delta_x * delta_y
    alphas = 0.99 * features[5][:, None, :] * jnp.exp(-exponent) * slot_live[:, None, :]
    return (alphas, jnp.log(1.0 - alphas))

def render_tiles(slot_feats, live, pix_x, pix_y):
    tiles_n = live.shape[0]
    blocks_n = live.shape[1] // 128
    feats_blocks = jnp.moveaxis(slot_feats.reshape(9, tiles_n, blocks_n, 128), 2, 0)
    live_blocks = jnp.moveaxis(live.reshape(tiles_n, blocks_n, 128), 1, 0)

    def one_block(state, block_in):
        log_left, colors = state
        features, slot_live = block_in
        alphas, log_keep = opacities(features, slot_live, pix_x, pix_y)
        before = jnp.cumsum(log_keep, axis=2) - log_keep
        weights = alphas * jnp.exp(log_left[:, :, None] + before)
        colors = colors + jnp.einsum('kpg,ckg->kcp', weights, features[6:9], precision=lax.Precision.HIGHEST)
        return ((log_left + lax.optimization_barrier(jnp.sum(log_keep, axis=2)), colors), None)
    start_state = (jnp.zeros((tiles_n, 256), jnp.float32), jnp.zeros((tiles_n, 3, 256), jnp.float32))
    (log_left, colors), unused = lax.scan(one_block, start_state, (feats_blocks, live_blocks))
    return colors

def learn_rates():
    position = jnp.arange(59)
    rate_rows = jnp.where(position < 3, 0.0016, jnp.where(position < 6, 0.005, jnp.where(position < 10, 0.001, jnp.where(position < 11, 0.05, jnp.where(position < 14, 0.0025, 0.000125)))))
    return rate_rows.astype(jnp.float32)[:, None]

def adam(params, gradients, moment_one, moment_two):
    moment_new = BETA_ONE * moment_one + (1.0 - BETA_ONE) * gradients
    square_new = BETA_TWO * moment_two + (1.0 - BETA_TWO) * gradients * gradients
    fix_one = 1.0 - BETA_ONE ** ADAM_STEP
    fix_two = 1.0 - BETA_TWO ** ADAM_STEP
    update = moment_new / fix_one / (jnp.sqrt(square_new / fix_two) + ADAM_EPS)
    return (params - learn_rates() * update, moment_new, square_new)

def reference(params, moment_one, moment_two, visible, counts, tile_pos, target):
    screen_width = TILES_X * 16.0
    screen_height = TILES // TILES_X * 16.0
    list_len = BLOCKS * 128
    group = 16
    live = (jnp.arange(128)[None, None, :] < counts[:, :, None]).reshape(TILES, list_len).astype(jnp.float32)
    safe_ids = jnp.where(live > 0, visible, 0).astype(jnp.int32)
    pix_x, pix_y = pixel_coords(tile_pos)
    target_f = target.astype(jnp.float32)

    def one_group(inputs):
        feats_group, live_group, px_group, py_group, target_group = inputs
        colors = render_tiles(feats_group, live_group, px_group, py_group)
        errors = colors - target_group
        return lax.optimization_barrier(jnp.sum(errors * errors, axis=(1, 2))) / 16.0

    def losses(all_params):
        features = project(all_params, screen_width, screen_height)
        slot_feats = jnp.take(features, safe_ids.reshape(-1), axis=1).reshape(9, TILES // group, group, list_len)
        slot_feats = jnp.moveaxis(slot_feats, 1, 0)
        per_group = lax.map(jax.checkpoint(one_group), (slot_feats, live.reshape(-1, group, list_len), pix_x.reshape(-1, group, 256), pix_y.reshape(-1, group, 256), target_f.reshape(-1, group, 3, 256)))
        return per_group.reshape(TILES)
    tile_loss, pull_back = jax.vjp(losses, params)
    gradients, = pull_back(jnp.ones_like(tile_loss))
    new_params, moment_new, square_new = adam(params, gradients, moment_one, moment_two)
    return (tile_loss, new_params, moment_new, square_new)
```

```python
import numpy as np
import jax
import jax.numpy as jnp
from jax import lax
from jax.experimental import pallas as pl
from jax.experimental.pallas import tpu as pltpu
from jax.sharding import PartitionSpec as P

N_DEV = 128
G_DEV = 4096
CAP = 64
TILES_X = 64
ADAM_STEP = 1000
SENTINEL = N_DEV * G_DEV
SCREEN_W = 1024.0
SCREEN_H = 512.0

SH_ZERO = 0.28209479177387814
SH_ONE = 0.4886025119029199
SH_TWO = (
    1.0925484305920792,
    -1.0925484305920792,
    0.31539156525252005,
    -1.0925484305920792,
    0.5462742152960396,
)
SH_THREE = (
    -0.5900435899266435,
    2.890611442640554,
    -0.4570457994644658,
    0.3731763325901154,
    -0.4570457994644658,
    1.445305721320277,
    -0.5900435899266435,
)
BETA_ONE = 0.9
BETA_TWO = 0.999
ADAM_EPS = 1e-15
LOG2_E = 1.4426950408889634

F32 = jnp.float32
BF16 = jnp.bfloat16
VMEM = pl.BlockSpec(memory_space=pltpu.VMEM)


def harmonics(dir_x, dir_y, dir_z):
    sq_x = dir_x * dir_x
    sq_y = dir_y * dir_y
    sq_z = dir_z * dir_z
    return [
        -SH_ONE * dir_y,
        SH_ONE * dir_z,
        -SH_ONE * dir_x,
        SH_TWO[0] * dir_x * dir_y,
        SH_TWO[1] * dir_y * dir_z,
        SH_TWO[2] * (2.0 * sq_z - sq_x - sq_y),
        SH_TWO[3] * dir_x * dir_z,
        SH_TWO[4] * (sq_x - sq_y),
        SH_THREE[0] * dir_y * (3.0 * sq_x - sq_y),
        SH_THREE[1] * dir_x * dir_y * dir_z,
        SH_THREE[2] * dir_y * (4.0 * sq_z - sq_x - sq_y),
        SH_THREE[3] * dir_z * (2.0 * sq_z - 3.0 * sq_x - 3.0 * sq_y),
        SH_THREE[4] * dir_x * (4.0 * sq_z - sq_x - sq_y),
        SH_THREE[5] * dir_z * (sq_x - sq_y),
        SH_THREE[6] * dir_x * (sq_x - 3.0 * sq_y),
    ]


def directions(mean_x, mean_y, depths):
    distance = jnp.sqrt(mean_x * mean_x + mean_y * mean_y + depths * depths)
    return harmonics(mean_x / distance, mean_y / distance, depths / distance)


def geometry(rows):
    mean_x, mean_y, depths = (rows[0], rows[1], rows[2])
    scale_x = jnp.exp(rows[3])
    scale_y = jnp.exp(rows[4])
    scale_z = jnp.exp(rows[5])
    quat_len = jnp.maximum(
        jnp.sqrt(rows[6] * rows[6] + rows[7] * rows[7] + rows[8] * rows[8] + rows[9] * rows[9]),
        0.5,
    )
    quat_w = rows[6] / quat_len
    quat_x = rows[7] / quat_len
    quat_y = rows[8] / quat_len
    quat_z = rows[9] / quat_len
    rot_xx = 1.0 - 2.0 * (quat_y * quat_y + quat_z * quat_z)
    rot_xy = 2.0 * (quat_x * quat_y - quat_w * quat_z)
    rot_xz = 2.0 * (quat_x * quat_z + quat_w * quat_y)
    rot_yx = 2.0 * (quat_x * quat_y + quat_w * quat_z)
    rot_yy = 1.0 - 2.0 * (quat_x * quat_x + quat_z * quat_z)
    rot_yz = 2.0 * (quat_y * quat_z - quat_w * quat_x)
    rot_zx = 2.0 * (quat_x * quat_z - quat_w * quat_y)
    rot_zy = 2.0 * (quat_y * quat_z + quat_w * quat_x)
    rot_zz = 1.0 - 2.0 * (quat_x * quat_x + quat_y * quat_y)
    m_xx, m_xy, m_xz = (rot_xx * scale_x, rot_xy * scale_y, rot_xz * scale_z)
    m_yx, m_yy, m_yz = (rot_yx * scale_x, rot_yy * scale_y, rot_yz * scale_z)
    m_zx, m_zy, m_zz = (rot_zx * scale_x, rot_zy * scale_y, rot_zz * scale_z)
    cov_xx = m_xx * m_xx + m_xy * m_xy + m_xz * m_xz
    cov_xy = m_xx * m_yx + m_xy * m_yy + m_xz * m_yz
    cov_xz = m_xx * m_zx + m_xy * m_zy + m_xz * m_zz
    cov_yy = m_yx * m_yx + m_yy * m_yy + m_yz * m_yz
    cov_yz = m_yx * m_zx + m_yy * m_zy + m_yz * m_zz
    cov_zz = m_zx * m_zx + m_zy * m_zy + m_zz * m_zz
    focal = 1.2 * SCREEN_W
    inverse = 1.0 / depths
    jac_xx = focal * inverse
    jac_xz = -focal * mean_x * inverse * inverse
    jac_yy = focal * inverse
    jac_yz = -focal * mean_y * inverse * inverse
    plane_a = (
        jac_xx * jac_xx * cov_xx + 2.0 * jac_xx * jac_xz * cov_xz + jac_xz * jac_xz * cov_zz + 0.3
    )
    plane_b = (
        jac_xx * jac_yy * cov_xy
        + jac_xx * jac_yz * cov_xz
        + jac_xz * jac_yy * cov_yz
        + jac_xz * jac_yz * cov_zz
    )
    plane_c = (
        jac_yy * jac_yy * cov_yy + 2.0 * jac_yy * jac_yz * cov_yz + jac_yz * jac_yz * cov_zz + 0.3
    )
    determ = plane_a * plane_c - plane_b * plane_b
    return (
        focal * mean_x * inverse + 0.5 * SCREEN_W,
        focal * mean_y * inverse + 0.5 * SCREEN_H,
        plane_c / determ,
        -plane_b / determ,
        plane_a / determ,
    )


def split(value):
    high = value.astype(BF16)
    return (high, (value - high.astype(F32)).astype(BF16))


def dot_nt(left, right):
    return lax.dot_general(left, right, (((1,), (1,)), ((), ())), preferred_element_type=F32)


def dot_nn(left, right):
    return jnp.dot(left, right, preferred_element_type=F32)


def one_hot(index_row, size):
    rows = lax.broadcasted_iota(jnp.int32, (size, index_row.shape[1]), 0)
    return jnp.where(rows == index_row, 1.0, 0.0).astype(BF16)


def iota(shape, axis):
    return lax.broadcasted_iota(jnp.int32, shape, axis)


def rows_first(ref, out_ref):
    for base in range(0, 59, 8):
        size = min(8, 59 - base)
        for piece in range(32):
            out_ref[pl.ds(base * 32 + piece, size, stride=32), :] = ref[
                base : base + size, piece * 128 : (piece + 1) * 128
            ]


def plan_kernel(sorted_ref, keys_ref, request_ref, rank_ref, owner_s, rank_s, first_s, local_s):
    keys = sorted_ref[...]
    lane = iota((64, 128), 1)
    before = pltpu.roll(keys, 1, 1)
    before = jnp.where(lane == 0, pltpu.roll(before, 1, 0), before)
    position = iota((64, 128), 0) * 128 + lane
    fresh = ((keys != before) | (position == 0)) & (keys < SENTINEL)
    fresh_f = jnp.where(fresh, 1.0, 0.0).astype(F32)
    fresh_h = fresh_f.astype(BF16)
    upto = jnp.where(iota((128, 128), 0) <= iota((128, 128), 1), 1.0, 0.0).astype(BF16)
    ones = jnp.ones((128, 128), BF16)
    lower = jnp.where(iota((64, 64), 1) < iota((64, 64), 0), 1.0, 0.0).astype(BF16)
    within = dot_nn(fresh_h, upto)
    totals = dot_nn(fresh_h, ones).astype(BF16)
    count = within + dot_nn(lower, totals)
    owner = keys >> 12
    owner_s[...] = owner
    first_s[...] = fresh_f
    local_s[...] = keys & (G_DEV - 1)

    def pair(ref, index):
        return jnp.concatenate(
            [ref[pl.ds(2 * index, 1), :], ref[pl.ds(2 * index + 1, 1), :]], axis=1
        )

    def smaller(index, total):
        owners = pair(owner_s, index)
        is_less = jnp.where(owners < iota((128, 256), 0), 1.0, 0.0).astype(BF16)
        firsts = jnp.broadcast_to(pair(first_s, index), (8, 256)).astype(BF16)
        return total + dot_nt(firsts, is_less)

    first_of = lax.fori_loop(0, 32, smaller, jnp.zeros((8, 128), F32), unroll=4)
    offsets = jnp.broadcast_to(first_of[0:1], (64, 128)).astype(jnp.int32)
    offset = jnp.take_along_axis(offsets, owner & 127, axis=1, mode="promise_in_bounds")
    rank_s[...] = count.astype(jnp.int32) - 1 - offset

    def fill(index, total):
        owners = pair(owner_s, index)
        ranks = pair(rank_s, index)
        firsts = pair(first_s, index) > 0.0
        local = pair(local_s, index)
        match = (ranks == iota((64, 256), 0)) & firsts
        high = jnp.where(match, (local >> 6).astype(F32), 0.0).astype(BF16)
        low = jnp.where(match, (local & 63).astype(F32), 0.0).astype(BF16)
        used = jnp.where(match, 1.0, 0.0).astype(BF16)
        parts = jnp.concatenate([high, low, used], axis=0)
        return total + dot_nt(parts, one_hot(owners, 128))

    filled = lax.fori_loop(0, 32, fill, jnp.zeros((192, 128), F32), unroll=2)
    locals_of = (filled[0:64] * 64.0 + filled[64:128]).astype(jnp.int32)
    table = jnp.where(filled[128:192] > 0.5, locals_of, -1)
    padded = jnp.concatenate([locals_of, jnp.zeros((64, 128), jnp.int32)], axis=0)
    request_ref[...] = jnp.transpose(padded)

    slots = keys_ref[...]
    slot_owner = (slots >> 12) & 127
    slot_local = slots & (G_DEV - 1)
    rank = jnp.zeros((64, 128), jnp.int32)
    for place in range(64):
        row = jnp.broadcast_to(table[place : place + 1], (64, 128))
        found = jnp.take_along_axis(row, slot_owner, axis=1, mode="promise_in_bounds")
        rank = jnp.where(found == slot_local, place, rank)
    rank_ref[...] = rank


def plan(keys_sorted, keys):
    return pl.pallas_call(
        plan_kernel,
        out_shape=(
            jax.ShapeDtypeStruct((128, 128), jnp.int32),
            jax.ShapeDtypeStruct((64, 128), jnp.int32),
        ),
        in_specs=[VMEM, VMEM],
        out_specs=(VMEM, VMEM),
        scratch_shapes=[
            pltpu.VMEM((64, 128), jnp.int32),
            pltpu.VMEM((64, 128), jnp.int32),
            pltpu.VMEM((64, 128), F32),
            pltpu.VMEM((64, 128), jnp.int32),
        ],
        compiler_params=pltpu.CompilerParams(vmem_limit_bytes=32 * 1024 * 1024),
    )(keys_sorted, keys)


def project_kernel(params_ref, feats_ref, rows_s):
    rows_first(params_ref, rows_s)

    def row(index):
        return rows_s[index * 32 : (index + 1) * 32, :]

    rows = [row(index) for index in range(10)]
    feats = list(geometry(rows))
    feats.append(1.0 / (1.0 + jnp.exp(-row(10))))
    basis = directions(rows[0], rows[1], rows[2])
    for channel in range(3):
        total = 0.5 + SH_ZERO * row(11 + channel)
        for degree in range(1, 16):
            total = total + basis[degree - 1] * row(11 + 3 * degree + channel)
        feats.append(total)
    for index in range(9):
        feats_ref[index * 32 : (index + 1) * 32, :] = feats[index]


def project(params):
    return pl.pallas_call(
        project_kernel,
        out_shape=jax.ShapeDtypeStruct((288, 128), F32),
        in_specs=[VMEM],
        out_specs=VMEM,
        scratch_shapes=[pltpu.VMEM((59 * 32, 128), F32)],
        compiler_params=pltpu.CompilerParams(vmem_limit_bytes=32 * 1024 * 1024),
    )(params)


def serve_kernel(feats_ref, wanted_ref, out_ref, place_s):
    wanted = jnp.transpose(wanted_ref[...])[0:64]
    high = wanted >> 7
    low = wanted & 127
    for feature in range(9):
        total = jnp.zeros((64, 128), F32)
        for piece in range(32):
            row = jnp.broadcast_to(
                feats_ref[feature * 32 + piece : feature * 32 + piece + 1, :], (64, 128)
            )
            found = jnp.take_along_axis(row, low, axis=1, mode="promise_in_bounds")
            total = jnp.where(high == piece, found, total)
        place_s[feature * 64 : (feature + 1) * 64, :] = total
    place_s[576:640, :] = jnp.zeros((64, 128), F32)
    for part in range(5):
        out_ref[pl.ds(part, 128, stride=5), :] = jnp.transpose(
            place_s[part * 128 : (part + 1) * 128, :]
        )


def serve(feats, wanted):
    return pl.pallas_call(
        serve_kernel,
        out_shape=jax.ShapeDtypeStruct((640, 128), F32),
        in_specs=[VMEM, VMEM],
        out_specs=VMEM,
        scratch_shapes=[pltpu.VMEM((640, 128), F32)],
        compiler_params=pltpu.CompilerParams(vmem_limit_bytes=32 * 1024 * 1024),
    )(feats, wanted)


def pixel_basis():
    pixel = np.arange(256)
    across = (pixel % 16) - 7.5
    down = (pixel // 16) - 7.5
    six = np.stack([across * across, across * down, down * down, across, down, np.ones(256)])
    basis = np.zeros((24, 256), np.float32)
    basis[0:18] = np.tile(six, (3, 1))
    moments = np.zeros((16, 256), np.float32)
    moments[0:6] = six
    return (jnp.asarray(basis, BF16), jnp.asarray(moments, BF16))


def render_kernel(
    arrived_ref,
    keys_ref,
    rank_ref,
    centre_ref,
    target_ref,
    basis_ref,
    moment_ref,
    out_ref,
    loss_ref,
    table_s,
    coef_s,
    alpha_s,
    weight_s,
    sums_s,
    grads_s,
):
    for part in range(5):
        table_s[part * 128 : (part + 1) * 128, :] = jnp.transpose(
            arrived_ref[pl.ds(part, 128, stride=5), :]
        )
    keys = keys_ref[...]
    rank = rank_ref[...]
    live = keys < SENTINEL
    owner = (keys >> 12) & 127
    feats = []
    for feature in range(9):
        total = jnp.zeros((64, 128), F32)
        for place in range(64):
            row = jnp.broadcast_to(
                table_s[feature * 64 + place : feature * 64 + place + 1, :], (64, 128)
            )
            found = jnp.take_along_axis(row, owner, axis=1, mode="promise_in_bounds")
            total = jnp.where(rank == place, found, total)
        feats.append(total)
    half = iota((64, 128), 0) < 32
    tile = jnp.where(
        half,
        jnp.broadcast_to(centre_ref[0:1, :], (64, 128)),
        jnp.broadcast_to(centre_ref[1:2, :], (64, 128)),
    )
    rel_u = feats[0] - ((tile & (TILES_X - 1)).astype(F32) * 16.0 + 7.5)
    rel_v = feats[1] - ((tile >> 6).astype(F32) * 16.0 + 7.5)
    conic_1, conic_2, conic_3 = (feats[2], feats[3], feats[4])
    h_1 = 0.5 * conic_1
    h_3 = 0.5 * conic_3
    pull_u = conic_1 * rel_u + conic_2 * rel_v
    pull_v = conic_3 * rel_v + conic_2 * rel_u
    centre_e = 0.5 * (conic_1 * rel_u * rel_u + conic_3 * rel_v * rel_v) + conic_2 * rel_u * rel_v
    level = jnp.log2(0.99 * feats[5])
    coefs = [
        -LOG2_E * h_1,
        -LOG2_E * conic_2,
        -LOG2_E * h_3,
        LOG2_E * pull_u,
        LOG2_E * pull_v,
        level - LOG2_E * centre_e,
    ]
    for index in range(6):
        value = jnp.where(live, coefs[index], -1024.0 if index == 5 else 0.0)
        high = value.astype(BF16).astype(F32)
        rest = value - high
        middle = rest.astype(BF16).astype(F32)
        coef_s[pl.ds(index, 64, stride=24), :] = high
        coef_s[pl.ds(index + 6, 64, stride=24), :] = middle
        coef_s[pl.ds(index + 12, 64, stride=24), :] = rest - middle
    for channel in range(3):
        value = feats[6 + channel]
        high = value.astype(BF16).astype(F32)
        coef_s[pl.ds(18 + channel, 64, stride=24), :] = high
        coef_s[pl.ds(21 + channel, 64, stride=24), :] = value - high

    diagonal = (iota((8, 128), 1) & 7) == iota((8, 128), 0)

    def spread(coef, base):
        return jnp.concatenate(
            [
                jnp.where(
                    diagonal,
                    jnp.broadcast_to(coef[base + channel : base + channel + 1], (8, 128)),
                    0.0,
                )
                for channel in range(3)
            ],
            axis=0,
        )

    for group in range(2):

        def forward(index, state):
            left, colors = state
            chunk = group * 32 + index
            coef = coef_s[pl.ds(pl.multiple_of(chunk * 24, 8), 24), :]
            powers = dot_nn(jnp.transpose(coef).astype(BF16), basis_ref[...])
            alpha = jnp.exp2(powers)
            rows = pl.ds(pl.multiple_of(index * 128, 128), 128)
            alpha_s[rows, :] = alpha
            parts = []
            for slot in range(16):
                weight = alpha[slot * 8 : (slot + 1) * 8] * left
                left = left - weight
                parts.append(weight)
            weights = jnp.concatenate(parts, axis=0)
            weight_s[rows, :] = weights
            high, low = split(weights)
            col_high = spread(coef, 18).astype(BF16)
            col_low = spread(coef, 21).astype(BF16)
            colors = (
                colors
                + dot_nn(col_high, high)
                + dot_nn(col_low, high)
                + dot_nn(col_high, low)
            )
            return (left, colors)

        left, colors = lax.fori_loop(
            0, 32, forward, (jnp.ones((8, 256), F32), jnp.zeros((24, 256), F32))
        )
        errors = colors - target_ref[group * 24 : (group + 1) * 24, :]
        squares = errors * errors
        total = jnp.sum(squares[0:8] + squares[8:16] + squares[16:24], axis=1, keepdims=True)
        loss_ref[group * 8 : (group + 1) * 8, :] = jnp.broadcast_to(total / 16.0, (8, 128))
        err = errors * 0.125
        err_high, err_low = split(err)
        err_three = jnp.concatenate([err_high, err_low, err_high], axis=0)

        def backward(step, behind):
            index = 31 - step
            chunk = group * 32 + index
            coef = coef_s[pl.ds(pl.multiple_of(chunk * 24, 8), 24), :]
            col_high = spread(coef, 18)
            col_low = spread(coef, 21)
            col_three = jnp.concatenate([col_high, col_high, col_low], axis=0)
            shades = dot_nn(jnp.transpose(col_three).astype(BF16), err_three)
            rows = pl.ds(pl.multiple_of(index * 128, 128), 128)
            alpha = alpha_s[rows, :]
            weights = weight_s[rows, :]
            parts = []
            for slot in range(15, -1, -1):
                cut = slice(slot * 8, (slot + 1) * 8)
                gap = shades[cut] - behind
                parts.append(weights[cut] * gap)
                behind = behind + alpha[cut] * gap
            pulls = jnp.concatenate(parts[::-1], axis=0)
            pull_high, pull_low = split(pulls)
            sums = dot_nt(moment_ref[...], pull_high) + dot_nt(moment_ref[...], pull_low)
            high, low = split(weights)
            tints = dot_nt(err_high, high) + dot_nt(err_low, high) + dot_nt(err_high, low)
            sums_s[pl.ds(pl.multiple_of(chunk * 16, 8), 8), :] = sums[0:8]
            for channel in range(3):
                own = jnp.where(diagonal, tints[channel * 8 : (channel + 1) * 8], 0.0)
                sums_s[pl.ds(chunk * 16 + 8 + channel, 1), :] = jnp.sum(
                    own, axis=0, keepdims=True
                )
            return behind

        lax.fori_loop(0, 32, backward, jnp.zeros((8, 256), F32))

    def sums_of(index):
        return sums_s[pl.ds(index, 64, stride=16), :]

    m_xx, m_xy, m_yy, m_x, m_y, m_0 = [sums_of(index) for index in range(6)]
    s_x = m_x - rel_u * m_0
    s_y = m_y - rel_v * m_0
    s_xx = m_xx - 2.0 * rel_u * m_x + rel_u * rel_u * m_0
    s_yy = m_yy - 2.0 * rel_v * m_y + rel_v * rel_v * m_0
    s_xy = m_xy - rel_u * m_y - rel_v * m_x + rel_u * rel_v * m_0
    slot_grads = [
        conic_1 * s_x + conic_2 * s_y,
        conic_3 * s_y + conic_2 * s_x,
        -0.5 * s_xx,
        -s_xy,
        -0.5 * s_yy,
        m_0,
        sums_of(8),
        sums_of(9),
        sums_of(10),
    ]
    for index in range(9):
        grads_s[pl.ds(index, 64, stride=16), :] = jnp.where(live, slot_grads[index], 0.0)
    grads_s[pl.ds(9, 64, stride=16), :] = ((rank >> 5) * 128 + owner).astype(F32)
    grads_s[pl.ds(10, 64, stride=16), :] = (rank & 31).astype(F32)

    def gather_rows(index, size, lanes, total):
        both = jnp.concatenate(
            [
                grads_s[pl.ds(pl.multiple_of(index * 32, 8), 16), :],
                grads_s[pl.ds(pl.multiple_of(index * 32 + 16, 8), 16), :],
            ],
            axis=1,
        )
        return scatter_step(both, size, total)

    def scatter(index, total):
        return gather_rows(index, 32, 256, total)

    collected = lax.fori_loop(0, 32, scatter, jnp.zeros((288, 256), F32))
    for feature in range(9):
        piece = collected[feature * 32 : (feature + 1) * 32]
        table_s[feature * 64 : feature * 64 + 32, :] = piece[:, 0:128]
        table_s[feature * 64 + 32 : feature * 64 + 64, :] = piece[:, 128:256]
    table_s[576:640, :] = jnp.zeros((64, 128), F32)
    for part in range(5):
        out_ref[pl.ds(part, 128, stride=5), :] = jnp.transpose(
            table_s[part * 128 : (part + 1) * 128, :]
        )


def scatter_step(both, size, total):
    lanes = one_hot(both[9:10].astype(jnp.int32), 256)
    match = iota((size, 256), 0) == both[10:11].astype(jnp.int32)
    high = both.astype(BF16).astype(F32)
    low = both - high
    masked = [
        jnp.where(match, jnp.broadcast_to(part[feature : feature + 1], (size, 256)), 0.0)
        for part in (high, low)
        for feature in range(9)
    ]
    found = dot_nt(jnp.concatenate(masked, axis=0).astype(BF16), lanes)
    return total + found[0 : 9 * size] + found[9 * size : 18 * size]


def render(arrived, keys, rank, centre, target):
    basis, moments = pixel_basis()
    return pl.pallas_call(
        render_kernel,
        out_shape=(
            jax.ShapeDtypeStruct((640, 128), F32),
            jax.ShapeDtypeStruct((16, 128), F32),
        ),
        in_specs=[VMEM] * 7,
        out_specs=(VMEM, VMEM),
        scratch_shapes=[
            pltpu.VMEM((640, 128), F32),
            pltpu.VMEM((64 * 24, 128), F32),
            pltpu.VMEM((4096, 256), F32),
            pltpu.VMEM((4096, 256), F32),
            pltpu.VMEM((64 * 16, 128), F32),
            pltpu.VMEM((64 * 16, 128), F32),
        ],
        compiler_params=pltpu.CompilerParams(vmem_limit_bytes=48 * 1024 * 1024),
    )(arrived, keys, rank, centre, target, basis, moments)


def learn_rate(index):
    if index < 3:
        return 0.0016
    if index < 6:
        return 0.005
    if index < 10:
        return 0.001
    if index < 11:
        return 0.05
    return 0.0025 if index < 14 else 0.000125


def update_kernel(
    received_ref,
    wanted_ref,
    params_ref,
    one_ref,
    two_ref,
    rates_ref,
    new_params_ref,
    new_one_ref,
    new_two_ref,
    rows_s,
    grads_s,
    table_s,
):
    wanted = jnp.transpose(wanted_ref[...])[0:64]
    piece = wanted >> 7
    for part in range(5):
        turned = jnp.transpose(received_ref[pl.ds(part, 128, stride=5), :])
        table_s[pl.ds(2 * part, 64, stride=16), :] = turned[0:64]
        if part < 4:
            table_s[pl.ds(2 * part + 1, 64, stride=16), :] = turned[64:128]
    table_s[pl.ds(9, 64, stride=16), :] = ((piece >> 4) * 128 + (wanted & 127)).astype(F32)
    table_s[pl.ds(10, 64, stride=16), :] = (piece & 15).astype(F32)

    def scatter(index, total):
        both = jnp.concatenate(
            [
                table_s[pl.ds(pl.multiple_of(index * 32, 8), 16), :],
                table_s[pl.ds(pl.multiple_of(index * 32 + 16, 8), 16), :],
            ],
            axis=1,
        )
        return scatter_step(both, 16, total)

    collected = lax.fori_loop(0, 32, scatter, jnp.zeros((144, 256), F32))

    def grad_of(feature):
        part = collected[feature * 16 : (feature + 1) * 16]
        return jnp.concatenate([part[:, 0:128], part[:, 128:256]], axis=0)

    rows_first(params_ref, rows_s)

    def row(index):
        return rows_s[index * 32 : (index + 1) * 32, :]

    def put(index, value):
        grads_s[index * 32 : (index + 1) * 32, :] = value

    rows = [row(index) for index in range(10)]
    unused, pull_geometry = jax.vjp(geometry, rows)
    (geo_grads,) = pull_geometry(tuple(grad_of(feature) for feature in range(5)))
    put(10, grad_of(5) * (1.0 / (1.0 + jnp.exp(row(10)))))
    basis, pull_basis = jax.vjp(directions, rows[0], rows[1], rows[2])
    tints = [grad_of(6 + channel) for channel in range(3)]
    basis_grads = []
    for channel in range(3):
        put(11 + channel, SH_ZERO * tints[channel])
    for degree in range(1, 16):
        total = None
        for channel in range(3):
            index = 11 + 3 * degree + channel
            put(index, basis[degree - 1] * tints[channel])
            term = row(index) * tints[channel]
            total = term if total is None else total + term
        basis_grads.append(total)
    mean_grads = pull_basis(basis_grads)
    for index in range(10):
        put(index, geo_grads[index] + mean_grads[index] if index < 3 else geo_grads[index])

    fix_one = 1.0 / (1.0 - BETA_ONE**ADAM_STEP)
    fix_two = 1.0 / (1.0 - BETA_TWO**ADAM_STEP)
    for base in range(0, 59, 8):
        size = min(8, 59 - base)
        rate = jnp.broadcast_to(rates_ref[base : base + size, 0:1], (size, 128))
        for piece in range(32):
            cut = (slice(base, base + size), slice(piece * 128, (piece + 1) * 128))
            grad = grads_s[pl.ds(base * 32 + piece, size, stride=32), :]
            one = BETA_ONE * one_ref[cut] + (1.0 - BETA_ONE) * grad
            two = BETA_TWO * two_ref[cut] + (1.0 - BETA_TWO) * grad * grad
            new_one_ref[cut] = one
            new_two_ref[cut] = two
            step = one * fix_one / (jnp.sqrt(two * fix_two) + ADAM_EPS)
            new_params_ref[cut] = params_ref[cut] - rate * step


def update(received, wanted, params, moment_one, moment_two):
    rates = np.zeros((64, 128), np.float32)
    rates[0:59] = np.array([learn_rate(index) for index in range(59)], np.float32)[:, None]
    whole = jax.ShapeDtypeStruct((59, G_DEV), F32)
    return pl.pallas_call(
        update_kernel,
        out_shape=(whole, whole, whole),
        in_specs=[VMEM] * 6,
        out_specs=(VMEM, VMEM, VMEM),
        scratch_shapes=[
            pltpu.VMEM((59 * 32, 128), F32),
            pltpu.VMEM((59 * 32, 128), F32),
            pltpu.VMEM((64 * 16, 128), F32),
        ],
        compiler_params=pltpu.CompilerParams(vmem_limit_bytes=48 * 1024 * 1024),
    )(received, wanted, params, moment_one, moment_two, jnp.asarray(rates))


def slot_keys(visible, counts):
    live = jnp.arange(128, dtype=jnp.int32)[None, None, :] < counts[:, :, None]
    keys = jnp.where(live.reshape(visible.shape), visible, SENTINEL)
    return jnp.transpose(keys.reshape(2, 8, 512), (0, 2, 1)).reshape(64, 128)


def exchange(array):
    flat = array.reshape(N_DEV, 1, -1)
    flat = lax.all_to_all(flat, "dev", split_axis=0, concat_axis=0, tiled=True)
    return flat.reshape(array.shape)


def shards(params, moment_one, moment_two, visible, counts, tile_pos, target):
    keys = slot_keys(visible, counts)
    keys_sorted = lax.sort(keys.reshape(-1), is_stable=False).reshape(64, 128)
    request, rank = plan(keys_sorted, keys)
    feats = project(params)
    wanted = exchange(request)
    arrived = exchange(serve(feats, wanted))
    centre = jnp.tile(tile_pos.reshape(2, 8), (1, 16))
    colours = target.astype(F32).reshape(2, 8, 3, 256)
    colours = jnp.transpose(colours, (0, 2, 1, 3)).reshape(48, 256)
    grads, loss = render(arrived, keys, rank, centre, colours)
    received = exchange(grads)
    outs = update(received, wanted, params, moment_one, moment_two)
    return (loss[:, 0], *outs)


def solution(mesh):
    placed = (
        P(None, "dev"),
        P(None, "dev"),
        P(None, "dev"),
        P("dev", None),
        P("dev", None),
        P("dev"),
        P("dev", None, None),
    )
    return jax.shard_map(
        shards,
        mesh=mesh,
        in_specs=placed,
        out_specs=(P("dev"), P(None, "dev"), P(None, "dev"), P(None, "dev")),
        check_vma=False,
    )
```

```python
import numpy as np
import jax
import jax.numpy as jnp
from jax import lax
from jax.experimental import pallas as pl
from jax.experimental.pallas import tpu as pltpu
from jax.sharding import PartitionSpec as P

N_DEV = 128
G_DEV = 4096
CAP = 64
TILES_X = 64
ADAM_STEP = 1000
SENTINEL = N_DEV * G_DEV
SCREEN_W = 1024.0
SCREEN_H = 512.0

SH_ZERO = 0.28209479177387814
SH_ONE = 0.4886025119029199
SH_TWO = (
    1.0925484305920792,
    -1.0925484305920792,
    0.31539156525252005,
    -1.0925484305920792,
    0.5462742152960396,
)
SH_THREE = (
    -0.5900435899266435,
    2.890611442640554,
    -0.4570457994644658,
    0.3731763325901154,
    -0.4570457994644658,
    1.445305721320277,
    -0.5900435899266435,
)
BETA_ONE = 0.9
BETA_TWO = 0.999
ADAM_EPS = 1e-15
LOG2_E = 1.4426950408889634

F32 = jnp.float32
BF16 = jnp.bfloat16
VMEM = pl.BlockSpec(memory_space=pltpu.VMEM)
FU = 4
BU = 4
PU = 8
GU = 4
SU = 8
MROWS = 1024
MU = 1


def harmonics(dir_x, dir_y, dir_z):
    sq_x = dir_x * dir_x
    sq_y = dir_y * dir_y
    sq_z = dir_z * dir_z
    return [
        -SH_ONE * dir_y,
        SH_ONE * dir_z,
        -SH_ONE * dir_x,
        SH_TWO[0] * dir_x * dir_y,
        SH_TWO[1] * dir_y * dir_z,
        SH_TWO[2] * (2.0 * sq_z - sq_x - sq_y),
        SH_TWO[3] * dir_x * dir_z,
        SH_TWO[4] * (sq_x - sq_y),
        SH_THREE[0] * dir_y * (3.0 * sq_x - sq_y),
        SH_THREE[1] * dir_x * dir_y * dir_z,
        SH_THREE[2] * dir_y * (4.0 * sq_z - sq_x - sq_y),
        SH_THREE[3] * dir_z * (2.0 * sq_z - 3.0 * sq_x - 3.0 * sq_y),
        SH_THREE[4] * dir_x * (4.0 * sq_z - sq_x - sq_y),
        SH_THREE[5] * dir_z * (sq_x - sq_y),
        SH_THREE[6] * dir_x * (sq_x - 3.0 * sq_y),
    ]


def directions(mean_x, mean_y, depths):
    distance = jnp.sqrt(mean_x * mean_x + mean_y * mean_y + depths * depths)
    return harmonics(mean_x / distance, mean_y / distance, depths / distance)


def geometry(rows):
    mean_x, mean_y, depths = (rows[0], rows[1], rows[2])
    scale_x = jnp.exp(rows[3])
    scale_y = jnp.exp(rows[4])
    scale_z = jnp.exp(rows[5])
    quat_len = jnp.maximum(
        jnp.sqrt(rows[6] * rows[6] + rows[7] * rows[7] + rows[8] * rows[8] + rows[9] * rows[9]),
        0.5,
    )
    quat_w = rows[6] / quat_len
    quat_x = rows[7] / quat_len
    quat_y = rows[8] / quat_len
    quat_z = rows[9] / quat_len
    rot_xx = 1.0 - 2.0 * (quat_y * quat_y + quat_z * quat_z)
    rot_xy = 2.0 * (quat_x * quat_y - quat_w * quat_z)
    rot_xz = 2.0 * (quat_x * quat_z + quat_w * quat_y)
    rot_yx = 2.0 * (quat_x * quat_y + quat_w * quat_z)
    rot_yy = 1.0 - 2.0 * (quat_x * quat_x + quat_z * quat_z)
    rot_yz = 2.0 * (quat_y * quat_z - quat_w * quat_x)
    rot_zx = 2.0 * (quat_x * quat_z - quat_w * quat_y)
    rot_zy = 2.0 * (quat_y * quat_z + quat_w * quat_x)
    rot_zz = 1.0 - 2.0 * (quat_x * quat_x + quat_y * quat_y)
    m_xx, m_xy, m_xz = (rot_xx * scale_x, rot_xy * scale_y, rot_xz * scale_z)
    m_yx, m_yy, m_yz = (rot_yx * scale_x, rot_yy * scale_y, rot_yz * scale_z)
    m_zx, m_zy, m_zz = (rot_zx * scale_x, rot_zy * scale_y, rot_zz * scale_z)
    cov_xx = m_xx * m_xx + m_xy * m_xy + m_xz * m_xz
    cov_xy = m_xx * m_yx + m_xy * m_yy + m_xz * m_yz
    cov_xz = m_xx * m_zx + m_xy * m_zy + m_xz * m_zz
    cov_yy = m_yx * m_yx + m_yy * m_yy + m_yz * m_yz
    cov_yz = m_yx * m_zx + m_yy * m_zy + m_yz * m_zz
    cov_zz = m_zx * m_zx + m_zy * m_zy + m_zz * m_zz
    focal = 1.2 * SCREEN_W
    inverse = 1.0 / depths
    jac_xx = focal * inverse
    jac_xz = -focal * mean_x * inverse * inverse
    jac_yy = focal * inverse
    jac_yz = -focal * mean_y * inverse * inverse
    plane_a = (
        jac_xx * jac_xx * cov_xx + 2.0 * jac_xx * jac_xz * cov_xz + jac_xz * jac_xz * cov_zz + 0.3
    )
    plane_b = (
        jac_xx * jac_yy * cov_xy
        + jac_xx * jac_yz * cov_xz
        + jac_xz * jac_yy * cov_yz
        + jac_xz * jac_yz * cov_zz
    )
    plane_c = (
        jac_yy * jac_yy * cov_yy + 2.0 * jac_yy * jac_yz * cov_yz + jac_yz * jac_yz * cov_zz + 0.3
    )
    determ = plane_a * plane_c - plane_b * plane_b
    return (
        focal * mean_x * inverse + 0.5 * SCREEN_W,
        focal * mean_y * inverse + 0.5 * SCREEN_H,
        plane_c / determ,
        -plane_b / determ,
        plane_a / determ,
    )


def split(value):
    high = value.astype(BF16)
    return (high, (value - high.astype(F32)).astype(BF16))


def dot_nt(left, right):
    return lax.dot_general(left, right, (((1,), (1,)), ((), ())), preferred_element_type=F32)


def dot_nn(left, right):
    return jnp.dot(left, right, preferred_element_type=F32)


def one_hot(index_row, size):
    rows = lax.broadcasted_iota(jnp.int32, (size, index_row.shape[1]), 0)
    return jnp.where(rows == index_row, 1.0, 0.0).astype(BF16)


def iota(shape, axis):
    return lax.broadcasted_iota(jnp.int32, shape, axis)


def rows_first(ref, out_ref):
    for base in range(0, 59, 8):
        size = min(8, 59 - base)
        for piece in range(32):
            out_ref[pl.ds(base * 32 + piece, size, stride=32), :] = ref[
                base : base + size, piece * 128 : (piece + 1) * 128
            ]


def pair(ref, index):
    return jnp.concatenate(
        [ref[pl.ds(2 * index, 1), :], ref[pl.ds(2 * index + 1, 1), :]], axis=1
    )


def plan_kernel(sorted_ref, request_ref, table_ref, owner_s, rank_s, local_s):
    keys = sorted_ref[...]
    lane = iota((64, 128), 1)
    line = iota((64, 128), 0)

    def earlier(value):
        shifted = pltpu.roll(value, 1, 1)
        return jnp.where(lane == 0, pltpu.roll(shifted, 1, 0), shifted)

    first_slot = (lane == 0) & (line == 0)
    before = earlier(keys)
    fresh = ((keys != before) | first_slot) & (keys < SENTINEL)
    fresh_h = jnp.where(fresh, 1.0, 0.0).astype(BF16)
    upto = jnp.where(iota((128, 128), 0) <= iota((128, 128), 1), 1.0, 0.0).astype(BF16)
    ones = jnp.ones((128, 128), BF16)
    lower = jnp.where(iota((64, 64), 1) < iota((64, 64), 0), 1.0, 0.0).astype(BF16)
    totals = dot_nn(fresh_h, ones).astype(BF16)
    count = (dot_nn(fresh_h, upto) + dot_nn(lower, totals)).astype(jnp.int32) - 1
    owner = keys >> 12
    opens = (owner != (before >> 12)) | first_slot
    base = jnp.where(opens, count, 0)
    for step in (1, 2, 4, 8, 16, 32, 64):
        base = jnp.maximum(base, jnp.where(lane >= step, pltpu.roll(base, step, 1), 0))
    above = jnp.broadcast_to(jnp.max(base, axis=1, keepdims=True), (64, 128))
    above = jnp.where(line >= 1, pltpu.roll(above, 1, 0), 0)
    for step in (1, 2, 4, 8, 16, 32):
        above = jnp.maximum(above, jnp.where(line >= step, pltpu.roll(above, step, 0), 0))
    rank = count - jnp.maximum(base, above)
    owner_s[...] = owner
    rank_s[...] = jnp.where(fresh, rank, -1)
    local_s[...] = keys & (G_DEV - 1)

    def fill(index, total):
        local = pair(local_s, index)
        match = pair(rank_s, index) == iota((64, 256), 0)
        high = jnp.where(match, (local >> 6).astype(F32), 0.0)
        low = jnp.where(match, (local & 63).astype(F32), 0.0)
        parts = jnp.concatenate([high, low], axis=0).astype(BF16)
        return total + dot_nt(parts, one_hot(pair(owner_s, index), 128))

    filled = lax.fori_loop(0, 32, fill, jnp.zeros((128, 128), F32), unroll=PU)
    locals_of = (filled[0:64] * 64.0 + filled[64:128]).astype(jnp.int32)
    table_ref[...] = locals_of
    padded = jnp.concatenate([locals_of, jnp.zeros((64, 128), jnp.int32)], axis=0)
    request_ref[...] = jnp.transpose(padded)


def plan(keys_sorted):
    return pl.pallas_call(
        plan_kernel,
        out_shape=(
            jax.ShapeDtypeStruct((128, 128), jnp.int32),
            jax.ShapeDtypeStruct((64, 128), jnp.int32),
        ),
        in_specs=[VMEM],
        out_specs=(VMEM, VMEM),
        scratch_shapes=[pltpu.VMEM((64, 128), jnp.int32)] * 3,
        compiler_params=pltpu.CompilerParams(vmem_limit_bytes=32 * 1024 * 1024),
    )(keys_sorted)


def find_kernel(table_ref, keys_ref, centre_ref, slots_ref):
    keys = keys_ref[...]
    owner = (keys >> 12) & 127
    local = keys & (G_DEV - 1)
    rank = jnp.zeros((64, 128), jnp.int32)
    for place in range(63, -1, -1):
        row = jnp.broadcast_to(table_ref[place : place + 1, :], (64, 128))
        found = jnp.take_along_axis(row, owner, axis=1, mode="promise_in_bounds")
        rank = jnp.where(found == local, place, rank)
    tile = jnp.where(
        iota((64, 128), 0) < 32,
        jnp.broadcast_to(centre_ref[0:1, :], (64, 128)),
        jnp.broadcast_to(centre_ref[1:2, :], (64, 128)),
    )
    slots_ref[0:64, :] = (rank >> 5) * 128 + owner
    slots_ref[64:128, :] = rank & 31
    slots_ref[128:192, :] = jnp.where(keys < SENTINEL, tile, -1)


def find(table, keys, centre):
    return pl.pallas_call(
        find_kernel,
        out_shape=jax.ShapeDtypeStruct((192, 128), jnp.int32),
        in_specs=[VMEM] * 3,
        out_specs=VMEM,
        compiler_params=pltpu.CompilerParams(vmem_limit_bytes=32 * 1024 * 1024),
    )(table, keys, centre)


def gather_all(table_ref, high_ref, low_ref, out_ref, size):
    def step(index, carry):
        lanes = one_hot(pair(high_ref, index), 256)
        match = pair(low_ref, index) == iota((size, 256), 0)
        found = dot_nn(table_ref[...], lanes)
        for feature in range(9):
            parts = [
                found[(9 * part + feature) * size : (9 * part + feature + 1) * size]
                for part in range(3)
            ]
            picked = jnp.where(match, (parts[0] + parts[1]) + parts[2], 0.0)
            line = jnp.sum(picked, axis=0, keepdims=True)
            out_ref[pl.ds(64 * feature + 2 * index, 1), :] = line[:, 0:128]
            out_ref[pl.ds(64 * feature + 2 * index + 1, 1), :] = line[:, 128:256]
        return carry

    lax.fori_loop(0, 32, step, 0, unroll=GU)


def three_parts(value, table_ref, feature, size):
    high = value.astype(BF16)
    rest = value - high.astype(F32)
    middle = rest.astype(BF16)
    low = (rest - middle.astype(F32)).astype(BF16)
    for part, piece in enumerate((high, middle, low)):
        base = (9 * part + feature) * size
        table_ref[base : base + size, :] = piece


def project_kernel(params_ref, feats_ref, rows_s):
    rows_first(params_ref, rows_s)

    def row(index):
        return rows_s[index * 32 : (index + 1) * 32, :]

    rows = [row(index) for index in range(10)]
    feats = list(geometry(rows))
    feats.append(1.0 / (1.0 + jnp.exp(-row(10))))
    basis = directions(rows[0], rows[1], rows[2])
    for channel in range(3):
        total = 0.5 + SH_ZERO * row(11 + channel)
        for degree in range(1, 16):
            total = total + basis[degree - 1] * row(11 + 3 * degree + channel)
        feats.append(total)
    for index in range(9):
        feats_ref[index * 32 : (index + 1) * 32, :] = feats[index]


def project(params):
    return pl.pallas_call(
        project_kernel,
        out_shape=jax.ShapeDtypeStruct((288, 128), F32),
        in_specs=[VMEM],
        out_specs=VMEM,
        scratch_shapes=[pltpu.VMEM((59 * 32, 128), F32)],
        compiler_params=pltpu.CompilerParams(vmem_limit_bytes=32 * 1024 * 1024),
    )(params)


def serve_kernel(feats_ref, wanted_ref, out_ref, place_s, table_s, high_s, low_s):
    wanted = jnp.transpose(wanted_ref[...])[0:64]
    high_s[...] = (wanted >> 11) * 128 + (wanted & 127)
    low_s[...] = (wanted >> 7) & 15
    for feature in range(9):
        rows = feats_ref[feature * 32 : (feature + 1) * 32, :]
        three_parts(jnp.concatenate([rows[0:16], rows[16:32]], axis=1), table_s, feature, 16)
    gather_all(table_s, high_s, low_s, place_s, 16)
    place_s[576:640, :] = jnp.zeros((64, 128), F32)
    for part in range(5):
        out_ref[pl.ds(part, 128, stride=5), :] = jnp.transpose(
            place_s[part * 128 : (part + 1) * 128, :]
        )


def serve(feats, wanted):
    return pl.pallas_call(
        serve_kernel,
        out_shape=jax.ShapeDtypeStruct((640, 128), F32),
        in_specs=[VMEM, VMEM],
        out_specs=VMEM,
        scratch_shapes=[
            pltpu.VMEM((640, 128), F32),
            pltpu.VMEM((27 * 16, 256), BF16),
            pltpu.VMEM((64, 128), jnp.int32),
            pltpu.VMEM((64, 128), jnp.int32),
        ],
        compiler_params=pltpu.CompilerParams(vmem_limit_bytes=32 * 1024 * 1024),
    )(feats, wanted)


def pixel_basis():
    pixel = iota((24, 256), 1)
    across = (pixel & 15).astype(F32) - 7.5
    down = (pixel >> 4).astype(F32) - 7.5
    kind = iota((24, 256), 0)
    kind = jnp.where(kind >= 12, kind - 12, jnp.where(kind >= 6, kind - 6, kind))
    return select_monomial(kind, across, down)


def select_monomial(kind, across, down):
    value = jnp.where(kind == 0, across * across, 0.0)
    value = jnp.where(kind == 1, across * down, value)
    value = jnp.where(kind == 2, down * down, value)
    value = jnp.where(kind == 3, across, value)
    value = jnp.where(kind == 4, down, value)
    return jnp.where(kind == 5, 1.0, value).astype(BF16)


def render_kernel(
    arrived_ref,
    slots_ref,
    target_ref,
    out_ref,
    loss_ref,
    places_s,
    table_s,
    coef_s,
    alpha_s,
    weight_s,
    sums_s,
    grads_s,
    weights_s,
    parts_s,
):
    for part in range(5):
        table_s[part * 128 : (part + 1) * 128, :] = jnp.transpose(
            arrived_ref[pl.ds(part, 128, stride=5), :]
        )
    for feature in range(9):
        base = feature * 64
        three_parts(
            jnp.concatenate(
                [table_s[base : base + 32, :], table_s[base + 32 : base + 64, :]], axis=1
            ),
            places_s,
            feature,
            32,
        )
    gather_all(
        places_s, slots_ref.at[pl.ds(0, 64), :], slots_ref.at[pl.ds(64, 64), :], table_s, 32
    )
    feats = [table_s[feature * 64 : (feature + 1) * 64, :] for feature in range(9)]
    tile = slots_ref[128:192, :]
    live = tile >= 0
    rel_u = feats[0] - ((tile & (TILES_X - 1)).astype(F32) * 16.0 + 7.5)
    rel_v = feats[1] - ((tile >> 6).astype(F32) * 16.0 + 7.5)
    conic_1, conic_2, conic_3 = (feats[2], feats[3], feats[4])
    h_1 = 0.5 * conic_1
    h_3 = 0.5 * conic_3
    pull_u = conic_1 * rel_u + conic_2 * rel_v
    pull_v = conic_3 * rel_v + conic_2 * rel_u
    centre_e = 0.5 * (conic_1 * rel_u * rel_u + conic_3 * rel_v * rel_v) + conic_2 * rel_u * rel_v
    level = jnp.log2(0.99 * feats[5])
    coefs = [
        -LOG2_E * h_1,
        -LOG2_E * conic_2,
        -LOG2_E * h_3,
        LOG2_E * pull_u,
        LOG2_E * pull_v,
        level - LOG2_E * centre_e,
    ]
    for index in range(6):
        value = jnp.where(live, coefs[index], -1024.0 if index == 5 else 0.0)
        high = value.astype(BF16).astype(F32)
        rest = value - high
        middle = rest.astype(BF16).astype(F32)
        coef_s[pl.ds(index, 64, stride=24), :] = high
        coef_s[pl.ds(index + 6, 64, stride=24), :] = middle
        coef_s[pl.ds(index + 12, 64, stride=24), :] = rest - middle
    for channel in range(3):
        value = feats[6 + channel]
        high = value.astype(BF16).astype(F32)
        coef_s[pl.ds(18 + channel, 64, stride=24), :] = high
        coef_s[pl.ds(21 + channel, 64, stride=24), :] = value - high

    def chunk_rows(group, index):
        return pl.ds(pl.multiple_of(group * 4096 + index * 256, 256), 256)

    def coef_of(group, index):
        base = group * 32 + index * 2
        return jnp.concatenate(
            [
                coef_s[pl.ds(pl.multiple_of((base + half) * 24, 8), 24), :]
                for half in range(2)
            ],
            axis=1,
        )

    basis = pixel_basis()
    pixel = iota((256, 128), 0)
    moments = select_monomial(
        iota((256, 128), 1), (pixel & 15).astype(F32) - 7.5, (pixel >> 4).astype(F32) - 7.5
    )

    diagonal = (iota((8, 256), 1) & 7) == iota((8, 256), 0)

    def spread(coef, base):
        return jnp.concatenate(
            [
                jnp.where(
                    diagonal,
                    jnp.broadcast_to(coef[base + channel : base + channel + 1], (8, 256)),
                    0.0,
                )
                for channel in range(3)
            ],
            axis=0,
        )

    def forward(index, state):
        results = []
        for group in range(2):
            left, colors = state[2 * group : 2 * group + 2]
            coef = coef_of(group, index)
            alpha = jnp.exp2(dot_nn(jnp.transpose(coef).astype(BF16), basis))
            rows = chunk_rows(group, index)
            alpha_s[rows, :] = alpha
            parts = []
            for slot in range(32):
                weight = alpha[slot * 8 : (slot + 1) * 8] * left
                left = left - weight
                parts.append(weight)
            weights = jnp.concatenate(parts, axis=0)
            weight_s[rows, :] = weights
            high, low = split(weights)
            parts_s[rows, 512:768] = high
            parts_s[rows, 768:1024] = low
            col_high = spread(coef, 18)
            col_low = spread(coef, 21)
            both = dot_nn(jnp.concatenate([col_high, col_low], axis=0).astype(BF16), high)
            colors = colors + both[0:24] + both[24:48] + dot_nn(col_high.astype(BF16), low)
            results += [left, colors]
        return tuple(results)

    start = (jnp.ones((8, 256), F32), jnp.zeros((24, 256), F32))
    state = lax.fori_loop(0, 16, forward, start + start, unroll=FU)
    err_all = []
    for group in range(2):
        errors = state[2 * group + 1] - target_ref[group * 24 : (group + 1) * 24, :]
        squares = errors * errors
        total = jnp.sum(squares[0:8] + squares[8:16] + squares[16:24], axis=1, keepdims=True)
        loss_ref[group * 8 : (group + 1) * 8, :] = jnp.broadcast_to(total / 16.0, (8, 128))
        err_high, err_low = split(errors * 0.125)
        err_all.append(jnp.concatenate([err_high, err_low, err_high], axis=0))
        turned = jnp.transpose(
            jnp.concatenate(
                [jnp.zeros((8, 256), F32), err_high.astype(F32), err_low.astype(F32)]
                + [jnp.zeros((72, 256), F32)],
                axis=0,
            )
        )
        lane = iota((256, 128), 1)
        weights_s[group, 0:256, :] = moments
        weights_s[group, 256:512, :] = moments
        weights_s[group, 512:768, :] = turned.astype(BF16)
        weights_s[group, 768:1024, :] = jnp.where(lane < 32, turned, 0.0).astype(BF16)

    def backward(step, state):
        index = 15 - step
        results = []
        for group in range(2):
            behind = state[group]
            err_three = err_all[group]
            coef = coef_of(group, index)
            col_high = spread(coef, 18)
            col_low = spread(coef, 21)
            col_three = jnp.concatenate([col_high, col_high, col_low], axis=0)
            shades = dot_nn(jnp.transpose(col_three).astype(BF16), err_three)
            rows = chunk_rows(group, index)
            alpha = alpha_s[rows, :]
            weights = weight_s[rows, :]
            parts = []
            for slot in range(31, -1, -1):
                cut = slice(slot * 8, (slot + 1) * 8)
                gap = shades[cut] - behind
                parts.append(weights[cut] * gap)
                behind = behind + alpha[cut] * gap
            pulls = jnp.concatenate(parts[::-1], axis=0)
            pull_high, pull_low = split(pulls)
            parts_s[rows, 0:256] = pull_high
            parts_s[rows, 256:512] = pull_low
            results.append(behind)
        return tuple(results)

    zero = jnp.zeros((8, 256), F32)
    lax.fori_loop(0, 16, backward, (zero, zero), unroll=BU)

    for group in range(2):

        def reduce_pixels(index, carry):
            rows = pl.ds(pl.multiple_of(group * 4096 + index * MROWS, MROWS), MROWS)
            sums = dot_nn(parts_s[rows, :], weights_s[group])
            for part in range(MROWS // 128):
                turned = jnp.transpose(sums[part * 128 : (part + 1) * 128])
                base = (group * 32 + index * (MROWS // 128) + part) * 16
                tints = turned[8:32] + turned[32:56]
                own = [
                    jnp.sum(
                        jnp.where(diagonal[:, 0:128], tints[ch * 8 : (ch + 1) * 8], 0.0),
                        axis=0,
                        keepdims=True,
                    )
                    for ch in range(3)
                ]
                sums_s[pl.ds(pl.multiple_of(base, 8), 8), :] = turned[0:8]
                for channel in range(3):
                    sums_s[pl.ds(base + 8 + channel, 1), :] = own[channel]
            return carry

        lax.fori_loop(0, 4096 // MROWS, reduce_pixels, 0, unroll=MU)

    def sums_of(index):
        return sums_s[pl.ds(index, 64, stride=16), :]

    m_xx, m_xy, m_yy, m_x, m_y, m_0 = [sums_of(index) for index in range(6)]
    s_x = m_x - rel_u * m_0
    s_y = m_y - rel_v * m_0
    s_xx = m_xx - 2.0 * rel_u * m_x + rel_u * rel_u * m_0
    s_yy = m_yy - 2.0 * rel_v * m_y + rel_v * rel_v * m_0
    s_xy = m_xy - rel_u * m_y - rel_v * m_x + rel_u * rel_v * m_0
    slot_grads = [
        conic_1 * s_x + conic_2 * s_y,
        conic_3 * s_y + conic_2 * s_x,
        -0.5 * s_xx,
        -s_xy,
        -0.5 * s_yy,
        m_0,
        sums_of(8),
        sums_of(9),
        sums_of(10),
    ]
    for index in range(9):
        grads_s[pl.ds(index, 64, stride=16), :] = jnp.where(live, slot_grads[index], 0.0)
    grads_s[pl.ds(9, 64, stride=16), :] = slots_ref[0:64, :].astype(F32)
    grads_s[pl.ds(10, 64, stride=16), :] = slots_ref[64:128, :].astype(F32)

    def scatter(index, total):
        return scatter_step(two_rows(grads_s, index), 32, total)

    collected = lax.fori_loop(0, 32, scatter, jnp.zeros((288, 256), F32), unroll=SU)
    for feature in range(9):
        piece = collected[feature * 32 : (feature + 1) * 32]
        table_s[feature * 64 : feature * 64 + 32, :] = piece[:, 0:128]
        table_s[feature * 64 + 32 : feature * 64 + 64, :] = piece[:, 128:256]
    table_s[576:640, :] = jnp.zeros((64, 128), F32)
    for part in range(5):
        out_ref[pl.ds(part, 128, stride=5), :] = jnp.transpose(
            table_s[part * 128 : (part + 1) * 128, :]
        )


def two_rows(ref, index):
    return jnp.concatenate(
        [
            ref[pl.ds(pl.multiple_of(index * 32, 16), 16), :],
            ref[pl.ds(pl.multiple_of(index * 32 + 16, 16), 16), :],
        ],
        axis=1,
    )


def scatter_step(both, size, total):
    lanes = one_hot(both[9:10].astype(jnp.int32), 256)
    match = iota((size, 256), 0) == both[10:11].astype(jnp.int32)
    high = both.astype(BF16).astype(F32)
    low = both - high
    masked = [
        jnp.where(match, jnp.broadcast_to(part[feature : feature + 1], (size, 256)), 0.0)
        for part in (high, low)
        for feature in range(9)
    ]
    found = dot_nt(jnp.concatenate(masked, axis=0).astype(BF16), lanes)
    return total + found[0 : 9 * size] + found[9 * size : 18 * size]


def render(arrived, slots, target):
    return pl.pallas_call(
        render_kernel,
        out_shape=(
            jax.ShapeDtypeStruct((640, 128), F32),
            jax.ShapeDtypeStruct((16, 128), F32),
        ),
        in_specs=[VMEM] * 3,
        out_specs=(VMEM, VMEM),
        scratch_shapes=[
            pltpu.VMEM((27 * 32, 256), BF16),
            pltpu.VMEM((640, 128), F32),
            pltpu.VMEM((64 * 24, 128), F32),
            pltpu.VMEM((8192, 256), F32),
            pltpu.VMEM((8192, 256), F32),
            pltpu.VMEM((64 * 16, 128), F32),
            pltpu.VMEM((64 * 16, 128), F32),
            pltpu.VMEM((2, 1024, 128), BF16),
            pltpu.VMEM((8192, 1024), BF16),
        ],
        compiler_params=pltpu.CompilerParams(vmem_limit_bytes=48 * 1024 * 1024),
    )(arrived, slots, target)


def learn_rate(index):
    if index < 3:
        return 0.0016
    if index < 6:
        return 0.005
    if index < 10:
        return 0.001
    if index < 11:
        return 0.05
    return 0.0025 if index < 14 else 0.000125


def update_kernel(
    received_ref,
    wanted_ref,
    params_ref,
    one_ref,
    two_ref,
    rates_ref,
    new_params_ref,
    new_one_ref,
    new_two_ref,
    rows_s,
    grads_s,
    table_s,
):
    wanted = jnp.transpose(wanted_ref[...])[0:64]
    piece = wanted >> 7
    for part in range(5):
        turned = jnp.transpose(received_ref[pl.ds(part, 128, stride=5), :])
        table_s[pl.ds(2 * part, 64, stride=16), :] = turned[0:64]
        if part < 4:
            table_s[pl.ds(2 * part + 1, 64, stride=16), :] = turned[64:128]
    table_s[pl.ds(9, 64, stride=16), :] = ((piece >> 4) * 128 + (wanted & 127)).astype(F32)
    table_s[pl.ds(10, 64, stride=16), :] = (piece & 15).astype(F32)

    def scatter(index, total):
        return scatter_step(two_rows(table_s, index), 16, total)

    collected = lax.fori_loop(0, 32, scatter, jnp.zeros((144, 256), F32), unroll=SU)

    def grad_of(feature):
        part = collected[feature * 16 : (feature + 1) * 16]
        return jnp.concatenate([part[:, 0:128], part[:, 128:256]], axis=0)

    rows_first(params_ref, rows_s)

    def row(index):
        return rows_s[index * 32 : (index + 1) * 32, :]

    def put(index, value):
        grads_s[index * 32 : (index + 1) * 32, :] = value

    rows = [row(index) for index in range(10)]
    unused, pull_geometry = jax.vjp(geometry, rows)
    (geo_grads,) = pull_geometry(tuple(grad_of(feature) for feature in range(5)))
    put(10, grad_of(5) * (1.0 / (1.0 + jnp.exp(row(10)))))
    basis, pull_basis = jax.vjp(directions, rows[0], rows[1], rows[2])
    tints = [grad_of(6 + channel) for channel in range(3)]
    basis_grads = []
    for channel in range(3):
        put(11 + channel, SH_ZERO * tints[channel])
    for degree in range(1, 16):
        total = None
        for channel in range(3):
            index = 11 + 3 * degree + channel
            put(index, basis[degree - 1] * tints[channel])
            term = row(index) * tints[channel]
            total = term if total is None else total + term
        basis_grads.append(total)
    mean_grads = pull_basis(basis_grads)
    for index in range(10):
        put(index, geo_grads[index] + mean_grads[index] if index < 3 else geo_grads[index])

    fix_one = 1.0 / (1.0 - BETA_ONE**ADAM_STEP)
    fix_two = 1.0 / (1.0 - BETA_TWO**ADAM_STEP)
    for base in range(0, 59, 8):
        size = min(8, 59 - base)
        rate = jnp.broadcast_to(rates_ref[base : base + size, 0:1], (size, 128))
        for piece in range(32):
            cut = (slice(base, base + size), slice(piece * 128, (piece + 1) * 128))
            grad = grads_s[pl.ds(base * 32 + piece, size, stride=32), :]
            one = BETA_ONE * one_ref[cut] + (1.0 - BETA_ONE) * grad
            two = BETA_TWO * two_ref[cut] + (1.0 - BETA_TWO) * grad * grad
            new_one_ref[cut] = one
            new_two_ref[cut] = two
            step = one * fix_one / (jnp.sqrt(two * fix_two) + ADAM_EPS)
            new_params_ref[cut] = params_ref[cut] - rate * step


def update(received, wanted, params, moment_one, moment_two):
    rates = np.zeros((64, 128), np.float32)
    rates[0:59] = np.array([learn_rate(index) for index in range(59)], np.float32)[:, None]
    whole = jax.ShapeDtypeStruct((59, G_DEV), F32)
    return pl.pallas_call(
        update_kernel,
        out_shape=(whole, whole, whole),
        in_specs=[VMEM] * 6,
        out_specs=(VMEM, VMEM, VMEM),
        scratch_shapes=[
            pltpu.VMEM((59 * 32, 128), F32),
            pltpu.VMEM((59 * 32, 128), F32),
            pltpu.VMEM((64 * 16, 128), F32),
        ],
        compiler_params=pltpu.CompilerParams(vmem_limit_bytes=48 * 1024 * 1024),
    )(received, wanted, params, moment_one, moment_two, jnp.asarray(rates))


def slot_keys(visible, counts):
    live = jnp.arange(128, dtype=jnp.int32)[None, None, :] < counts[:, :, None]
    keys = jnp.where(live.reshape(visible.shape), visible, SENTINEL)
    return jnp.transpose(keys.reshape(2, 8, 512), (0, 2, 1)).reshape(64, 128)


def exchange(array):
    flat = array.reshape(N_DEV, 1, -1)
    flat = lax.all_to_all(flat, "dev", split_axis=0, concat_axis=0, tiled=True)
    return flat.reshape(array.shape)


def shards(params, moment_one, moment_two, visible, counts, tile_pos, target):
    keys = slot_keys(visible, counts)
    keys_sorted = lax.sort(keys.reshape(-1), is_stable=False).reshape(64, 128)
    request, table = plan(keys_sorted)
    wanted = exchange(request)
    feats = project(params)
    centre = jnp.tile(tile_pos.reshape(2, 8), (1, 16))
    slots = find(table, keys, centre)
    colours = target.astype(F32).reshape(2, 8, 3, 256)
    colours = jnp.transpose(colours, (0, 2, 1, 3)).reshape(48, 256)
    arrived = exchange(serve(feats, wanted))
    grads, loss = render(arrived, slots, colours)
    received = exchange(grads)
    outs = update(received, wanted, params, moment_one, moment_two)
    return (loss[:, 0], *outs)


def solution(mesh):
    placed = (
        P(None, "dev"),
        P(None, "dev"),
        P(None, "dev"),
        P("dev", None),
        P("dev", None),
        P("dev"),
        P("dev", None, None),
    )
    return jax.shard_map(
        shards,
        mesh=mesh,
        in_specs=placed,
        out_specs=(P("dev"), P(None, "dev"), P(None, "dev"), P(None, "dev")),
        check_vma=False,
    )
```

```python
import jax
import jax.numpy as jnp
from jax import lax
from jax.experimental import pallas as pl
from jax.experimental.pallas import tpu as pltpu
from jax.sharding import PartitionSpec as P

N_DEV = 128
G_DEV = 4096
CAP = 64
TILES_X = 64
ADAM_STEP = 1000
SENTINEL = N_DEV * G_DEV
SCREEN_W = 1024.0
SCREEN_H = 512.0

SH_ZERO = 0.28209479177387814
SH_ONE = 0.4886025119029199
SH_TWO = (
    1.0925484305920792,
    -1.0925484305920792,
    0.31539156525252005,
    -1.0925484305920792,
    0.5462742152960396,
)
SH_THREE = (
    -0.5900435899266435,
    2.890611442640554,
    -0.4570457994644658,
    0.3731763325901154,
    -0.4570457994644658,
    1.445305721320277,
    -0.5900435899266435,
)
BETA_ONE = 0.9
BETA_TWO = 0.999
ADAM_EPS = 1e-15
LOG2_E = 1.4426950408889634

F32 = jnp.float32
BF16 = jnp.bfloat16
VMEM = pl.BlockSpec(memory_space=pltpu.VMEM)
ANY = pl.BlockSpec(memory_space=pl.ANY)
FU = 4
BU = 4
PU = 8
GU = 4
SU = 8
MROWS = 1024
MU = 1


def harmonics(dir_x, dir_y, dir_z):
    sq_x = dir_x * dir_x
    sq_y = dir_y * dir_y
    sq_z = dir_z * dir_z
    return [
        -SH_ONE * dir_y,
        SH_ONE * dir_z,
        -SH_ONE * dir_x,
        SH_TWO[0] * dir_x * dir_y,
        SH_TWO[1] * dir_y * dir_z,
        SH_TWO[2] * (2.0 * sq_z - sq_x - sq_y),
        SH_TWO[3] * dir_x * dir_z,
        SH_TWO[4] * (sq_x - sq_y),
        SH_THREE[0] * dir_y * (3.0 * sq_x - sq_y),
        SH_THREE[1] * dir_x * dir_y * dir_z,
        SH_THREE[2] * dir_y * (4.0 * sq_z - sq_x - sq_y),
        SH_THREE[3] * dir_z * (2.0 * sq_z - 3.0 * sq_x - 3.0 * sq_y),
        SH_THREE[4] * dir_x * (4.0 * sq_z - sq_x - sq_y),
        SH_THREE[5] * dir_z * (sq_x - sq_y),
        SH_THREE[6] * dir_x * (sq_x - 3.0 * sq_y),
    ]


def directions(mean_x, mean_y, depths):
    distance = jnp.sqrt(mean_x * mean_x + mean_y * mean_y + depths * depths)
    return harmonics(mean_x / distance, mean_y / distance, depths / distance)


def geometry(rows):
    mean_x, mean_y, depths = (rows[0], rows[1], rows[2])
    scale_x = jnp.exp(rows[3])
    scale_y = jnp.exp(rows[4])
    scale_z = jnp.exp(rows[5])
    quat_len = jnp.maximum(
        jnp.sqrt(rows[6] * rows[6] + rows[7] * rows[7] + rows[8] * rows[8] + rows[9] * rows[9]),
        0.5,
    )
    quat_w = rows[6] / quat_len
    quat_x = rows[7] / quat_len
    quat_y = rows[8] / quat_len
    quat_z = rows[9] / quat_len
    rot_xx = 1.0 - 2.0 * (quat_y * quat_y + quat_z * quat_z)
    rot_xy = 2.0 * (quat_x * quat_y - quat_w * quat_z)
    rot_xz = 2.0 * (quat_x * quat_z + quat_w * quat_y)
    rot_yx = 2.0 * (quat_x * quat_y + quat_w * quat_z)
    rot_yy = 1.0 - 2.0 * (quat_x * quat_x + quat_z * quat_z)
    rot_yz = 2.0 * (quat_y * quat_z - quat_w * quat_x)
    rot_zx = 2.0 * (quat_x * quat_z - quat_w * quat_y)
    rot_zy = 2.0 * (quat_y * quat_z + quat_w * quat_x)
    rot_zz = 1.0 - 2.0 * (quat_x * quat_x + quat_y * quat_y)
    m_xx, m_xy, m_xz = (rot_xx * scale_x, rot_xy * scale_y, rot_xz * scale_z)
    m_yx, m_yy, m_yz = (rot_yx * scale_x, rot_yy * scale_y, rot_yz * scale_z)
    m_zx, m_zy, m_zz = (rot_zx * scale_x, rot_zy * scale_y, rot_zz * scale_z)
    cov_xx = m_xx * m_xx + m_xy * m_xy + m_xz * m_xz
    cov_xy = m_xx * m_yx + m_xy * m_yy + m_xz * m_yz
    cov_xz = m_xx * m_zx + m_xy * m_zy + m_xz * m_zz
    cov_yy = m_yx * m_yx + m_yy * m_yy + m_yz * m_yz
    cov_yz = m_yx * m_zx + m_yy * m_zy + m_yz * m_zz
    cov_zz = m_zx * m_zx + m_zy * m_zy + m_zz * m_zz
    focal = 1.2 * SCREEN_W
    inverse = 1.0 / depths
    jac_xx = focal * inverse
    jac_xz = -focal * mean_x * inverse * inverse
    jac_yy = focal * inverse
    jac_yz = -focal * mean_y * inverse * inverse
    plane_a = (
        jac_xx * jac_xx * cov_xx + 2.0 * jac_xx * jac_xz * cov_xz + jac_xz * jac_xz * cov_zz + 0.3
    )
    plane_b = (
        jac_xx * jac_yy * cov_xy
        + jac_xx * jac_yz * cov_xz
        + jac_xz * jac_yy * cov_yz
        + jac_xz * jac_yz * cov_zz
    )
    plane_c = (
        jac_yy * jac_yy * cov_yy + 2.0 * jac_yy * jac_yz * cov_yz + jac_yz * jac_yz * cov_zz + 0.3
    )
    determ = plane_a * plane_c - plane_b * plane_b
    return (
        focal * mean_x * inverse + 0.5 * SCREEN_W,
        focal * mean_y * inverse + 0.5 * SCREEN_H,
        plane_c / determ,
        -plane_b / determ,
        plane_a / determ,
    )


def split(value):
    high = value.astype(BF16)
    return (high, (value - high.astype(F32)).astype(BF16))


def dot_nt(left, right):
    return lax.dot_general(left, right, (((1,), (1,)), ((), ())), preferred_element_type=F32)


def dot_nn(left, right):
    return jnp.dot(left, right, preferred_element_type=F32)


def one_hot(index_row, size):
    rows = lax.broadcasted_iota(jnp.int32, (size, index_row.shape[1]), 0)
    return jnp.where(rows == index_row, 1.0, 0.0).astype(BF16)


def iota(shape, axis):
    return lax.broadcasted_iota(jnp.int32, shape, axis)


def rows_first(ref, out_ref):
    for base in range(0, 59, 8):
        size = min(8, 59 - base)
        for piece in range(32):
            out_ref[pl.ds(base * 32 + piece, size, stride=32), :] = ref[
                base : base + size, piece * 128 : (piece + 1) * 128
            ]


def pair(ref, index):
    return jnp.concatenate(
        [ref[pl.ds(2 * index, 1), :], ref[pl.ds(2 * index + 1, 1), :]], axis=1
    )


def sort_all(parts):
    sublane = iota((8, 128), 0)
    lane = iota((8, 128), 1)

    def bit_of(bit, number):
        if bit < 3:
            return (number >> bit) & 1
        if bit < 6:
            return (sublane >> (bit - 3)) & 1
        return (lane >> (bit - 6)) & 1

    flipped = [0] * 8
    for level in range(1, 14):
        for number in range(8):
            turn = bit_of(level, number) if level < 13 else 0
            change = flipped[number] ^ turn
            if not isinstance(change, int):
                parts[number] = parts[number] ^ (0 - change)
            elif change:
                parts[number] = ~parts[number]
            flipped[number] = turn
        for bit in range(level - 1, -1, -1):
            if bit < 3:
                stride = 1 << bit
                for number in range(8):
                    if not number & stride:
                        one, two = parts[number], parts[number + stride]
                        parts[number] = jnp.minimum(one, two)
                        parts[number + stride] = jnp.maximum(one, two)
            else:
                axis, size = (0, 8) if bit < 6 else (1, 128)
                stride = 1 << (bit - 3 if bit < 6 else bit - 6)
                is_low = bit_of(bit, 0) == 0
                for number in range(8):
                    here = parts[number]
                    up = pltpu.roll(here, size - stride, axis)
                    down = pltpu.roll(here, stride, axis) if 2 * stride < size else up
                    parts[number] = jnp.where(
                        is_low, jnp.minimum(here, up), jnp.maximum(here, down)
                    )
    return parts


def plan_kernel(visible_ref, counts_ref, request_ref, owner_s, rank_s, local_s):
    lane = iota((8, 128), 1)
    sublane = iota((8, 128), 0)
    keys = []
    for rows in (slice(0, 8), slice(8, 16)):
        for block in range(4):
            limit = jnp.broadcast_to(counts_ref[rows, block : block + 1], (8, 128))
            ids = visible_ref[rows, block * 128 : (block + 1) * 128]
            keys.append(jnp.where(lane < limit, ids, SENTINEL))
    keys = sort_all(keys)

    def earlier(value, fill):
        shifted = pltpu.roll(value, 1, 0)
        shifted = jnp.where(sublane == 0, pltpu.roll(shifted, 1, 1), shifted)
        return jnp.where((sublane == 0) & (lane == 0), fill, shifted)

    before = [earlier(keys[7], -1)] + keys[0:7]
    fresh = [(keys[n] != before[n]) & (keys[n] < SENTINEL) for n in range(8)]
    opens = [(keys[n] >> 12) != (before[n] >> 12) for n in range(8)]
    counts = []
    for number in range(8):
        one = jnp.where(fresh[number], 1, 0)
        counts.append(one if number == 0 else counts[-1] + one)
    column = counts[7]
    for step in (1, 2, 4):
        column = column + jnp.where(sublane >= step, pltpu.roll(column, step, 0), 0)
    whole = jnp.broadcast_to(column[7:8], (8, 128)).astype(F32).astype(BF16)
    strictly = jnp.where(iota((128, 128), 0) < iota((128, 128), 1), 1.0, 0.0).astype(BF16)
    offset = dot_nn(whole, strictly).astype(jnp.int32) + column - counts[7] - 1
    counts = [count + offset for count in counts]
    bases = []
    for number in range(8):
        one = jnp.where(opens[number], counts[number], 0)
        bases.append(one if number == 0 else jnp.maximum(bases[-1], one))
    column = bases[7]
    for step in (1, 2, 4):
        column = jnp.maximum(column, jnp.where(sublane >= step, pltpu.roll(column, step, 0), 0))
    whole = jnp.broadcast_to(column[7:8], (8, 128))
    for step in (1, 2, 4, 8, 16, 32, 64):
        whole = jnp.maximum(whole, jnp.where(lane >= step, pltpu.roll(whole, step, 1), 0))
    whole = jnp.where(lane >= 1, pltpu.roll(whole, 1, 1), 0)
    above = jnp.maximum(whole, jnp.where(sublane >= 1, pltpu.roll(column, 1, 0), 0))
    for number in range(8):
        rows = slice(number * 8, (number + 1) * 8)
        rank = counts[number] - jnp.maximum(bases[number], above)
        owner_s[rows, :] = keys[number] >> 12
        rank_s[rows, :] = jnp.where(fresh[number], rank, -1)
        local_s[rows, :] = keys[number] & (G_DEV - 1)

    def fill(index, total):
        local = pair(local_s, index)
        match = pair(rank_s, index) == iota((64, 256), 0)
        high = jnp.where(match, (local >> 6).astype(F32), 0.0)
        low = jnp.where(match, (local & 63).astype(F32), 0.0)
        parts = jnp.concatenate([high, low], axis=0).astype(BF16)
        return total + dot_nt(parts, one_hot(pair(owner_s, index), 128))

    filled = lax.fori_loop(0, 32, fill, jnp.zeros((128, 128), F32), unroll=PU)
    locals_of = (filled[0:64] * 64.0 + filled[64:128]).astype(jnp.int32)
    padded = jnp.concatenate([locals_of, jnp.zeros((64, 128), jnp.int32)], axis=0)
    request_ref[...] = jnp.transpose(padded)


def plan(visible, counts):
    return pl.pallas_call(
        plan_kernel,
        out_shape=jax.ShapeDtypeStruct((128, 128), jnp.int32),
        in_specs=[VMEM] * 2,
        out_specs=VMEM,
        scratch_shapes=[pltpu.VMEM((64, 128), jnp.int32)] * 3,
        compiler_params=pltpu.CompilerParams(vmem_limit_bytes=32 * 1024 * 1024),
    )(visible, counts)


def find_kernel(request_ref, keys_ref, centre_ref, slots_ref):
    table = jnp.transpose(request_ref[...])
    keys = keys_ref[...]
    owner = (keys >> 12) & 127
    local = keys & (G_DEV - 1)
    rank = jnp.zeros((64, 128), jnp.int32)
    for place in range(63, -1, -1):
        row = jnp.broadcast_to(table[place : place + 1], (64, 128))
        found = jnp.take_along_axis(row, owner, axis=1, mode="promise_in_bounds")
        rank = jnp.where(found == local, place, rank)
    tile = jnp.where(
        iota((64, 128), 0) < 32,
        jnp.broadcast_to(centre_ref[0:1, :], (64, 128)),
        jnp.broadcast_to(centre_ref[1:2, :], (64, 128)),
    )
    slots_ref[0:64, :] = (rank >> 5) * 128 + owner
    slots_ref[64:128, :] = rank & 31
    slots_ref[128:192, :] = jnp.where(keys < SENTINEL, tile, -1)


def find(request, keys, centre):
    return pl.pallas_call(
        find_kernel,
        out_shape=jax.ShapeDtypeStruct((192, 128), jnp.int32),
        in_specs=[VMEM] * 3,
        out_specs=VMEM,
        compiler_params=pltpu.CompilerParams(vmem_limit_bytes=32 * 1024 * 1024),
    )(request, keys, centre)


def gather_all(table_ref, high_ref, low_ref, out_ref, size):
    def step(index, carry):
        lanes = one_hot(pair(high_ref, index), 256)
        match = pair(low_ref, index) == iota((size, 256), 0)
        found = dot_nn(table_ref[...], lanes)
        for feature in range(9):
            parts = [
                found[(9 * part + feature) * size : (9 * part + feature + 1) * size]
                for part in range(3)
            ]
            picked = jnp.where(match, (parts[0] + parts[1]) + parts[2], 0.0)
            line = jnp.sum(picked, axis=0, keepdims=True)
            out_ref[pl.ds(64 * feature + 2 * index, 1), :] = line[:, 0:128]
            out_ref[pl.ds(64 * feature + 2 * index + 1, 1), :] = line[:, 128:256]
        return carry

    lax.fori_loop(0, 32, step, 0, unroll=GU)


def three_parts(value, table_ref, feature, size):
    high = value.astype(BF16)
    rest = value - high.astype(F32)
    middle = rest.astype(BF16)
    low = (rest - middle.astype(F32)).astype(BF16)
    for part, piece in enumerate((high, middle, low)):
        base = (9 * part + feature) * size
        table_ref[base : base + size, :] = piece


def project_kernel(params_ref, feats_ref, rows_s):
    rows_first(params_ref, rows_s)

    def row(index):
        return rows_s[index * 32 : (index + 1) * 32, :]

    rows = [row(index) for index in range(10)]
    feats = list(geometry(rows))
    feats.append(1.0 / (1.0 + jnp.exp(-row(10))))
    basis = directions(rows[0], rows[1], rows[2])
    for channel in range(3):
        total = 0.5 + SH_ZERO * row(11 + channel)
        for degree in range(1, 16):
            total = total + basis[degree - 1] * row(11 + 3 * degree + channel)
        feats.append(total)
    for index in range(9):
        rows = feats[index]
        three_parts(jnp.concatenate([rows[0:16], rows[16:32]], axis=1), feats_ref, index, 16)


def project(params):
    return pl.pallas_call(
        project_kernel,
        out_shape=jax.ShapeDtypeStruct((27 * 16, 256), BF16),
        in_specs=[VMEM],
        out_specs=VMEM,
        scratch_shapes=[pltpu.VMEM((59 * 32, 128), F32)],
        compiler_params=pltpu.CompilerParams(vmem_limit_bytes=32 * 1024 * 1024),
    )(params)


def serve_kernel(table_ref, wanted_ref, out_ref, place_s, high_s, low_s):
    wanted = jnp.transpose(wanted_ref[...])[0:64]
    high_s[...] = (wanted >> 11) * 128 + (wanted & 127)
    low_s[...] = (wanted >> 7) & 15
    gather_all(table_ref, high_s, low_s, place_s, 16)
    place_s[576:640, :] = jnp.zeros((64, 128), F32)
    for part in range(5):
        out_ref[pl.ds(part, 128, stride=5), :] = jnp.transpose(
            place_s[part * 128 : (part + 1) * 128, :]
        )


def serve(feats, wanted):
    return pl.pallas_call(
        serve_kernel,
        out_shape=jax.ShapeDtypeStruct((640, 128), F32),
        in_specs=[VMEM, VMEM],
        out_specs=VMEM,
        scratch_shapes=[
            pltpu.VMEM((640, 128), F32),
            pltpu.VMEM((64, 128), jnp.int32),
            pltpu.VMEM((64, 128), jnp.int32),
        ],
        compiler_params=pltpu.CompilerParams(vmem_limit_bytes=32 * 1024 * 1024),
    )(feats, wanted)


def pixel_basis():
    pixel = iota((24, 256), 1)
    across = (pixel & 15).astype(F32) - 7.5
    down = (pixel >> 4).astype(F32) - 7.5
    kind = iota((24, 256), 0)
    kind = jnp.where(kind >= 12, kind - 12, jnp.where(kind >= 6, kind - 6, kind))
    return select_monomial(kind, across, down)


def select_monomial(kind, across, down):
    value = jnp.where(kind == 0, across * across, 0.0)
    value = jnp.where(kind == 1, across * down, value)
    value = jnp.where(kind == 2, down * down, value)
    value = jnp.where(kind == 3, across, value)
    value = jnp.where(kind == 4, down, value)
    return jnp.where(kind == 5, 1.0, value).astype(BF16)


def render_kernel(
    arrived_ref,
    slots_hbm,
    target_hbm,
    out_ref,
    loss_ref,
    places_s,
    table_s,
    coef_s,
    alpha_s,
    weight_s,
    sums_s,
    grads_s,
    weights_s,
    parts_s,
    slots_ref,
    target_ref,
    sems,
):
    slots_copy = pltpu.make_async_copy(slots_hbm, slots_ref, sems.at[0])
    target_copy = pltpu.make_async_copy(target_hbm, target_ref, sems.at[1])
    slots_copy.start()
    target_copy.start()
    for part in range(5):
        table_s[part * 128 : (part + 1) * 128, :] = jnp.transpose(
            arrived_ref[pl.ds(part, 128, stride=5), :]
        )
    for feature in range(9):
        base = feature * 64
        three_parts(
            jnp.concatenate(
                [table_s[base : base + 32, :], table_s[base + 32 : base + 64, :]], axis=1
            ),
            places_s,
            feature,
            32,
        )
    slots_copy.wait()
    target_copy.wait()
    gather_all(
        places_s, slots_ref.at[pl.ds(0, 64), :], slots_ref.at[pl.ds(64, 64), :], table_s, 32
    )
    feats = [table_s[feature * 64 : (feature + 1) * 64, :] for feature in range(9)]
    tile = slots_ref[128:192, :]
    live = tile >= 0
    rel_u = feats[0] - ((tile & (TILES_X - 1)).astype(F32) * 16.0 + 7.5)
    rel_v = feats[1] - ((tile >> 6).astype(F32) * 16.0 + 7.5)
    conic_1, conic_2, conic_3 = (feats[2], feats[3], feats[4])
    h_1 = 0.5 * conic_1
    h_3 = 0.5 * conic_3
    pull_u = conic_1 * rel_u + conic_2 * rel_v
    pull_v = conic_3 * rel_v + conic_2 * rel_u
    centre_e = 0.5 * (conic_1 * rel_u * rel_u + conic_3 * rel_v * rel_v) + conic_2 * rel_u * rel_v
    level = jnp.log2(0.99 * feats[5])
    coefs = [
        -LOG2_E * h_1,
        -LOG2_E * conic_2,
        -LOG2_E * h_3,
        LOG2_E * pull_u,
        LOG2_E * pull_v,
        level - LOG2_E * centre_e,
    ]
    for index in range(6):
        value = jnp.where(live, coefs[index], -1024.0 if index == 5 else 0.0)
        high = value.astype(BF16).astype(F32)
        rest = value - high
        middle = rest.astype(BF16).astype(F32)
        coef_s[pl.ds(index, 64, stride=24), :] = high
        coef_s[pl.ds(index + 6, 64, stride=24), :] = middle
        coef_s[pl.ds(index + 12, 64, stride=24), :] = rest - middle
    for channel in range(3):
        value = feats[6 + channel]
        high = value.astype(BF16).astype(F32)
        coef_s[pl.ds(18 + channel, 64, stride=24), :] = high
        coef_s[pl.ds(21 + channel, 64, stride=24), :] = value - high

    def chunk_rows(group, index):
        return pl.ds(pl.multiple_of(group * 4096 + index * 256, 256), 256)

    def coef_of(group, index):
        base = group * 32 + index * 2
        return jnp.concatenate(
            [
                coef_s[pl.ds(pl.multiple_of((base + half) * 24, 8), 24), :]
                for half in range(2)
            ],
            axis=1,
        )

    basis = pixel_basis()
    pixel = iota((256, 128), 0)
    moments = select_monomial(
        iota((256, 128), 1), (pixel & 15).astype(F32) - 7.5, (pixel >> 4).astype(F32) - 7.5
    )

    diagonal = (iota((8, 256), 1) & 7) == iota((8, 256), 0)

    def spread(coef, base):
        return jnp.concatenate(
            [
                jnp.where(
                    diagonal,
                    jnp.broadcast_to(coef[base + channel : base + channel + 1], (8, 256)),
                    0.0,
                )
                for channel in range(3)
            ],
            axis=0,
        )

    def forward(index, state):
        results = []
        for group in range(2):
            left, colors = state[2 * group : 2 * group + 2]
            coef = coef_of(group, index)
            alpha = jnp.exp2(dot_nn(jnp.transpose(coef).astype(BF16), basis))
            rows = chunk_rows(group, index)
            alpha_s[rows, :] = alpha
            parts = []
            for slot in range(32):
                weight = alpha[slot * 8 : (slot + 1) * 8] * left
                left = left - weight
                parts.append(weight)
            weights = jnp.concatenate(parts, axis=0)
            weight_s[rows, :] = weights
            high, low = split(weights)
            parts_s[rows, 512:768] = high
            parts_s[rows, 768:1024] = low
            col_high = spread(coef, 18)
            col_low = spread(coef, 21)
            both = dot_nn(jnp.concatenate([col_high, col_low], axis=0).astype(BF16), high)
            colors = colors + both[0:24] + both[24:48] + dot_nn(col_high.astype(BF16), low)
            results += [left, colors]
        return tuple(results)

    start = (jnp.ones((8, 256), F32), jnp.zeros((24, 256), F32))
    state = lax.fori_loop(0, 16, forward, start + start, unroll=FU)
    err_all = []
    for group in range(2):
        errors = state[2 * group + 1] - target_ref[group * 24 : (group + 1) * 24, :]
        squares = errors * errors
        total = jnp.sum(squares[0:8] + squares[8:16] + squares[16:24], axis=1, keepdims=True)
        loss_ref[group * 8 : (group + 1) * 8, :] = jnp.broadcast_to(total / 16.0, (8, 128))
        err_high, err_low = split(errors * 0.125)
        err_all.append(jnp.concatenate([err_high, err_low, err_high], axis=0))
        turned = jnp.transpose(
            jnp.concatenate(
                [jnp.zeros((8, 256), F32), err_high.astype(F32), err_low.astype(F32)]
                + [jnp.zeros((72, 256), F32)],
                axis=0,
            )
        )
        lane = iota((256, 128), 1)
        weights_s[group, 0:256, :] = moments
        weights_s[group, 256:512, :] = moments
        weights_s[group, 512:768, :] = turned.astype(BF16)
        weights_s[group, 768:1024, :] = jnp.where(lane < 32, turned, 0.0).astype(BF16)

    def backward(step, state):
        index = 15 - step
        results = []
        for group in range(2):
            behind = state[group]
            err_three = err_all[group]
            coef = coef_of(group, index)
            col_high = spread(coef, 18)
            col_low = spread(coef, 21)
            col_three = jnp.concatenate([col_high, col_high, col_low], axis=0)
            shades = dot_nn(jnp.transpose(col_three).astype(BF16), err_three)
            rows = chunk_rows(group, index)
            alpha = alpha_s[rows, :]
            weights = weight_s[rows, :]
            parts = []
            for slot in range(31, -1, -1):
                cut = slice(slot * 8, (slot + 1) * 8)
                gap = shades[cut] - behind
                parts.append(weights[cut] * gap)
                behind = behind + alpha[cut] * gap
            pulls = jnp.concatenate(parts[::-1], axis=0)
            pull_high, pull_low = split(pulls)
            parts_s[rows, 0:256] = pull_high
            parts_s[rows, 256:512] = pull_low
            results.append(behind)
        return tuple(results)

    zero = jnp.zeros((8, 256), F32)
    lax.fori_loop(0, 16, backward, (zero, zero), unroll=BU)

    for group in range(2):

        def reduce_pixels(index, carry):
            rows = pl.ds(pl.multiple_of(group * 4096 + index * MROWS, MROWS), MROWS)
            sums = dot_nn(parts_s[rows, :], weights_s[group])
            for part in range(MROWS // 128):
                turned = jnp.transpose(sums[part * 128 : (part + 1) * 128])
                base = (group * 32 + index * (MROWS // 128) + part) * 16
                tints = turned[8:32] + turned[32:56]
                own = [
                    jnp.sum(
                        jnp.where(diagonal[:, 0:128], tints[ch * 8 : (ch + 1) * 8], 0.0),
                        axis=0,
                        keepdims=True,
                    )
                    for ch in range(3)
                ]
                sums_s[pl.ds(pl.multiple_of(base, 8), 8), :] = turned[0:8]
                for channel in range(3):
                    sums_s[pl.ds(base + 8 + channel, 1), :] = own[channel]
            return carry

        lax.fori_loop(0, 4096 // MROWS, reduce_pixels, 0, unroll=MU)

    def sums_of(index):
        return sums_s[pl.ds(index, 64, stride=16), :]

    m_xx, m_xy, m_yy, m_x, m_y, m_0 = [sums_of(index) for index in range(6)]
    s_x = m_x - rel_u * m_0
    s_y = m_y - rel_v * m_0
    s_xx = m_xx - 2.0 * rel_u * m_x + rel_u * rel_u * m_0
    s_yy = m_yy - 2.0 * rel_v * m_y + rel_v * rel_v * m_0
    s_xy = m_xy - rel_u * m_y - rel_v * m_x + rel_u * rel_v * m_0
    slot_grads = [
        conic_1 * s_x + conic_2 * s_y,
        conic_3 * s_y + conic_2 * s_x,
        -0.5 * s_xx,
        -s_xy,
        -0.5 * s_yy,
        m_0,
        sums_of(8),
        sums_of(9),
        sums_of(10),
    ]
    for index in range(9):
        grads_s[pl.ds(index, 64, stride=16), :] = jnp.where(live, slot_grads[index], 0.0)
    grads_s[pl.ds(9, 64, stride=16), :] = slots_ref[0:64, :].astype(F32)
    grads_s[pl.ds(10, 64, stride=16), :] = slots_ref[64:128, :].astype(F32)

    def scatter(index, total):
        return scatter_step(two_rows(grads_s, index), 32, total)

    collected = lax.fori_loop(0, 32, scatter, jnp.zeros((288, 256), F32), unroll=SU)
    for feature in range(9):
        piece = collected[feature * 32 : (feature + 1) * 32]
        table_s[feature * 64 : feature * 64 + 32, :] = piece[:, 0:128]
        table_s[feature * 64 + 32 : feature * 64 + 64, :] = piece[:, 128:256]
    table_s[576:640, :] = jnp.zeros((64, 128), F32)
    for part in range(5):
        out_ref[pl.ds(part, 128, stride=5), :] = jnp.transpose(
            table_s[part * 128 : (part + 1) * 128, :]
        )


def two_rows(ref, index):
    return jnp.concatenate(
        [
            ref[pl.ds(pl.multiple_of(index * 32, 16), 16), :],
            ref[pl.ds(pl.multiple_of(index * 32 + 16, 16), 16), :],
        ],
        axis=1,
    )


def scatter_step(both, size, total):
    lanes = one_hot(both[9:10].astype(jnp.int32), 256)
    match = iota((size, 256), 0) == both[10:11].astype(jnp.int32)
    high = both.astype(BF16).astype(F32)
    low = both - high
    masked = [
        jnp.where(match, jnp.broadcast_to(part[feature : feature + 1], (size, 256)), 0.0)
        for part in (high, low)
        for feature in range(9)
    ]
    found = dot_nt(jnp.concatenate(masked, axis=0).astype(BF16), lanes)
    return total + found[0 : 9 * size] + found[9 * size : 18 * size]


def render(arrived, slots, target):
    return pl.pallas_call(
        render_kernel,
        out_shape=(
            jax.ShapeDtypeStruct((640, 128), F32),
            jax.ShapeDtypeStruct((16, 128), F32),
        ),
        in_specs=[VMEM, ANY, ANY],
        out_specs=(VMEM, VMEM),
        scratch_shapes=[
            pltpu.VMEM((27 * 32, 256), BF16),
            pltpu.VMEM((640, 128), F32),
            pltpu.VMEM((64 * 24, 128), F32),
            pltpu.VMEM((8192, 256), F32),
            pltpu.VMEM((8192, 256), F32),
            pltpu.VMEM((64 * 16, 128), F32),
            pltpu.VMEM((64 * 16, 128), F32),
            pltpu.VMEM((2, 1024, 128), BF16),
            pltpu.VMEM((8192, 1024), BF16),
            pltpu.VMEM((192, 128), jnp.int32),
            pltpu.VMEM((48, 256), F32),
            pltpu.SemaphoreType.DMA((2,)),
        ],
        compiler_params=pltpu.CompilerParams(vmem_limit_bytes=48 * 1024 * 1024),
    )(arrived, slots, target)


def learn_rate(index):
    if index < 3:
        return 0.0016
    if index < 6:
        return 0.005
    if index < 10:
        return 0.001
    if index < 11:
        return 0.05
    return 0.0025 if index < 14 else 0.000125


def update_kernel(
    received_ref,
    wanted_ref,
    params_ref,
    one_ref,
    two_ref,
    new_params_ref,
    new_one_ref,
    new_two_ref,
    rows_s,
    grads_s,
    table_s,
):
    wanted = jnp.transpose(wanted_ref[...])[0:64]
    piece = wanted >> 7
    for part in range(5):
        turned = jnp.transpose(received_ref[pl.ds(part, 128, stride=5), :])
        table_s[pl.ds(2 * part, 64, stride=16), :] = turned[0:64]
        if part < 4:
            table_s[pl.ds(2 * part + 1, 64, stride=16), :] = turned[64:128]
    table_s[pl.ds(9, 64, stride=16), :] = ((piece >> 4) * 128 + (wanted & 127)).astype(F32)
    table_s[pl.ds(10, 64, stride=16), :] = (piece & 15).astype(F32)

    def scatter(index, total):
        return scatter_step(two_rows(table_s, index), 16, total)

    collected = lax.fori_loop(0, 32, scatter, jnp.zeros((144, 256), F32), unroll=SU)

    def grad_of(feature):
        part = collected[feature * 16 : (feature + 1) * 16]
        return jnp.concatenate([part[:, 0:128], part[:, 128:256]], axis=0)

    rows_first(params_ref, rows_s)

    def row(index):
        return rows_s[index * 32 : (index + 1) * 32, :]

    def put(index, value):
        grads_s[index * 32 : (index + 1) * 32, :] = value

    rows = [row(index) for index in range(10)]
    unused, pull_geometry = jax.vjp(geometry, rows)
    (geo_grads,) = pull_geometry(tuple(grad_of(feature) for feature in range(5)))
    put(10, grad_of(5) * (1.0 / (1.0 + jnp.exp(row(10)))))
    basis, pull_basis = jax.vjp(directions, rows[0], rows[1], rows[2])
    tints = [grad_of(6 + channel) for channel in range(3)]
    basis_grads = []
    for channel in range(3):
        put(11 + channel, SH_ZERO * tints[channel])
    for degree in range(1, 16):
        total = None
        for channel in range(3):
            index = 11 + 3 * degree + channel
            put(index, basis[degree - 1] * tints[channel])
            term = row(index) * tints[channel]
            total = term if total is None else total + term
        basis_grads.append(total)
    mean_grads = pull_basis(basis_grads)
    for index in range(10):
        put(index, geo_grads[index] + mean_grads[index] if index < 3 else geo_grads[index])

    fix_one = 1.0 / (1.0 - BETA_ONE**ADAM_STEP)
    fix_two = 1.0 / (1.0 - BETA_TWO**ADAM_STEP)
    for base in range(0, 59, 8):
        size = min(8, 59 - base)
        rate = jnp.zeros((size, 128), F32)
        for index in range(size):
            rate = jnp.where(iota((size, 128), 0) == index, learn_rate(base + index), rate)
        for piece in range(32):
            cut = (slice(base, base + size), slice(piece * 128, (piece + 1) * 128))
            grad = grads_s[pl.ds(base * 32 + piece, size, stride=32), :]
            one = BETA_ONE * one_ref[cut] + (1.0 - BETA_ONE) * grad
            two = BETA_TWO * two_ref[cut] + (1.0 - BETA_TWO) * grad * grad
            new_one_ref[cut] = one
            new_two_ref[cut] = two
            step = one * fix_one / (jnp.sqrt(two * fix_two) + ADAM_EPS)
            new_params_ref[cut] = params_ref[cut] - rate * step


def update(received, wanted, params, moment_one, moment_two):
    whole = jax.ShapeDtypeStruct((59, G_DEV), F32)
    return pl.pallas_call(
        update_kernel,
        out_shape=(whole, whole, whole),
        in_specs=[VMEM] * 5,
        out_specs=(VMEM, VMEM, VMEM),
        scratch_shapes=[
            pltpu.VMEM((59 * 32, 128), F32),
            pltpu.VMEM((59 * 32, 128), F32),
            pltpu.VMEM((64 * 16, 128), F32),
        ],
        compiler_params=pltpu.CompilerParams(vmem_limit_bytes=48 * 1024 * 1024),
    )(received, wanted, params, moment_one, moment_two)


def slot_keys(visible, counts):
    live = jnp.arange(128, dtype=jnp.int32)[None, None, :] < counts[:, :, None]
    keys = jnp.where(live.reshape(visible.shape), visible, SENTINEL)
    return jnp.transpose(keys.reshape(2, 8, 512), (0, 2, 1)).reshape(64, 128)


def exchange(array):
    flat = array.reshape(N_DEV, 1, -1)
    flat = lax.all_to_all(flat, "dev", split_axis=0, concat_axis=0, tiled=True)
    return flat.reshape(array.shape)


def shards(params, moment_one, moment_two, visible, counts, tile_pos, target):
    keys = slot_keys(visible, counts)
    request = plan(visible, counts)
    wanted = exchange(request)
    feats = project(params)
    centre = jnp.tile(tile_pos.reshape(2, 8), (1, 16))
    slots = find(request, keys, centre)
    colours = target.astype(F32).reshape(2, 8, 3, 256)
    colours = jnp.transpose(colours, (0, 2, 1, 3)).reshape(48, 256)
    arrived = exchange(serve(feats, wanted))
    grads, loss = render(arrived, slots, colours)
    received = exchange(grads)
    outs = update(received, wanted, params, moment_one, moment_two)
    return (loss[:, 0], *outs)


def solution(mesh):
    placed = (
        P(None, "dev"),
        P(None, "dev"),
        P(None, "dev"),
        P("dev", None),
        P("dev", None),
        P("dev"),
        P("dev", None, None),
    )
    return jax.shard_map(
        shards,
        mesh=mesh,
        in_specs=placed,
        out_specs=(P("dev"), P(None, "dev"), P(None, "dev"), P(None, "dev")),
        check_vma=False,
    )
```

```python
import jax
import jax.numpy as jnp
from jax import lax
from jax.experimental import pallas as pl
from jax.experimental.pallas import tpu as pltpu
from jax.sharding import PartitionSpec as P

N_DEV = 128
G_DEV = 4096
CAP = 64
TILES_X = 64
ADAM_STEP = 1000
SENTINEL = N_DEV * G_DEV
SCREEN_W = 1024.0
SCREEN_H = 512.0

SH_ZERO = 0.28209479177387814
SH_ONE = 0.4886025119029199
SH_TWO = (
    1.0925484305920792,
    -1.0925484305920792,
    0.31539156525252005,
    -1.0925484305920792,
    0.5462742152960396,
)
SH_THREE = (
    -0.5900435899266435,
    2.890611442640554,
    -0.4570457994644658,
    0.3731763325901154,
    -0.4570457994644658,
    1.445305721320277,
    -0.5900435899266435,
)
BETA_ONE = 0.9
BETA_TWO = 0.999
ADAM_EPS = 1e-15
LOG2_E = 1.4426950408889634

F32 = jnp.float32
BF16 = jnp.bfloat16
VMEM = pl.BlockSpec(memory_space=pltpu.VMEM)
HBM = pl.BlockSpec(memory_space=pltpu.HBM)
PU = 8
GU = 4


def harmonics(dir_x, dir_y, dir_z):
    sq_x = dir_x * dir_x
    sq_y = dir_y * dir_y
    sq_z = dir_z * dir_z
    return [
        -SH_ONE * dir_y,
        SH_ONE * dir_z,
        -SH_ONE * dir_x,
        SH_TWO[0] * dir_x * dir_y,
        SH_TWO[1] * dir_y * dir_z,
        SH_TWO[2] * (2.0 * sq_z - sq_x - sq_y),
        SH_TWO[3] * dir_x * dir_z,
        SH_TWO[4] * (sq_x - sq_y),
        SH_THREE[0] * dir_y * (3.0 * sq_x - sq_y),
        SH_THREE[1] * dir_x * dir_y * dir_z,
        SH_THREE[2] * dir_y * (4.0 * sq_z - sq_x - sq_y),
        SH_THREE[3] * dir_z * (2.0 * sq_z - 3.0 * sq_x - 3.0 * sq_y),
        SH_THREE[4] * dir_x * (4.0 * sq_z - sq_x - sq_y),
        SH_THREE[5] * dir_z * (sq_x - sq_y),
        SH_THREE[6] * dir_x * (sq_x - 3.0 * sq_y),
    ]


def directions(mean_x, mean_y, depths):
    distance = jnp.sqrt(mean_x * mean_x + mean_y * mean_y + depths * depths)
    return harmonics(mean_x / distance, mean_y / distance, depths / distance)


def geometry(rows):
    mean_x, mean_y, depths = (rows[0], rows[1], rows[2])
    scale_x = jnp.exp(rows[3])
    scale_y = jnp.exp(rows[4])
    scale_z = jnp.exp(rows[5])
    quat_len = jnp.maximum(
        jnp.sqrt(rows[6] * rows[6] + rows[7] * rows[7] + rows[8] * rows[8] + rows[9] * rows[9]),
        0.5,
    )
    quat_w = rows[6] / quat_len
    quat_x = rows[7] / quat_len
    quat_y = rows[8] / quat_len
    quat_z = rows[9] / quat_len
    rot_xx = 1.0 - 2.0 * (quat_y * quat_y + quat_z * quat_z)
    rot_xy = 2.0 * (quat_x * quat_y - quat_w * quat_z)
    rot_xz = 2.0 * (quat_x * quat_z + quat_w * quat_y)
    rot_yx = 2.0 * (quat_x * quat_y + quat_w * quat_z)
    rot_yy = 1.0 - 2.0 * (quat_x * quat_x + quat_z * quat_z)
    rot_yz = 2.0 * (quat_y * quat_z - quat_w * quat_x)
    rot_zx = 2.0 * (quat_x * quat_z - quat_w * quat_y)
    rot_zy = 2.0 * (quat_y * quat_z + quat_w * quat_x)
    rot_zz = 1.0 - 2.0 * (quat_x * quat_x + quat_y * quat_y)
    m_xx, m_xy, m_xz = (rot_xx * scale_x, rot_xy * scale_y, rot_xz * scale_z)
    m_yx, m_yy, m_yz = (rot_yx * scale_x, rot_yy * scale_y, rot_yz * scale_z)
    m_zx, m_zy, m_zz = (rot_zx * scale_x, rot_zy * scale_y, rot_zz * scale_z)
    cov_xx = m_xx * m_xx + m_xy * m_xy + m_xz * m_xz
    cov_xy = m_xx * m_yx + m_xy * m_yy + m_xz * m_yz
    cov_xz = m_xx * m_zx + m_xy * m_zy + m_xz * m_zz
    cov_yy = m_yx * m_yx + m_yy * m_yy + m_yz * m_yz
    cov_yz = m_yx * m_zx + m_yy * m_zy + m_yz * m_zz
    cov_zz = m_zx * m_zx + m_zy * m_zy + m_zz * m_zz
    focal = 1.2 * SCREEN_W
    inverse = 1.0 / depths
    jac_xx = focal * inverse
    jac_xz = -focal * mean_x * inverse * inverse
    jac_yy = focal * inverse
    jac_yz = -focal * mean_y * inverse * inverse
    plane_a = (
        jac_xx * jac_xx * cov_xx + 2.0 * jac_xx * jac_xz * cov_xz + jac_xz * jac_xz * cov_zz + 0.3
    )
    plane_b = (
        jac_xx * jac_yy * cov_xy
        + jac_xx * jac_yz * cov_xz
        + jac_xz * jac_yy * cov_yz
        + jac_xz * jac_yz * cov_zz
    )
    plane_c = (
        jac_yy * jac_yy * cov_yy + 2.0 * jac_yy * jac_yz * cov_yz + jac_yz * jac_yz * cov_zz + 0.3
    )
    determ = plane_a * plane_c - plane_b * plane_b
    return (
        focal * mean_x * inverse + 0.5 * SCREEN_W,
        focal * mean_y * inverse + 0.5 * SCREEN_H,
        plane_c / determ,
        -plane_b / determ,
        plane_a / determ,
    )


def split(value):
    high = value.astype(BF16)
    return (high, (value - high.astype(F32)).astype(BF16))


def dot_nt(left, right):
    return lax.dot_general(left, right, (((1,), (1,)), ((), ())), preferred_element_type=F32)


def dot_nn(left, right):
    return jnp.dot(left, right, preferred_element_type=F32)


def one_hot(index_row, size):
    rows = lax.broadcasted_iota(jnp.int32, (size, index_row.shape[1]), 0)
    return jnp.where(rows == index_row, 1.0, 0.0).astype(BF16)


def iota(shape, axis):
    return lax.broadcasted_iota(jnp.int32, shape, axis)


def rows_first(ref, out_ref):
    for base in range(0, 59, 8):
        size = min(8, 59 - base)
        for piece in range(32):
            out_ref[pl.ds(base * 32 + piece, size, stride=32), :] = ref[
                base : base + size, piece * 128 : (piece + 1) * 128
            ]


def pair(ref, index):
    return jnp.concatenate(
        [ref[pl.ds(2 * index, 1), :], ref[pl.ds(2 * index + 1, 1), :]], axis=1
    )


def sort_all(parts):
    sublane = iota((8, 128), 0)
    lane = iota((8, 128), 1)

    def bit_of(bit, number):
        if bit < 3:
            return (number >> bit) & 1
        if bit < 6:
            return (sublane >> (bit - 3)) & 1
        return (lane >> (bit - 6)) & 1

    flipped = [0] * 8
    for level in range(1, 14):
        for number in range(8):
            turn = bit_of(level, number) if level < 13 else 0
            change = flipped[number] ^ turn
            if not isinstance(change, int):
                parts[number] = parts[number] ^ (0 - change)
            elif change:
                parts[number] = ~parts[number]
            flipped[number] = turn
        for bit in range(level - 1, -1, -1):
            if bit < 3:
                stride = 1 << bit
                for number in range(8):
                    if not number & stride:
                        one, two = parts[number], parts[number + stride]
                        parts[number] = jnp.minimum(one, two)
                        parts[number + stride] = jnp.maximum(one, two)
            else:
                axis, size = (0, 8) if bit < 6 else (1, 128)
                stride = 1 << (bit - 3 if bit < 6 else bit - 6)
                is_low = bit_of(bit, 0) == 0
                for number in range(8):
                    here = parts[number]
                    up = pltpu.roll(here, size - stride, axis)
                    down = pltpu.roll(here, stride, axis) if 2 * stride < size else up
                    parts[number] = jnp.where(
                        is_low, jnp.minimum(here, up), jnp.maximum(here, down)
                    )
    return parts


def plan_kernel(visible_ref, request_ref, owner_s, rank_s, local_s):
    lane = iota((8, 128), 1)
    sublane = iota((8, 128), 0)
    keys = []
    for rows in (slice(0, 8), slice(8, 16)):
        for block in range(4):
            ids = visible_ref[rows, block * 128 : (block + 1) * 128]
            keys.append(jnp.where(ids < 0, SENTINEL, ids))
    keys = sort_all(keys)

    def earlier(value, fill):
        shifted = pltpu.roll(value, 1, 0)
        shifted = jnp.where(sublane == 0, pltpu.roll(shifted, 1, 1), shifted)
        return jnp.where((sublane == 0) & (lane == 0), fill, shifted)

    before = [earlier(keys[7], -1)] + keys[0:7]
    fresh = [(keys[n] != before[n]) & (keys[n] < SENTINEL) for n in range(8)]
    opens = [(keys[n] >> 12) != (before[n] >> 12) for n in range(8)]
    counts = []
    for number in range(8):
        one = jnp.where(fresh[number], 1, 0)
        counts.append(one if number == 0 else counts[-1] + one)
    column = counts[7]
    for step in (1, 2, 4):
        column = column + jnp.where(sublane >= step, pltpu.roll(column, step, 0), 0)
    whole = jnp.broadcast_to(column[7:8], (8, 128)).astype(F32).astype(BF16)
    strictly = jnp.where(iota((128, 128), 0) < iota((128, 128), 1), 1.0, 0.0).astype(BF16)
    offset = dot_nn(whole, strictly).astype(jnp.int32) + column - counts[7] - 1
    counts = [count + offset for count in counts]
    bases = []
    for number in range(8):
        one = jnp.where(opens[number], counts[number], 0)
        bases.append(one if number == 0 else jnp.maximum(bases[-1], one))
    column = bases[7]
    for step in (1, 2, 4):
        column = jnp.maximum(column, jnp.where(sublane >= step, pltpu.roll(column, step, 0), 0))
    whole = jnp.broadcast_to(column[7:8], (8, 128))
    for step in (1, 2, 4, 8, 16, 32, 64):
        whole = jnp.maximum(whole, jnp.where(lane >= step, pltpu.roll(whole, step, 1), 0))
    whole = jnp.where(lane >= 1, pltpu.roll(whole, 1, 1), 0)
    above = jnp.maximum(whole, jnp.where(sublane >= 1, pltpu.roll(column, 1, 0), 0))
    for number in range(8):
        rows = slice(number * 8, (number + 1) * 8)
        rank = counts[number] - jnp.maximum(bases[number], above)
        owner_s[rows, :] = keys[number] >> 12
        rank_s[rows, :] = jnp.where(fresh[number], rank, -1)
        local_s[rows, :] = keys[number] & (G_DEV - 1)

    def fill(index, total):
        local = pair(local_s, index)
        match = pair(rank_s, index) == iota((64, 256), 0)
        high = jnp.where(match, (local >> 6).astype(F32), 0.0)
        low = jnp.where(match, (local & 63).astype(F32), 0.0)
        parts = jnp.concatenate([high, low], axis=0).astype(BF16)
        return total + dot_nt(parts, one_hot(pair(owner_s, index), 128))

    filled = lax.fori_loop(0, 32, fill, jnp.zeros((128, 128), F32), unroll=PU)
    locals_of = (filled[0:64] * 64.0 + filled[64:128]).astype(jnp.int32)
    padded = jnp.concatenate([locals_of, jnp.zeros((64, 128), jnp.int32)], axis=0)
    request_ref[...] = jnp.transpose(padded)


def plan(visible):
    return pl.pallas_call(
        plan_kernel,
        out_shape=jax.ShapeDtypeStruct((128, 128), jnp.int32),
        in_specs=[VMEM],
        out_specs=VMEM,
        scratch_shapes=[pltpu.VMEM((64, 128), jnp.int32)] * 3,
        compiler_params=pltpu.CompilerParams(vmem_limit_bytes=32 * 1024 * 1024),
    )(visible)


def find_kernel(request_ref, keys_ref, centre_ref, slots_ref):
    table = jnp.transpose(request_ref[...])
    keys = keys_ref[...]
    owner = (keys >> 12) & 127
    local = keys & (G_DEV - 1)
    rank = jnp.zeros((64, 128), jnp.int32)
    for place in range(63, -1, -1):
        row = jnp.broadcast_to(table[place : place + 1], (64, 128))
        found = jnp.take_along_axis(row, owner, axis=1, mode="promise_in_bounds")
        rank = jnp.where(found == local, place, rank)
    tile = jnp.where(
        iota((64, 128), 0) < 32,
        jnp.broadcast_to(centre_ref[0:1, :], (64, 128)),
        jnp.broadcast_to(centre_ref[1:2, :], (64, 128)),
    )
    slots_ref[0:64, :] = (rank >> 5) * 128 + owner
    slots_ref[64:128, :] = rank & 31
    slots_ref[128:192, :] = jnp.where(keys < SENTINEL, tile, -1)


def find(request, keys, centre):
    return pl.pallas_call(
        find_kernel,
        out_shape=jax.ShapeDtypeStruct((192, 128), jnp.int32),
        in_specs=[VMEM] * 3,
        out_specs=VMEM,
        compiler_params=pltpu.CompilerParams(vmem_limit_bytes=32 * 1024 * 1024),
    )(request, keys, centre)


def gather_one(table_ref, high_ref, low_ref, out_ref, size, index):
    lanes = one_hot(pair(high_ref, index), 256)
    match = pair(low_ref, index) == iota((size, 256), 0)
    found = dot_nn(table_ref[...], lanes)
    for feature in range(9):
        parts = [
            found[(9 * part + feature) * size : (9 * part + feature + 1) * size]
            for part in range(3)
        ]
        picked = jnp.where(match, (parts[0] + parts[1]) + parts[2], 0.0)
        line = jnp.sum(picked, axis=0, keepdims=True)
        out_ref[pl.ds(64 * feature + 2 * index, 1), :] = line[:, 0:128]
        out_ref[pl.ds(64 * feature + 2 * index + 1, 1), :] = line[:, 128:256]


def three_parts(value, table_ref, feature, size):
    high = value.astype(BF16)
    rest = value - high.astype(F32)
    middle = rest.astype(BF16)
    low = (rest - middle.astype(F32)).astype(BF16)
    for part, piece in enumerate((high, middle, low)):
        base = (9 * part + feature) * size
        table_ref[base : base + size, :] = piece


def project_kernel(params_ref, feats_ref, rows_s):
    rows_first(params_ref, rows_s)

    def row(index):
        return rows_s[index * 32 : (index + 1) * 32, :]

    rows = [row(index) for index in range(10)]
    feats = list(geometry(rows))
    feats.append(1.0 / (1.0 + jnp.exp(-row(10))))
    basis = directions(rows[0], rows[1], rows[2])
    for channel in range(3):
        total = 0.5 + SH_ZERO * row(11 + channel)
        for degree in range(1, 16):
            total = total + basis[degree - 1] * row(11 + 3 * degree + channel)
        feats.append(total)
    for index in range(9):
        rows = feats[index]
        three_parts(jnp.concatenate([rows[0:16], rows[16:32]], axis=1), feats_ref, index, 16)


def project(params):
    return pl.pallas_call(
        project_kernel,
        out_shape=jax.ShapeDtypeStruct((27 * 16, 256), BF16),
        in_specs=[VMEM],
        out_specs=VMEM,
        scratch_shapes=[pltpu.VMEM((59 * 32, 128), F32)],
        compiler_params=pltpu.CompilerParams(vmem_limit_bytes=32 * 1024 * 1024),
    )(params)


def serve_kernel(table_ref, wanted_ref, out_ref, place_s, high_s, low_s):
    wanted = jnp.transpose(wanted_ref[...])[0:64]
    high_s[...] = (wanted >> 11) * 128 + (wanted & 127)
    low_s[...] = (wanted >> 7) & 15

    def step(index, carry):
        gather_one(table_ref, high_s, low_s, place_s, 16, index)
        return carry

    lax.fori_loop(0, 32, step, 0, unroll=GU)
    place_s[576:640, :] = jnp.zeros((64, 128), F32)
    for part in range(5):
        out_ref[pl.ds(part, 128, stride=5), :] = jnp.transpose(
            place_s[part * 128 : (part + 1) * 128, :]
        )


def serve(feats, wanted):
    return pl.pallas_call(
        serve_kernel,
        out_shape=jax.ShapeDtypeStruct((640, 128), F32),
        in_specs=[VMEM, VMEM],
        out_specs=VMEM,
        scratch_shapes=[
            pltpu.VMEM((640, 128), F32),
            pltpu.VMEM((64, 128), jnp.int32),
            pltpu.VMEM((64, 128), jnp.int32),
        ],
        compiler_params=pltpu.CompilerParams(vmem_limit_bytes=32 * 1024 * 1024),
    )(feats, wanted)


def pixel_basis():
    pixel = iota((24, 256), 1)
    across = (pixel & 15).astype(F32) - 7.5
    down = (pixel >> 4).astype(F32) - 7.5
    kind = iota((24, 256), 0)
    kind = jnp.where(kind >= 12, kind - 12, jnp.where(kind >= 6, kind - 6, kind))
    return select_monomial(kind, across, down)


def select_monomial(kind, across, down):
    value = jnp.where(kind == 0, across * across, 0.0)
    value = jnp.where(kind == 1, across * down, value)
    value = jnp.where(kind == 2, down * down, value)
    value = jnp.where(kind == 3, across, value)
    value = jnp.where(kind == 4, down, value)
    return jnp.where(kind == 5, 1.0, value).astype(BF16)


def render_kernel(
    arrived_ref,
    slots_hbm,
    target_hbm,
    out_ref,
    loss_ref,
    places_s,
    table_s,
    coef_s,
    alpha_s,
    weight_s,
    sums_s,
    feats_s,
    weights_s,
    parts_s,
    slots_ref,
    target_ref,
    sems,
):
    slots_copy = pltpu.make_async_copy(slots_hbm, slots_ref, sems.at[0])
    target_copy = pltpu.make_async_copy(target_hbm, target_ref, sems.at[1])
    slots_copy.start()
    target_copy.start()
    for part in range(5):
        table_s[part * 128 : (part + 1) * 128, :] = jnp.transpose(
            arrived_ref[pl.ds(part, 128, stride=5), :]
        )
    for feature in range(9):
        base = feature * 64
        three_parts(
            jnp.concatenate(
                [table_s[base : base + 32, :], table_s[base + 32 : base + 64, :]], axis=1
            ),
            places_s,
            feature,
            32,
        )
    slots_copy.wait()
    target_copy.wait()
    def gather(stage):
        for group in range(2):
            for step in range(4):
                gather_one(
                    places_s,
                    slots_ref.at[pl.ds(0, 64), :],
                    slots_ref.at[pl.ds(64, 64), :],
                    feats_s,
                    32,
                    group * 16 + stage * 4 + step,
                )

    def slot_values(first):
        feats = [feats_s[64 * f + first : 64 * f + first + 8, :] for f in range(9)]
        tile = slots_ref[128 + first : 136 + first, :]
        rel_u = feats[0] - ((tile & (TILES_X - 1)).astype(F32) * 16.0 + 7.5)
        rel_v = feats[1] - ((tile >> 6).astype(F32) * 16.0 + 7.5)
        return (feats, rel_u, rel_v, tile >= 0)

    def prepare(first):
        feats, rel_u, rel_v, live = slot_values(first)
        conic_1, conic_2, conic_3 = (feats[2], feats[3], feats[4])
        pull_u = conic_1 * rel_u + conic_2 * rel_v
        pull_v = conic_3 * rel_v + conic_2 * rel_u
        centre_e = (
            0.5 * (conic_1 * rel_u * rel_u + conic_3 * rel_v * rel_v) + conic_2 * rel_u * rel_v
        )
        level = jnp.log2(0.99 * feats[5])
        coefs = [
            -0.5 * LOG2_E * conic_1,
            -LOG2_E * conic_2,
            -0.5 * LOG2_E * conic_3,
            LOG2_E * pull_u,
            LOG2_E * pull_v,
            level - LOG2_E * centre_e,
        ]
        for index in range(6):
            value = jnp.where(live, coefs[index], -1024.0 if index == 5 else 0.0)
            high = value.astype(BF16).astype(F32)
            rest = value - high
            middle = rest.astype(BF16).astype(F32)
            coef_s[pl.ds(first * 24 + index, 8, stride=24), :] = high
            coef_s[pl.ds(first * 24 + index + 6, 8, stride=24), :] = middle
            coef_s[pl.ds(first * 24 + index + 12, 8, stride=24), :] = rest - middle
        for channel in range(3):
            value = feats[6 + channel]
            high = value.astype(BF16).astype(F32)
            coef_s[pl.ds(first * 24 + 18 + channel, 8, stride=24), :] = high
            coef_s[pl.ds(first * 24 + 21 + channel, 8, stride=24), :] = value - high

    def chunk_of(number, size):
        base = number * size
        return pl.ds(base if isinstance(base, int) else pl.multiple_of(base, 8), size)

    def chunk_rows(group, index):
        base = group * 4096 + index * 256
        return pl.ds(base if isinstance(base, int) else pl.multiple_of(base, 256), 256)

    def coef_of(group, index):
        base = group * 32 + index * 2
        return jnp.concatenate(
            [
                coef_s[chunk_of(base + half, 24), :]
                for half in range(2)
            ],
            axis=1,
        )

    basis = pixel_basis()
    pixel = iota((256, 128), 0)
    moments = select_monomial(
        iota((256, 128), 1), (pixel & 15).astype(F32) - 7.5, (pixel >> 4).astype(F32) - 7.5
    )

    diagonal = (iota((8, 256), 1) & 7) == iota((8, 256), 0)

    def spread(coef, base):
        return jnp.concatenate(
            [
                jnp.where(
                    diagonal,
                    jnp.broadcast_to(coef[base + channel : base + channel + 1], (8, 256)),
                    0.0,
                )
                for channel in range(3)
            ],
            axis=0,
        )

    def forward(index, state):
        results = []
        for group in range(2):
            left, colors = state[2 * group : 2 * group + 2]
            coef = coef_of(group, index)
            alpha = jnp.exp2(dot_nn(jnp.transpose(coef).astype(BF16), basis))
            rows = chunk_rows(group, index)
            alpha_s[rows, :] = alpha
            parts = []
            for slot in range(32):
                weight = alpha[slot * 8 : (slot + 1) * 8] * left
                left = left - weight
                parts.append(weight)
            weights = jnp.concatenate(parts, axis=0)
            weight_s[rows, :] = weights
            high, low = split(weights)
            parts_s[rows, 512:768] = high
            parts_s[rows, 768:1024] = low
            col_high = spread(coef, 18)
            col_low = spread(coef, 21)
            both = dot_nn(jnp.concatenate([col_high, col_low], axis=0).astype(BF16), high)
            colors = colors + both[0:24] + both[24:48] + dot_nn(col_high.astype(BF16), low)
            results += [left, colors]
        return tuple(results)

    start = (jnp.ones((8, 256), F32), jnp.zeros((24, 256), F32))
    state = start + start
    gather(0)
    for stage in range(4):
        if stage < 3:
            gather(stage + 1)
        for group in range(2):
            prepare(group * 32 + stage * 8)
        for step in range(4):
            state = forward(4 * stage + step, state)
    err_all = []
    for group in range(2):
        errors = state[2 * group + 1] - target_ref[group * 24 : (group + 1) * 24, :]
        squares = errors * errors
        total = jnp.sum(squares[0:8] + squares[8:16] + squares[16:24], axis=1, keepdims=True)
        loss_ref[group * 8 : (group + 1) * 8, :] = jnp.broadcast_to(total / 16.0, (8, 128))
        err_high, err_low = split(errors * 0.125)
        err_all.append(jnp.concatenate([err_high, err_low, err_high], axis=0))
        turned = jnp.transpose(
            jnp.concatenate(
                [jnp.zeros((8, 256), F32), err_high.astype(F32), err_low.astype(F32)]
                + [jnp.zeros((72, 256), F32)],
                axis=0,
            )
        )
        lane = iota((256, 128), 1)
        weights_s[group, 0:256, :] = moments
        weights_s[group, 256:512, :] = moments
        weights_s[group, 512:768, :] = turned.astype(BF16)
        weights_s[group, 768:1024, :] = jnp.where(lane < 32, turned, 0.0).astype(BF16)

    def backward(step, state):
        index = 15 - step
        results = []
        for group in range(2):
            behind = state[group]
            err_three = err_all[group]
            coef = coef_of(group, index)
            col_high = spread(coef, 18)
            col_low = spread(coef, 21)
            col_three = jnp.concatenate([col_high, col_high, col_low], axis=0)
            shades = dot_nn(jnp.transpose(col_three).astype(BF16), err_three)
            rows = chunk_rows(group, index)
            alpha = alpha_s[rows, :]
            weights = weight_s[rows, :]
            parts = []
            for slot in range(31, -1, -1):
                cut = slice(slot * 8, (slot + 1) * 8)
                gap = shades[cut] - behind
                parts.append(weights[cut] * gap)
                behind = behind + alpha[cut] * gap
            pulls = jnp.concatenate(parts[::-1], axis=0)
            pull_high, pull_low = split(pulls)
            parts_s[rows, 0:256] = pull_high
            parts_s[rows, 256:512] = pull_low
            results.append(behind)
        return tuple(results)

    zero = jnp.zeros((8, 256), F32)
    def reduce_pixels(stage):
        for group in range(2):
            first = group * 4096 + (3 - stage) * 1024
            sums = dot_nn(parts_s[first : first + 1024, :], weights_s[group])
            for part in range(8):
                turned = jnp.transpose(sums[part * 128 : (part + 1) * 128])
                base = (first // 128 + part) * 16
                tints = turned[8:32] + turned[32:56]
                sums_s[base : base + 8, :] = turned[0:8]
                for channel in range(3):
                    own = jnp.where(
                        diagonal[:, 0:128], tints[channel * 8 : (channel + 1) * 8], 0.0
                    )
                    sums_s[base + 8 + channel : base + 9 + channel, :] = jnp.sum(
                        own, axis=0, keepdims=True
                    )

    def scatter(stage, total):
        steps = []
        for group in range(2):
            first = group * 32 + (3 - stage) * 8
            feats, rel_u, rel_v, live = slot_values(first)
            conic_1, conic_2, conic_3 = (feats[2], feats[3], feats[4])

            def sums_of(index):
                return sums_s[pl.ds(first * 16 + index, 8, stride=16), :]

            m_xx, m_xy, m_yy, m_x, m_y, m_0 = [sums_of(index) for index in range(6)]
            s_x = m_x - rel_u * m_0
            s_y = m_y - rel_v * m_0
            s_xx = m_xx - 2.0 * rel_u * m_x + rel_u * rel_u * m_0
            s_yy = m_yy - 2.0 * rel_v * m_y + rel_v * rel_v * m_0
            s_xy = m_xy - rel_u * m_y - rel_v * m_x + rel_u * rel_v * m_0
            slot_grads = [
                conic_1 * s_x + conic_2 * s_y,
                conic_3 * s_y + conic_2 * s_x,
                -0.5 * s_xx,
                -s_xy,
                -0.5 * s_yy,
                m_0,
                sums_of(8),
                sums_of(9),
                sums_of(10),
            ]
            slot_grads = [jnp.where(live, grad, 0.0) for grad in slot_grads]
            steps.append(
                (
                    slot_grads,
                    slots_ref[first : first + 8, :],
                    slots_ref[64 + first : 72 + first, :],
                )
            )
        return total + scatter_rows(steps, 32)

    state = (zero, zero)
    collected = jnp.zeros((288, 256), F32)
    for stage in range(6):
        if stage >= 2:
            collected = scatter(stage - 2, collected)
        if 1 <= stage < 5:
            reduce_pixels(stage - 1)
        if stage < 4:
            for step in range(4):
                state = backward(4 * stage + step, state)
    for feature in range(9):
        piece = collected[feature * 32 : (feature + 1) * 32]
        table_s[feature * 64 : feature * 64 + 32, :] = piece[:, 0:128]
        table_s[feature * 64 + 32 : feature * 64 + 64, :] = piece[:, 128:256]
    table_s[576:640, :] = jnp.zeros((64, 128), F32)
    for part in range(5):
        out_ref[pl.ds(part, 128, stride=5), :] = jnp.transpose(
            table_s[part * 128 : (part + 1) * 128, :]
        )


def scatter_rows(steps, size):
    lanes, masked_high, masked_low = [], [], []
    for values, high, low in steps:
        tops = [value.astype(BF16).astype(F32) for value in values]
        rests = [value - top for value, top in zip(values, tops)]
        for row in range(8):
            cut = slice(row, row + 1)
            lanes.append(one_hot(high[cut], 256))
            match = low[cut] == iota((size, 128), 0)
            for parts, found in ((tops, masked_high), (rests, masked_low)):
                found.append(
                    jnp.concatenate(
                        [
                            jnp.where(match, jnp.broadcast_to(part[cut], (size, 128)), 0.0)
                            for part in parts
                        ],
                        axis=0,
                    ).astype(BF16)
                )
    masked = jnp.concatenate(
        [jnp.concatenate(masked_high, axis=1), jnp.concatenate(masked_low, axis=1)], axis=0
    )
    found = dot_nt(masked, jnp.concatenate(lanes, axis=1))
    return found[0 : 9 * size] + found[9 * size : 18 * size]


def render(arrived, slots, target):
    return pl.pallas_call(
        render_kernel,
        out_shape=(
            jax.ShapeDtypeStruct((640, 128), F32),
            jax.ShapeDtypeStruct((16, 128), F32),
        ),
        in_specs=[VMEM, HBM, HBM],
        out_specs=(VMEM, VMEM),
        scratch_shapes=[
            pltpu.VMEM((27 * 32, 256), BF16),
            pltpu.VMEM((640, 128), F32),
            pltpu.VMEM((64 * 24, 128), F32),
            pltpu.VMEM((8192, 256), F32),
            pltpu.VMEM((8192, 256), F32),
            pltpu.VMEM((64 * 16, 128), F32),
            pltpu.VMEM((576, 128), F32),
            pltpu.VMEM((2, 1024, 128), BF16),
            pltpu.VMEM((8192, 1024), BF16),
            pltpu.VMEM((192, 128), jnp.int32),
            pltpu.VMEM((48, 256), F32),
            pltpu.SemaphoreType.DMA((2,)),
        ],
        compiler_params=pltpu.CompilerParams(vmem_limit_bytes=48 * 1024 * 1024),
    )(arrived, slots, target)


def learn_rate(index):
    if index < 3:
        return 0.0016
    if index < 6:
        return 0.005
    if index < 10:
        return 0.001
    if index < 11:
        return 0.05
    return 0.0025 if index < 14 else 0.000125


def update_kernel(
    received_ref,
    wanted_ref,
    params_ref,
    one_ref,
    two_ref,
    new_params_ref,
    new_one_ref,
    new_two_ref,
    rows_s,
    grads_s,
    table_s,
):
    wanted = jnp.transpose(wanted_ref[...])[0:64]
    piece = wanted >> 7
    for part in range(5):
        turned = jnp.transpose(received_ref[pl.ds(part, 128, stride=5), :])
        table_s[part * 128 : (part + 1) * 128, :] = turned
    high = (piece >> 4) * 128 + (wanted & 127)
    low = piece & 15
    collected = jnp.zeros((144, 256), F32)
    for group in range(4):
        steps = []
        for first in (group * 16, group * 16 + 8):
            rows = slice(first, first + 8)
            values = [table_s[f * 64 + first : f * 64 + first + 8, :] for f in range(9)]
            steps.append((values, high[rows], low[rows]))
        collected = collected + scatter_rows(steps, 16)

    def grad_of(feature):
        part = collected[feature * 16 : (feature + 1) * 16]
        return jnp.concatenate([part[:, 0:128], part[:, 128:256]], axis=0)

    rows_first(params_ref, rows_s)

    def row(index):
        return rows_s[index * 32 : (index + 1) * 32, :]

    def put(index, value):
        grads_s[index * 32 : (index + 1) * 32, :] = value

    rows = [row(index) for index in range(10)]
    unused, pull_geometry = jax.vjp(geometry, rows)
    (geo_grads,) = pull_geometry(tuple(grad_of(feature) for feature in range(5)))
    put(10, grad_of(5) * (1.0 / (1.0 + jnp.exp(row(10)))))
    basis, pull_basis = jax.vjp(directions, rows[0], rows[1], rows[2])
    tints = [grad_of(6 + channel) for channel in range(3)]
    basis_grads = []
    for channel in range(3):
        put(11 + channel, SH_ZERO * tints[channel])
    for degree in range(1, 16):
        total = None
        for channel in range(3):
            index = 11 + 3 * degree + channel
            put(index, basis[degree - 1] * tints[channel])
            term = row(index) * tints[channel]
            total = term if total is None else total + term
        basis_grads.append(total)
    mean_grads = pull_basis(basis_grads)
    for index in range(10):
        put(index, geo_grads[index] + mean_grads[index] if index < 3 else geo_grads[index])

    fix_one = 1.0 / (1.0 - BETA_ONE**ADAM_STEP)
    fix_two = 1.0 / (1.0 - BETA_TWO**ADAM_STEP)
    for base in range(0, 59, 8):
        size = min(8, 59 - base)
        rate = jnp.zeros((size, 128), F32)
        for index in range(size):
            rate = jnp.where(iota((size, 128), 0) == index, learn_rate(base + index), rate)
        for piece in range(32):
            cut = (slice(base, base + size), slice(piece * 128, (piece + 1) * 128))
            grad = grads_s[pl.ds(base * 32 + piece, size, stride=32), :]
            one = BETA_ONE * one_ref[cut] + (1.0 - BETA_ONE) * grad
            two = BETA_TWO * two_ref[cut] + (1.0 - BETA_TWO) * grad * grad
            new_one_ref[cut] = one
            new_two_ref[cut] = two
            step = one * fix_one / (jnp.sqrt(two * fix_two) + ADAM_EPS)
            new_params_ref[cut] = params_ref[cut] - rate * step


def update(received, wanted, params, moment_one, moment_two):
    whole = jax.ShapeDtypeStruct((59, G_DEV), F32)
    return pl.pallas_call(
        update_kernel,
        out_shape=(whole, whole, whole),
        in_specs=[VMEM] * 5,
        out_specs=(VMEM, VMEM, VMEM),
        scratch_shapes=[
            pltpu.VMEM((59 * 32, 128), F32),
            pltpu.VMEM((59 * 32, 128), F32),
            pltpu.VMEM((640, 128), F32),
        ],
        compiler_params=pltpu.CompilerParams(vmem_limit_bytes=48 * 1024 * 1024),
    )(received, wanted, params, moment_one, moment_two)


def slot_keys(visible):
    keys = jnp.where(visible < 0, SENTINEL, visible)
    return jnp.transpose(keys.reshape(2, 8, 512), (0, 2, 1)).reshape(64, 128)


def exchange(array):
    flat = array.reshape(N_DEV, 1, -1)
    flat = lax.all_to_all(flat, "dev", split_axis=0, concat_axis=0, tiled=True)
    return flat.reshape(array.shape)


def shards(params, moment_one, moment_two, visible, counts, tile_pos, target):
    keys = slot_keys(visible)
    request = plan(visible)
    wanted = exchange(request)
    feats = project(params)
    centre = jnp.tile(tile_pos.reshape(2, 8), (1, 16))
    slots = find(request, keys, centre)
    colours = target.astype(F32).reshape(2, 8, 3, 256)
    colours = jnp.transpose(colours, (0, 2, 1, 3)).reshape(48, 256)
    arrived = exchange(serve(feats, wanted))
    grads, loss = render(arrived, slots, colours)
    received = exchange(grads)
    outs = update(received, wanted, params, moment_one, moment_two)
    return (loss[:, 0], *outs)


def solution(mesh):
    placed = (
        P(None, "dev"),
        P(None, "dev"),
        P(None, "dev"),
        P("dev", None),
        P("dev", None),
        P("dev"),
        P("dev", None, None),
    )
    return jax.shard_map(
        shards,
        mesh=mesh,
        in_specs=placed,
        out_specs=(P("dev"), P(None, "dev"), P(None, "dev"), P(None, "dev")),
        check_vma=False,
    )
```

```python
import jax
import jax.numpy as jnp
from jax import lax
from jax.experimental import pallas as pl
from jax.experimental.pallas import tpu as pltpu
from jax.sharding import PartitionSpec as P

N_DEV = 128
G_DEV = 4096
CAP = 64
TILES_X = 64
ADAM_STEP = 1000
SENTINEL = N_DEV * G_DEV
SCREEN_W = 1024.0
SCREEN_H = 512.0

SH_ZERO = 0.28209479177387814
SH_ONE = 0.4886025119029199
SH_TWO = (
    1.0925484305920792,
    -1.0925484305920792,
    0.31539156525252005,
    -1.0925484305920792,
    0.5462742152960396,
)
SH_THREE = (
    -0.5900435899266435,
    2.890611442640554,
    -0.4570457994644658,
    0.3731763325901154,
    -0.4570457994644658,
    1.445305721320277,
    -0.5900435899266435,
)
BETA_ONE = 0.9
BETA_TWO = 0.999
ADAM_EPS = 1e-15
LOG2_E = 1.4426950408889634

F32 = jnp.float32
BF16 = jnp.bfloat16
VMEM = pl.BlockSpec(memory_space=pltpu.VMEM)
HBM = pl.BlockSpec(memory_space=pltpu.HBM)
GU = 8
TABLE_ROWS = 27


def harmonics(dir_x, dir_y, dir_z):
    sq_x = dir_x * dir_x
    sq_y = dir_y * dir_y
    sq_z = dir_z * dir_z
    return [
        -SH_ONE * dir_y,
        SH_ONE * dir_z,
        -SH_ONE * dir_x,
        SH_TWO[0] * dir_x * dir_y,
        SH_TWO[1] * dir_y * dir_z,
        SH_TWO[2] * (2.0 * sq_z - sq_x - sq_y),
        SH_TWO[3] * dir_x * dir_z,
        SH_TWO[4] * (sq_x - sq_y),
        SH_THREE[0] * dir_y * (3.0 * sq_x - sq_y),
        SH_THREE[1] * dir_x * dir_y * dir_z,
        SH_THREE[2] * dir_y * (4.0 * sq_z - sq_x - sq_y),
        SH_THREE[3] * dir_z * (2.0 * sq_z - 3.0 * sq_x - 3.0 * sq_y),
        SH_THREE[4] * dir_x * (4.0 * sq_z - sq_x - sq_y),
        SH_THREE[5] * dir_z * (sq_x - sq_y),
        SH_THREE[6] * dir_x * (sq_x - 3.0 * sq_y),
    ]


def directions(mean_x, mean_y, depths):
    distance = jnp.sqrt(mean_x * mean_x + mean_y * mean_y + depths * depths)
    return harmonics(mean_x / distance, mean_y / distance, depths / distance)


def geometry(rows):
    mean_x, mean_y, depths = (rows[0], rows[1], rows[2])
    scale_x = jnp.exp(rows[3])
    scale_y = jnp.exp(rows[4])
    scale_z = jnp.exp(rows[5])
    quat_len = jnp.maximum(
        jnp.sqrt(rows[6] * rows[6] + rows[7] * rows[7] + rows[8] * rows[8] + rows[9] * rows[9]),
        0.5,
    )
    quat_w = rows[6] / quat_len
    quat_x = rows[7] / quat_len
    quat_y = rows[8] / quat_len
    quat_z = rows[9] / quat_len
    rot_xx = 1.0 - 2.0 * (quat_y * quat_y + quat_z * quat_z)
    rot_xy = 2.0 * (quat_x * quat_y - quat_w * quat_z)
    rot_xz = 2.0 * (quat_x * quat_z + quat_w * quat_y)
    rot_yx = 2.0 * (quat_x * quat_y + quat_w * quat_z)
    rot_yy = 1.0 - 2.0 * (quat_x * quat_x + quat_z * quat_z)
    rot_yz = 2.0 * (quat_y * quat_z - quat_w * quat_x)
    rot_zx = 2.0 * (quat_x * quat_z - quat_w * quat_y)
    rot_zy = 2.0 * (quat_y * quat_z + quat_w * quat_x)
    rot_zz = 1.0 - 2.0 * (quat_x * quat_x + quat_y * quat_y)
    m_xx, m_xy, m_xz = (rot_xx * scale_x, rot_xy * scale_y, rot_xz * scale_z)
    m_yx, m_yy, m_yz = (rot_yx * scale_x, rot_yy * scale_y, rot_yz * scale_z)
    m_zx, m_zy, m_zz = (rot_zx * scale_x, rot_zy * scale_y, rot_zz * scale_z)
    cov_xx = m_xx * m_xx + m_xy * m_xy + m_xz * m_xz
    cov_xy = m_xx * m_yx + m_xy * m_yy + m_xz * m_yz
    cov_xz = m_xx * m_zx + m_xy * m_zy + m_xz * m_zz
    cov_yy = m_yx * m_yx + m_yy * m_yy + m_yz * m_yz
    cov_yz = m_yx * m_zx + m_yy * m_zy + m_yz * m_zz
    cov_zz = m_zx * m_zx + m_zy * m_zy + m_zz * m_zz
    focal = 1.2 * SCREEN_W
    inverse = 1.0 / depths
    jac_xx = focal * inverse
    jac_xz = -focal * mean_x * inverse * inverse
    jac_yy = focal * inverse
    jac_yz = -focal * mean_y * inverse * inverse
    plane_a = (
        jac_xx * jac_xx * cov_xx + 2.0 * jac_xx * jac_xz * cov_xz + jac_xz * jac_xz * cov_zz + 0.3
    )
    plane_b = (
        jac_xx * jac_yy * cov_xy
        + jac_xx * jac_yz * cov_xz
        + jac_xz * jac_yy * cov_yz
        + jac_xz * jac_yz * cov_zz
    )
    plane_c = (
        jac_yy * jac_yy * cov_yy + 2.0 * jac_yy * jac_yz * cov_yz + jac_yz * jac_yz * cov_zz + 0.3
    )
    determ = plane_a * plane_c - plane_b * plane_b
    return (
        focal * mean_x * inverse + 0.5 * SCREEN_W,
        focal * mean_y * inverse + 0.5 * SCREEN_H,
        plane_c / determ,
        -plane_b / determ,
        plane_a / determ,
    )


def split(value):
    high = value.astype(BF16)
    return (high, (value - high.astype(F32)).astype(BF16))


def dot_nt(left, right):
    return lax.dot_general(left, right, (((1,), (1,)), ((), ())), preferred_element_type=F32)


def dot_nn(left, right):
    return jnp.dot(left, right, preferred_element_type=F32)


def one_hot(index_row, size):
    rows = lax.broadcasted_iota(jnp.int32, (size, index_row.shape[1]), 0)
    return jnp.where(rows == index_row, 1.0, 0.0).astype(BF16)


def iota(shape, axis):
    return lax.broadcasted_iota(jnp.int32, shape, axis)


def rows_first(ref, out_ref):
    for base in range(0, 59, 8):
        size = min(8, 59 - base)
        for piece in range(32):
            out_ref[pl.ds(base * 32 + piece, size, stride=32), :] = ref[
                base : base + size, piece * 128 : (piece + 1) * 128
            ]


def pair(ref, index):
    return jnp.concatenate(
        [ref[pl.ds(2 * index, 1), :], ref[pl.ds(2 * index + 1, 1), :]], axis=1
    )


def sort_all(parts):
    sublane = iota((8, 128), 0)
    lane = iota((8, 128), 1)

    def bit_of(bit, number):
        if bit < 3:
            return (number >> bit) & 1
        if bit < 6:
            return (sublane >> (bit - 3)) & 1
        return (lane >> (bit - 6)) & 1

    flipped = [0] * 8
    for level in range(1, 14):
        for number in range(8):
            turn = bit_of(level, number) if level < 13 else 0
            change = flipped[number] ^ turn
            if not isinstance(change, int):
                parts[number] = parts[number] ^ (0 - change)
            elif change:
                parts[number] = ~parts[number]
            flipped[number] = turn
        for bit in range(level - 1, -1, -1):
            if bit < 3:
                stride = 1 << bit
                for number in range(8):
                    if not number & stride:
                        one, two = parts[number], parts[number + stride]
                        parts[number] = jnp.minimum(one, two)
                        parts[number + stride] = jnp.maximum(one, two)
            else:
                axis, size = (0, 8) if bit < 6 else (1, 128)
                stride = 1 << (bit - 3 if bit < 6 else bit - 6)
                is_low = bit_of(bit, 0) == 0
                for number in range(8):
                    here = parts[number]
                    up = pltpu.roll(here, size - stride, axis)
                    down = pltpu.roll(here, stride, axis) if 2 * stride < size else up
                    parts[number] = jnp.where(
                        is_low, jnp.minimum(here, up), jnp.maximum(here, down)
                    )
    return parts


def plan_kernel(visible_ref, request_ref):
    lane = iota((8, 128), 1)
    sublane = iota((8, 128), 0)
    keys = []
    for rows in (slice(0, 8), slice(8, 16)):
        for block in range(4):
            ids = visible_ref[rows, block * 128 : (block + 1) * 128]
            keys.append(jnp.where(ids < 0, SENTINEL, ids))
    keys = sort_all(keys)

    def earlier(value, fill):
        shifted = pltpu.roll(value, 1, 0)
        shifted = jnp.where(sublane == 0, pltpu.roll(shifted, 1, 1), shifted)
        return jnp.where((sublane == 0) & (lane == 0), fill, shifted)

    before = [earlier(keys[7], -1)] + keys[0:7]
    fresh = [(keys[n] != before[n]) & (keys[n] < SENTINEL) for n in range(8)]
    opens = [(keys[n] >> 12) != (before[n] >> 12) for n in range(8)]
    counts = []
    for number in range(8):
        one = jnp.where(fresh[number], 1, 0)
        counts.append(one if number == 0 else counts[-1] + one)
    column = counts[7]
    for step in (1, 2, 4):
        column = column + jnp.where(sublane >= step, pltpu.roll(column, step, 0), 0)
    whole = jnp.broadcast_to(column[7:8], (8, 128)).astype(F32).astype(BF16)
    strictly = jnp.where(iota((128, 128), 0) < iota((128, 128), 1), 1.0, 0.0).astype(BF16)
    offset = dot_nn(whole, strictly).astype(jnp.int32) + column - counts[7] - 1
    counts = [count + offset for count in counts]
    bases = []
    for number in range(8):
        one = jnp.where(opens[number], counts[number], 0)
        bases.append(one if number == 0 else jnp.maximum(bases[-1], one))
    column = bases[7]
    for step in (1, 2, 4):
        column = jnp.maximum(column, jnp.where(sublane >= step, pltpu.roll(column, step, 0), 0))
    whole = jnp.broadcast_to(column[7:8], (8, 128))
    for step in (1, 2, 4, 8, 16, 32, 64):
        whole = jnp.maximum(whole, jnp.where(lane >= step, pltpu.roll(whole, step, 1), 0))
    whole = jnp.where(lane >= 1, pltpu.roll(whole, 1, 1), 0)
    above = jnp.maximum(whole, jnp.where(sublane >= 1, pltpu.roll(column, 1, 0), 0))
    filled = jnp.zeros((128, 128), F32)
    for half in range(4):
        lanes, marks = [], []
        for number in (2 * half, 2 * half + 1):
            rank = counts[number] - jnp.maximum(bases[number], above)
            rank = jnp.where(fresh[number], rank, -1)
            owner = keys[number] >> 12
            local = keys[number] & (G_DEV - 1)
            high, low = ((local >> 6).astype(F32), (local & 63).astype(F32))
            for row in range(8):
                cut = slice(row, row + 1)
                match = iota((64, 128), 0) == rank[cut]
                pieces = [
                    jnp.where(match, jnp.broadcast_to(part[cut], (64, 128)), 0.0)
                    for part in (high, low)
                ]
                marks.append(jnp.concatenate(pieces, axis=0).astype(BF16))
                lanes.append(one_hot(owner[cut], 128))
        filled = filled + dot_nt(jnp.concatenate(marks, axis=1), jnp.concatenate(lanes, axis=1))
    locals_of = (filled[0:64] * 64.0 + filled[64:128]).astype(jnp.int32)
    padded = jnp.concatenate([locals_of, jnp.zeros((64, 128), jnp.int32)], axis=0)
    request_ref[...] = jnp.transpose(padded)


def plan(visible):
    return pl.pallas_call(
        plan_kernel,
        out_shape=jax.ShapeDtypeStruct((128, 128), jnp.int32),
        in_specs=[VMEM],
        out_specs=VMEM,
        compiler_params=pltpu.CompilerParams(vmem_limit_bytes=32 * 1024 * 1024),
    )(visible)


def find_kernel(request_ref, keys_ref, centre_ref, slots_ref):
    table = jnp.transpose(request_ref[...])
    keys = keys_ref[...]
    owner = (keys >> 12) & 127
    local = keys & (G_DEV - 1)
    rank = jnp.zeros((64, 128), jnp.int32)
    for place in range(63, -1, -1):
        row = jnp.broadcast_to(table[place : place + 1], (64, 128))
        found = jnp.take_along_axis(row, owner, axis=1, mode="promise_in_bounds")
        rank = jnp.where(found == local, place, rank)
    tile = jnp.where(
        iota((64, 128), 0) < 32,
        jnp.broadcast_to(centre_ref[0:1, :], (64, 128)),
        jnp.broadcast_to(centre_ref[1:2, :], (64, 128)),
    )
    slots_ref[0:64, :] = (rank >> 5) * 128 + owner
    slots_ref[64:128, :] = rank & 31
    slots_ref[128:192, :] = jnp.where(keys < SENTINEL, tile, -1)


def find(request, keys, centre):
    return pl.pallas_call(
        find_kernel,
        out_shape=jax.ShapeDtypeStruct((192, 128), jnp.int32),
        in_specs=[VMEM] * 3,
        out_specs=VMEM,
        compiler_params=pltpu.CompilerParams(vmem_limit_bytes=32 * 1024 * 1024),
    )(request, keys, centre)


def gather_one(table_ref, high_ref, low_ref, out_ref, size, index):
    lanes = one_hot(pair(high_ref, index), 256)
    match = pair(low_ref, index) == iota((size, 256), 0)
    found = dot_nn(table_ref[...], lanes)
    for feature in range(9):
        parts = [
            found[part_row(part, feature) * size : (part_row(part, feature) + 1) * size]
            for part in range(parts_of(feature))
        ]
        total = parts[0] + parts[1]
        if len(parts) == 3:
            total = total + parts[2]
        picked = jnp.where(match, total, 0.0)
        line = jnp.sum(picked, axis=0, keepdims=True)
        out_ref[pl.ds(64 * feature + 2 * index, 1), :] = line[:, 0:128]
        out_ref[pl.ds(64 * feature + 2 * index + 1, 1), :] = line[:, 128:256]


def parts_of(feature):
    return 3


def part_row(part, feature):
    return part * 9 + feature


def put_parts(value, table_ref, feature, size):
    rest = value
    for part in range(parts_of(feature)):
        piece = rest.astype(BF16)
        base = part_row(part, feature) * size
        table_ref[base : base + size, :] = piece
        rest = rest - piece.astype(F32)


def project_kernel(params_ref, feats_ref, rows_s):
    rows_first(params_ref, rows_s)

    def row(index):
        return rows_s[index * 32 : (index + 1) * 32, :]

    rows = [row(index) for index in range(10)]
    feats = list(geometry(rows))
    feats.append(1.0 / (1.0 + jnp.exp(-row(10))))
    basis = directions(rows[0], rows[1], rows[2])
    for channel in range(3):
        total = 0.5 + SH_ZERO * row(11 + channel)
        for degree in range(1, 16):
            total = total + basis[degree - 1] * row(11 + 3 * degree + channel)
        feats.append(total)
    for index in range(9):
        rows = feats[index]
        put_parts(jnp.concatenate([rows[0:16], rows[16:32]], axis=1), feats_ref, index, 16)


def project(params):
    return pl.pallas_call(
        project_kernel,
        out_shape=jax.ShapeDtypeStruct((TABLE_ROWS * 16, 256), BF16),
        in_specs=[VMEM],
        out_specs=VMEM,
        scratch_shapes=[pltpu.VMEM((59 * 32, 128), F32)],
        compiler_params=pltpu.CompilerParams(vmem_limit_bytes=32 * 1024 * 1024),
    )(params)


def serve_kernel(table_ref, wanted_ref, out_ref, place_s, high_s, low_s):
    wanted = jnp.transpose(wanted_ref[...])[0:64]
    high_s[...] = (wanted >> 11) * 128 + (wanted & 127)
    low_s[...] = (wanted >> 7) & 15

    def step(index, carry):
        gather_one(table_ref, high_s, low_s, place_s, 16, index)
        return carry

    lax.fori_loop(0, 32, step, 0, unroll=GU)
    place_s[576:640, :] = jnp.zeros((64, 128), F32)
    for part in range(5):
        out_ref[pl.ds(part, 128, stride=5), :] = jnp.transpose(
            place_s[part * 128 : (part + 1) * 128, :]
        )


def serve(feats, wanted):
    return pl.pallas_call(
        serve_kernel,
        out_shape=jax.ShapeDtypeStruct((640, 128), F32),
        in_specs=[VMEM, VMEM],
        out_specs=VMEM,
        scratch_shapes=[
            pltpu.VMEM((640, 128), F32),
            pltpu.VMEM((64, 128), jnp.int32),
            pltpu.VMEM((64, 128), jnp.int32),
        ],
        compiler_params=pltpu.CompilerParams(vmem_limit_bytes=32 * 1024 * 1024),
    )(feats, wanted)


def pixel_basis():
    pixel = iota((24, 256), 1)
    across = (pixel & 15).astype(F32) - 7.5
    down = (pixel >> 4).astype(F32) - 7.5
    kind = iota((24, 256), 0)
    kind = jnp.where(kind >= 12, kind - 12, jnp.where(kind >= 6, kind - 6, kind))
    return select_monomial(kind, across, down)


def select_monomial(kind, across, down):
    value = jnp.where(kind == 0, across * across, 0.0)
    value = jnp.where(kind == 1, across * down, value)
    value = jnp.where(kind == 2, down * down, value)
    value = jnp.where(kind == 3, across, value)
    value = jnp.where(kind == 4, down, value)
    return jnp.where(kind == 5, 1.0, value).astype(BF16)


def render_kernel(
    arrived_hbm,
    slots_hbm,
    target_hbm,
    out_ref,
    loss_ref,
    places_s,
    table_s,
    coef_s,
    alpha_s,
    weight_s,
    sums_s,
    feats_s,
    weights_s,
    parts_s,
    slots_ref,
    target_ref,
    arrived_ref,
    sems,
):
    slots_copy = pltpu.make_async_copy(slots_hbm, slots_ref, sems.at[0])
    target_copy = pltpu.make_async_copy(target_hbm, target_ref, sems.at[1])
    arrived_copy = pltpu.make_async_copy(arrived_hbm, arrived_ref, sems.at[2])
    arrived_copy.start()
    slots_copy.start()
    target_copy.start()
    arrived_copy.wait()
    for part in range(5):
        table_s[part * 128 : (part + 1) * 128, :] = jnp.transpose(
            arrived_ref[pl.ds(part, 128, stride=5), :]
        )
    for feature in range(9):
        base = feature * 64
        put_parts(
            jnp.concatenate(
                [table_s[base : base + 32, :], table_s[base + 32 : base + 64, :]], axis=1
            ),
            places_s,
            feature,
            32,
        )
    slots_copy.wait()
    target_copy.wait()
    def gather(stage):
        for group in range(2):
            for step in range(4):
                gather_one(
                    places_s,
                    slots_ref.at[pl.ds(0, 64), :],
                    slots_ref.at[pl.ds(64, 64), :],
                    feats_s,
                    32,
                    group * 16 + stage * 4 + step,
                )

    def slot_values(first):
        feats = [feats_s[64 * f + first : 64 * f + first + 8, :] for f in range(9)]
        tile = slots_ref[128 + first : 136 + first, :]
        rel_u = feats[0] - ((tile & (TILES_X - 1)).astype(F32) * 16.0 + 7.5)
        rel_v = feats[1] - ((tile >> 6).astype(F32) * 16.0 + 7.5)
        return (feats, rel_u, rel_v, tile >= 0)

    def prepare(first):
        feats, rel_u, rel_v, live = slot_values(first)
        conic_1, conic_2, conic_3 = (feats[2], feats[3], feats[4])
        pull_u = conic_1 * rel_u + conic_2 * rel_v
        pull_v = conic_3 * rel_v + conic_2 * rel_u
        centre_e = (
            0.5 * (conic_1 * rel_u * rel_u + conic_3 * rel_v * rel_v) + conic_2 * rel_u * rel_v
        )
        level = jnp.log2(0.99 * feats[5])
        coefs = [
            -0.5 * LOG2_E * conic_1,
            -LOG2_E * conic_2,
            -0.5 * LOG2_E * conic_3,
            LOG2_E * pull_u,
            LOG2_E * pull_v,
            level - LOG2_E * centre_e,
        ]
        for index in range(6):
            value = jnp.where(live, coefs[index], -1024.0 if index == 5 else 0.0)
            high = value.astype(BF16).astype(F32)
            rest = value - high
            middle = rest.astype(BF16).astype(F32)
            coef_s[pl.ds(first * 24 + index, 8, stride=24), :] = high
            coef_s[pl.ds(first * 24 + index + 6, 8, stride=24), :] = middle
            coef_s[pl.ds(first * 24 + index + 12, 8, stride=24), :] = rest - middle
        for channel in range(3):
            value = feats[6 + channel]
            high = value.astype(BF16).astype(F32)
            coef_s[pl.ds(first * 24 + 18 + channel, 8, stride=24), :] = high
            coef_s[pl.ds(first * 24 + 21 + channel, 8, stride=24), :] = value - high

    def chunk_of(number, size):
        base = number * size
        return pl.ds(base if isinstance(base, int) else pl.multiple_of(base, 8), size)

    def chunk_rows(group, index):
        base = group * 4096 + index * 256
        return pl.ds(base if isinstance(base, int) else pl.multiple_of(base, 256), 256)

    def coef_of(group, index):
        base = group * 32 + index * 2
        return jnp.concatenate(
            [
                coef_s[chunk_of(base + half, 24), :]
                for half in range(2)
            ],
            axis=1,
        )

    basis = pixel_basis()
    pixel = iota((256, 128), 0)
    moments = select_monomial(
        iota((256, 128), 1), (pixel & 15).astype(F32) - 7.5, (pixel >> 4).astype(F32) - 7.5
    )

    diagonal = (iota((8, 256), 1) & 7) == iota((8, 256), 0)

    def spread(coef, base):
        return jnp.concatenate(
            [
                jnp.where(
                    diagonal,
                    jnp.broadcast_to(coef[base + channel : base + channel + 1], (8, 256)),
                    0.0,
                )
                for channel in range(3)
            ],
            axis=0,
        )

    def forward(index, state):
        results = []
        for group in range(2):
            left, colors = state[2 * group : 2 * group + 2]
            coef = coef_of(group, index)
            turned = jnp.transpose(coef)
            alpha = jnp.exp2(dot_nn(turned.astype(BF16), basis))
            tones = [
                turned[:, 18 + ch : 19 + ch] + turned[:, 21 + ch : 22 + ch] for ch in range(3)
            ]
            rows = chunk_rows(group, index)
            alpha_s[rows, :] = alpha
            parts = []
            sums = [colors[ch * 8 : (ch + 1) * 8] for ch in range(3)]
            for slot in range(32):
                cut = slice(slot * 8, (slot + 1) * 8)
                weight = alpha[cut] * left
                left = left - weight
                parts.append(weight)
                sums = [sums[ch] + weight * tones[ch][cut] for ch in range(3)]
            colors = jnp.concatenate(sums, axis=0)
            weights = jnp.concatenate(parts, axis=0)
            weight_s[rows, :] = weights
            high, low = split(weights)
            parts_s[rows, 512:768] = high
            parts_s[rows, 768:1024] = low
            results += [left, colors]
        return tuple(results)

    start = (jnp.ones((8, 256), F32), jnp.zeros((24, 256), F32))
    state = start + start
    gather(0)
    for stage in range(4):
        if stage < 3:
            gather(stage + 1)
        for group in range(2):
            prepare(group * 32 + stage * 8)
        for step in range(4):
            state = forward(4 * stage + step, state)
    err_all = []
    for group in range(2):
        errors = state[2 * group + 1] - target_ref[group * 24 : (group + 1) * 24, :]
        squares = errors * errors
        total = jnp.sum(squares[0:8] + squares[8:16] + squares[16:24], axis=1, keepdims=True)
        loss_ref[group * 8 : (group + 1) * 8, :] = jnp.broadcast_to(total / 16.0, (8, 128))
        err_high, err_low = split(errors * 0.125)
        err_all.append(jnp.concatenate([err_high, err_low, err_high], axis=0))
        turned = jnp.transpose(
            jnp.concatenate(
                [jnp.zeros((8, 256), F32), err_high.astype(F32), err_low.astype(F32)]
                + [jnp.zeros((72, 256), F32)],
                axis=0,
            )
        )
        lane = iota((256, 128), 1)
        weights_s[group, 0:256, :] = moments
        weights_s[group, 256:512, :] = moments
        weights_s[group, 512:768, :] = turned.astype(BF16)
        weights_s[group, 768:1024, :] = jnp.where(lane < 32, turned, 0.0).astype(BF16)

    def backward(step, state):
        index = 15 - step
        results = []
        for group in range(2):
            behind = state[group]
            err_three = err_all[group]
            coef = coef_of(group, index)
            col_high = spread(coef, 18)
            col_low = spread(coef, 21)
            col_three = jnp.concatenate([col_high, col_high, col_low], axis=0)
            shades = dot_nn(jnp.transpose(col_three).astype(BF16), err_three)
            rows = chunk_rows(group, index)
            alpha = alpha_s[rows, :]
            weights = weight_s[rows, :]
            parts = []
            for slot in range(31, -1, -1):
                cut = slice(slot * 8, (slot + 1) * 8)
                gap = shades[cut] - behind
                parts.append(weights[cut] * gap)
                behind = behind + alpha[cut] * gap
            pulls = jnp.concatenate(parts[::-1], axis=0)
            pull_high, pull_low = split(pulls)
            parts_s[rows, 0:256] = pull_high
            parts_s[rows, 256:512] = pull_low
            results.append(behind)
        return tuple(results)

    zero = jnp.zeros((8, 256), F32)
    def reduce_pixels(stage):
        for group in range(2):
            first = group * 4096 + (3 - stage) * 1024
            sums = dot_nn(parts_s[first : first + 1024, :], weights_s[group])
            for part in range(8):
                turned = jnp.transpose(sums[part * 128 : (part + 1) * 128])
                base = (first // 128 + part) * 16
                tints = turned[8:32] + turned[32:56]
                sums_s[base : base + 8, :] = turned[0:8]
                for channel in range(3):
                    own = jnp.where(
                        diagonal[:, 0:128], tints[channel * 8 : (channel + 1) * 8], 0.0
                    )
                    sums_s[base + 8 + channel : base + 9 + channel, :] = jnp.sum(
                        own, axis=0, keepdims=True
                    )

    def scatter(stage, total):
        steps = []
        for group in range(2):
            first = group * 32 + (3 - stage) * 8
            feats, rel_u, rel_v, live = slot_values(first)
            conic_1, conic_2, conic_3 = (feats[2], feats[3], feats[4])

            def sums_of(index):
                return sums_s[pl.ds(first * 16 + index, 8, stride=16), :]

            m_xx, m_xy, m_yy, m_x, m_y, m_0 = [sums_of(index) for index in range(6)]
            s_x = m_x - rel_u * m_0
            s_y = m_y - rel_v * m_0
            s_xx = m_xx - 2.0 * rel_u * m_x + rel_u * rel_u * m_0
            s_yy = m_yy - 2.0 * rel_v * m_y + rel_v * rel_v * m_0
            s_xy = m_xy - rel_u * m_y - rel_v * m_x + rel_u * rel_v * m_0
            slot_grads = [
                conic_1 * s_x + conic_2 * s_y,
                conic_3 * s_y + conic_2 * s_x,
                -0.5 * s_xx,
                -s_xy,
                -0.5 * s_yy,
                m_0,
                sums_of(8),
                sums_of(9),
                sums_of(10),
            ]
            slot_grads = [jnp.where(live, grad, 0.0) for grad in slot_grads]
            steps.append(
                (
                    slot_grads,
                    slots_ref[first : first + 8, :],
                    slots_ref[64 + first : 72 + first, :],
                )
            )
        return total + scatter_rows(steps, 32)

    state = (zero, zero)
    collected = jnp.zeros((288, 256), F32)
    for stage in range(6):
        if stage >= 2:
            collected = scatter(stage - 2, collected)
        if 1 <= stage < 5:
            reduce_pixels(stage - 1)
        if stage < 4:
            for step in range(4):
                state = backward(4 * stage + step, state)
    for feature in range(9):
        piece = collected[feature * 32 : (feature + 1) * 32]
        table_s[feature * 64 : feature * 64 + 32, :] = piece[:, 0:128]
        table_s[feature * 64 + 32 : feature * 64 + 64, :] = piece[:, 128:256]
    table_s[576:640, :] = jnp.zeros((64, 128), F32)
    for part in range(5):
        out_ref[pl.ds(part, 128, stride=5), :] = jnp.transpose(
            table_s[part * 128 : (part + 1) * 128, :]
        )


def scatter_rows(steps, size):
    lanes, masked_high, masked_low = [], [], []
    for values, high, low in steps:
        tops = [value.astype(BF16).astype(F32) for value in values]
        rests = [value - top for value, top in zip(values, tops)]
        for row in range(8):
            cut = slice(row, row + 1)
            lanes.append(one_hot(high[cut], 256))
            match = low[cut] == iota((size, 128), 0)
            for parts, found in ((tops, masked_high), (rests, masked_low)):
                found.append(
                    jnp.concatenate(
                        [
                            jnp.where(match, jnp.broadcast_to(part[cut], (size, 128)), 0.0)
                            for part in parts
                        ],
                        axis=0,
                    ).astype(BF16)
                )
    masked = jnp.concatenate(
        [jnp.concatenate(masked_high, axis=1), jnp.concatenate(masked_low, axis=1)], axis=0
    )
    found = dot_nt(masked, jnp.concatenate(lanes, axis=1))
    return found[0 : 9 * size] + found[9 * size : 18 * size]


def render(arrived, slots, target):
    return pl.pallas_call(
        render_kernel,
        out_shape=(
            jax.ShapeDtypeStruct((640, 128), F32),
            jax.ShapeDtypeStruct((16, 128), F32),
        ),
        in_specs=[HBM, HBM, HBM],
        out_specs=(VMEM, VMEM),
        scratch_shapes=[
            pltpu.VMEM((TABLE_ROWS * 32, 256), BF16),
            pltpu.VMEM((640, 128), F32),
            pltpu.VMEM((64 * 24, 128), F32),
            pltpu.VMEM((8192, 256), F32),
            pltpu.VMEM((8192, 256), F32),
            pltpu.VMEM((64 * 16, 128), F32),
            pltpu.VMEM((576, 128), F32),
            pltpu.VMEM((2, 1024, 128), BF16),
            pltpu.VMEM((8192, 1024), BF16),
            pltpu.VMEM((192, 128), jnp.int32),
            pltpu.VMEM((48, 256), F32),
            pltpu.VMEM((640, 128), F32),
            pltpu.SemaphoreType.DMA((3,)),
        ],
        compiler_params=pltpu.CompilerParams(vmem_limit_bytes=62 * 1024 * 1024),
    )(arrived, slots, target)


def learn_rate(index):
    if index < 3:
        return 0.0016
    if index < 6:
        return 0.005
    if index < 10:
        return 0.001
    if index < 11:
        return 0.05
    return 0.0025 if index < 14 else 0.000125


def update_kernel(
    received_ref,
    wanted_ref,
    params_ref,
    one_ref,
    two_ref,
    new_params_ref,
    new_one_ref,
    new_two_ref,
    rows_s,
    grads_s,
    table_s,
):
    wanted = jnp.transpose(wanted_ref[...])[0:64]
    piece = wanted >> 7
    for part in range(5):
        turned = jnp.transpose(received_ref[pl.ds(part, 128, stride=5), :])
        table_s[part * 128 : (part + 1) * 128, :] = turned
    high = (piece >> 4) * 128 + (wanted & 127)
    low = piece & 15
    collected = jnp.zeros((144, 256), F32)
    for group in range(4):
        steps = []
        for first in (group * 16, group * 16 + 8):
            rows = slice(first, first + 8)
            values = [table_s[f * 64 + first : f * 64 + first + 8, :] for f in range(9)]
            steps.append((values, high[rows], low[rows]))
        collected = collected + scatter_rows(steps, 16)

    def grad_of(feature):
        part = collected[feature * 16 : (feature + 1) * 16]
        return jnp.concatenate([part[:, 0:128], part[:, 128:256]], axis=0)

    rows_first(params_ref, rows_s)

    def row(index):
        return rows_s[index * 32 : (index + 1) * 32, :]

    def put(index, value):
        grads_s[index * 32 : (index + 1) * 32, :] = value

    rows = [row(index) for index in range(10)]
    unused, pull_geometry = jax.vjp(geometry, rows)
    (geo_grads,) = pull_geometry(tuple(grad_of(feature) for feature in range(5)))
    put(10, grad_of(5) * (1.0 / (1.0 + jnp.exp(row(10)))))
    basis, pull_basis = jax.vjp(directions, rows[0], rows[1], rows[2])
    tints = [grad_of(6 + channel) for channel in range(3)]
    basis_grads = []
    for channel in range(3):
        put(11 + channel, SH_ZERO * tints[channel])
    for degree in range(1, 16):
        total = None
        for channel in range(3):
            index = 11 + 3 * degree + channel
            put(index, basis[degree - 1] * tints[channel])
            term = row(index) * tints[channel]
            total = term if total is None else total + term
        basis_grads.append(total)
    mean_grads = pull_basis(basis_grads)
    for index in range(10):
        put(index, geo_grads[index] + mean_grads[index] if index < 3 else geo_grads[index])

    fix_one = 1.0 / (1.0 - BETA_ONE**ADAM_STEP)
    fix_two = 1.0 / (1.0 - BETA_TWO**ADAM_STEP)
    for base in range(0, 59, 8):
        size = min(8, 59 - base)
        rate = jnp.zeros((size, 128), F32)
        for index in range(size):
            rate = jnp.where(iota((size, 128), 0) == index, learn_rate(base + index), rate)
        for piece in range(32):
            cut = (slice(base, base + size), slice(piece * 128, (piece + 1) * 128))
            grad = grads_s[pl.ds(base * 32 + piece, size, stride=32), :]
            one = BETA_ONE * one_ref[cut] + (1.0 - BETA_ONE) * grad
            two = BETA_TWO * two_ref[cut] + (1.0 - BETA_TWO) * grad * grad
            new_one_ref[cut] = one
            new_two_ref[cut] = two
            step = one * fix_one / (jnp.sqrt(two * fix_two) + ADAM_EPS)
            new_params_ref[cut] = params_ref[cut] - rate * step


def update(received, wanted, params, moment_one, moment_two):
    whole = jax.ShapeDtypeStruct((59, G_DEV), F32)
    return pl.pallas_call(
        update_kernel,
        out_shape=(whole, whole, whole),
        in_specs=[VMEM] * 5,
        out_specs=(VMEM, VMEM, VMEM),
        scratch_shapes=[
            pltpu.VMEM((59 * 32, 128), F32),
            pltpu.VMEM((59 * 32, 128), F32),
            pltpu.VMEM((640, 128), F32),
        ],
        compiler_params=pltpu.CompilerParams(vmem_limit_bytes=48 * 1024 * 1024),
    )(received, wanted, params, moment_one, moment_two)


def slot_keys(visible):
    keys = jnp.where(visible < 0, SENTINEL, visible)
    return jnp.transpose(keys.reshape(2, 8, 512), (0, 2, 1)).reshape(64, 128)


def exchange(array):
    flat = array.reshape(N_DEV, 1, -1)
    flat = lax.all_to_all(flat, "dev", split_axis=0, concat_axis=0, tiled=True)
    return flat.reshape(array.shape)


def shards(params, moment_one, moment_two, visible, counts, tile_pos, target):
    keys = slot_keys(visible)
    request = plan(visible)
    wanted = exchange(request)
    feats = project(params)
    centre = jnp.tile(tile_pos.reshape(2, 8), (1, 16))
    slots = find(request, keys, centre)
    colours = target.astype(F32).reshape(2, 8, 3, 256)
    colours = jnp.transpose(colours, (0, 2, 1, 3)).reshape(48, 256)
    arrived = exchange(serve(feats, wanted))
    grads, loss = render(arrived, slots, colours)
    received = exchange(grads)
    outs = update(received, wanted, params, moment_one, moment_two)
    return (loss[:, 0], *outs)


def solution(mesh):
    placed = (
        P(None, "dev"),
        P(None, "dev"),
        P(None, "dev"),
        P("dev", None),
        P("dev", None),
        P("dev"),
        P("dev", None, None),
    )
    return jax.shard_map(
        shards,
        mesh=mesh,
        in_specs=placed,
        out_specs=(P("dev"), P(None, "dev"), P(None, "dev"), P(None, "dev")),
        check_vma=False,
    )
```

```python
import jax
import jax.numpy as jnp
from jax import lax
from jax.experimental import pallas as pl
from jax.experimental.pallas import tpu as pltpu
from jax.sharding import PartitionSpec as P

N_DEV = 128
G_DEV = 4096
CAP = 64
TILES_X = 64
ADAM_STEP = 1000
SENTINEL = N_DEV * G_DEV
SCREEN_W = 1024.0
SCREEN_H = 512.0

SH_ZERO = 0.28209479177387814
SH_ONE = 0.4886025119029199
SH_TWO = (
    1.0925484305920792,
    -1.0925484305920792,
    0.31539156525252005,
    -1.0925484305920792,
    0.5462742152960396,
)
SH_THREE = (
    -0.5900435899266435,
    2.890611442640554,
    -0.4570457994644658,
    0.3731763325901154,
    -0.4570457994644658,
    1.445305721320277,
    -0.5900435899266435,
)
BETA_ONE = 0.9
BETA_TWO = 0.999
ADAM_EPS = 1e-15
LOG2_E = 1.4426950408889634

F32 = jnp.float32
BF16 = jnp.bfloat16
VMEM = pl.BlockSpec(memory_space=pltpu.VMEM)
HBM = pl.BlockSpec(memory_space=pltpu.HBM)
GU = 8
TABLE_ROWS = 27


def harmonics(dir_x, dir_y, dir_z):
    sq_x = dir_x * dir_x
    sq_y = dir_y * dir_y
    sq_z = dir_z * dir_z
    return [
        -SH_ONE * dir_y,
        SH_ONE * dir_z,
        -SH_ONE * dir_x,
        SH_TWO[0] * dir_x * dir_y,
        SH_TWO[1] * dir_y * dir_z,
        SH_TWO[2] * (2.0 * sq_z - sq_x - sq_y),
        SH_TWO[3] * dir_x * dir_z,
        SH_TWO[4] * (sq_x - sq_y),
        SH_THREE[0] * dir_y * (3.0 * sq_x - sq_y),
        SH_THREE[1] * dir_x * dir_y * dir_z,
        SH_THREE[2] * dir_y * (4.0 * sq_z - sq_x - sq_y),
        SH_THREE[3] * dir_z * (2.0 * sq_z - 3.0 * sq_x - 3.0 * sq_y),
        SH_THREE[4] * dir_x * (4.0 * sq_z - sq_x - sq_y),
        SH_THREE[5] * dir_z * (sq_x - sq_y),
        SH_THREE[6] * dir_x * (sq_x - 3.0 * sq_y),
    ]


def directions(mean_x, mean_y, depths):
    distance = jnp.sqrt(mean_x * mean_x + mean_y * mean_y + depths * depths)
    return harmonics(mean_x / distance, mean_y / distance, depths / distance)


def geometry(rows):
    mean_x, mean_y, depths = (rows[0], rows[1], rows[2])
    scale_x = jnp.exp(rows[3])
    scale_y = jnp.exp(rows[4])
    scale_z = jnp.exp(rows[5])
    quat_len = jnp.maximum(
        jnp.sqrt(rows[6] * rows[6] + rows[7] * rows[7] + rows[8] * rows[8] + rows[9] * rows[9]),
        0.5,
    )
    quat_w = rows[6] / quat_len
    quat_x = rows[7] / quat_len
    quat_y = rows[8] / quat_len
    quat_z = rows[9] / quat_len
    rot_xx = 1.0 - 2.0 * (quat_y * quat_y + quat_z * quat_z)
    rot_xy = 2.0 * (quat_x * quat_y - quat_w * quat_z)
    rot_xz = 2.0 * (quat_x * quat_z + quat_w * quat_y)
    rot_yx = 2.0 * (quat_x * quat_y + quat_w * quat_z)
    rot_yy = 1.0 - 2.0 * (quat_x * quat_x + quat_z * quat_z)
    rot_yz = 2.0 * (quat_y * quat_z - quat_w * quat_x)
    rot_zx = 2.0 * (quat_x * quat_z - quat_w * quat_y)
    rot_zy = 2.0 * (quat_y * quat_z + quat_w * quat_x)
    rot_zz = 1.0 - 2.0 * (quat_x * quat_x + quat_y * quat_y)
    m_xx, m_xy, m_xz = (rot_xx * scale_x, rot_xy * scale_y, rot_xz * scale_z)
    m_yx, m_yy, m_yz = (rot_yx * scale_x, rot_yy * scale_y, rot_yz * scale_z)
    m_zx, m_zy, m_zz = (rot_zx * scale_x, rot_zy * scale_y, rot_zz * scale_z)
    cov_xx = m_xx * m_xx + m_xy * m_xy + m_xz * m_xz
    cov_xy = m_xx * m_yx + m_xy * m_yy + m_xz * m_yz
    cov_xz = m_xx * m_zx + m_xy * m_zy + m_xz * m_zz
    cov_yy = m_yx * m_yx + m_yy * m_yy + m_yz * m_yz
    cov_yz = m_yx * m_zx + m_yy * m_zy + m_yz * m_zz
    cov_zz = m_zx * m_zx + m_zy * m_zy + m_zz * m_zz
    focal = 1.2 * SCREEN_W
    inverse = 1.0 / depths
    jac_xx = focal * inverse
    jac_xz = -focal * mean_x * inverse * inverse
    jac_yy = focal * inverse
    jac_yz = -focal * mean_y * inverse * inverse
    plane_a = (
        jac_xx * jac_xx * cov_xx + 2.0 * jac_xx * jac_xz * cov_xz + jac_xz * jac_xz * cov_zz + 0.3
    )
    plane_b = (
        jac_xx * jac_yy * cov_xy
        + jac_xx * jac_yz * cov_xz
        + jac_xz * jac_yy * cov_yz
        + jac_xz * jac_yz * cov_zz
    )
    plane_c = (
        jac_yy * jac_yy * cov_yy + 2.0 * jac_yy * jac_yz * cov_yz + jac_yz * jac_yz * cov_zz + 0.3
    )
    determ = plane_a * plane_c - plane_b * plane_b
    return (
        focal * mean_x * inverse + 0.5 * SCREEN_W,
        focal * mean_y * inverse + 0.5 * SCREEN_H,
        plane_c / determ,
        -plane_b / determ,
        plane_a / determ,
    )


def split(value):
    high = value.astype(BF16)
    return (high, (value - high.astype(F32)).astype(BF16))


def dot_nt(left, right):
    return lax.dot_general(left, right, (((1,), (1,)), ((), ())), preferred_element_type=F32)


def dot_nn(left, right):
    return jnp.dot(left, right, preferred_element_type=F32)


def one_hot(index_row, size):
    rows = lax.broadcasted_iota(jnp.int32, (size, index_row.shape[1]), 0)
    return jnp.where(rows == index_row, 1.0, 0.0).astype(BF16)


def iota(shape, axis):
    return lax.broadcasted_iota(jnp.int32, shape, axis)


def rows_first(ref, out_ref):
    for base in range(0, 59, 8):
        size = min(8, 59 - base)
        for piece in range(32):
            out_ref[pl.ds(base * 32 + piece, size, stride=32), :] = ref[
                base : base + size, piece * 128 : (piece + 1) * 128
            ]


def pair(ref, index):
    return jnp.concatenate(
        [ref[pl.ds(2 * index, 1), :], ref[pl.ds(2 * index + 1, 1), :]], axis=1
    )


def sort_all(parts):
    sublane = iota((8, 128), 0)
    lane = iota((8, 128), 1)

    def bit_of(bit, number):
        if bit < 3:
            return (number >> bit) & 1
        if bit < 6:
            return (sublane >> (bit - 3)) & 1
        return (lane >> (bit - 6)) & 1

    flipped = [0] * 8
    for level in range(1, 14):
        for number in range(8):
            turn = bit_of(level, number) if level < 13 else 0
            change = flipped[number] ^ turn
            if not isinstance(change, int):
                parts[number] = parts[number] ^ (0 - change)
            elif change:
                parts[number] = ~parts[number]
            flipped[number] = turn
        for bit in range(level - 1, -1, -1):
            if bit < 3:
                stride = 1 << bit
                for number in range(8):
                    if not number & stride:
                        one, two = parts[number], parts[number + stride]
                        parts[number] = jnp.minimum(one, two)
                        parts[number + stride] = jnp.maximum(one, two)
            else:
                axis, size = (0, 8) if bit < 6 else (1, 128)
                stride = 1 << (bit - 3 if bit < 6 else bit - 6)
                is_low = bit_of(bit, 0) == 0
                for number in range(8):
                    here = parts[number]
                    up = pltpu.roll(here, size - stride, axis)
                    down = pltpu.roll(here, stride, axis) if 2 * stride < size else up
                    parts[number] = jnp.where(
                        is_low, jnp.minimum(here, up), jnp.maximum(here, down)
                    )
    return parts


def plan_kernel(visible_ref, request_ref):
    lane = iota((8, 128), 1)
    sublane = iota((8, 128), 0)
    keys = []
    for rows in (slice(0, 8), slice(8, 16)):
        for block in range(4):
            ids = visible_ref[rows, block * 128 : (block + 1) * 128]
            keys.append(jnp.where(ids < 0, SENTINEL, ids))
    keys = sort_all(keys)

    def earlier(value, fill):
        shifted = pltpu.roll(value, 1, 0)
        shifted = jnp.where(sublane == 0, pltpu.roll(shifted, 1, 1), shifted)
        return jnp.where((sublane == 0) & (lane == 0), fill, shifted)

    before = [earlier(keys[7], -1)] + keys[0:7]
    fresh = [(keys[n] != before[n]) & (keys[n] < SENTINEL) for n in range(8)]
    opens = [(keys[n] >> 12) != (before[n] >> 12) for n in range(8)]
    counts = []
    for number in range(8):
        one = jnp.where(fresh[number], 1, 0)
        counts.append(one if number == 0 else counts[-1] + one)
    column = counts[7]
    for step in (1, 2, 4):
        column = column + jnp.where(sublane >= step, pltpu.roll(column, step, 0), 0)
    whole = jnp.broadcast_to(column[7:8], (8, 128)).astype(F32).astype(BF16)
    strictly = jnp.where(iota((128, 128), 0) < iota((128, 128), 1), 1.0, 0.0).astype(BF16)
    offset = dot_nn(whole, strictly).astype(jnp.int32) + column - counts[7] - 1
    counts = [count + offset for count in counts]
    bases = []
    for number in range(8):
        one = jnp.where(opens[number], counts[number], 0)
        bases.append(one if number == 0 else jnp.maximum(bases[-1], one))
    column = bases[7]
    for step in (1, 2, 4):
        column = jnp.maximum(column, jnp.where(sublane >= step, pltpu.roll(column, step, 0), 0))
    whole = jnp.broadcast_to(column[7:8], (8, 128))
    for step in (1, 2, 4, 8, 16, 32, 64):
        whole = jnp.maximum(whole, jnp.where(lane >= step, pltpu.roll(whole, step, 1), 0))
    whole = jnp.where(lane >= 1, pltpu.roll(whole, 1, 1), 0)
    above = jnp.maximum(whole, jnp.where(sublane >= 1, pltpu.roll(column, 1, 0), 0))
    filled = jnp.zeros((128, 128), F32)
    for half in range(4):
        lanes, marks = [], []
        for number in (2 * half, 2 * half + 1):
            rank = counts[number] - jnp.maximum(bases[number], above)
            rank = jnp.where(fresh[number], rank, -1)
            owner = keys[number] >> 12
            local = keys[number] & (G_DEV - 1)
            high, low = ((local >> 6).astype(F32), (local & 63).astype(F32))
            for row in range(8):
                cut = slice(row, row + 1)
                match = iota((64, 128), 0) == rank[cut]
                pieces = [
                    jnp.where(match, jnp.broadcast_to(part[cut], (64, 128)), 0.0)
                    for part in (high, low)
                ]
                marks.append(jnp.concatenate(pieces, axis=0).astype(BF16))
                lanes.append(one_hot(owner[cut], 128))
        filled = filled + dot_nt(jnp.concatenate(marks, axis=1), jnp.concatenate(lanes, axis=1))
    locals_of = (filled[0:64] * 64.0 + filled[64:128]).astype(jnp.int32)
    padded = jnp.concatenate([locals_of, jnp.zeros((64, 128), jnp.int32)], axis=0)
    request_ref[...] = jnp.transpose(padded)


def plan(visible):
    return pl.pallas_call(
        plan_kernel,
        out_shape=jax.ShapeDtypeStruct((128, 128), jnp.int32),
        in_specs=[VMEM],
        out_specs=VMEM,
        compiler_params=pltpu.CompilerParams(vmem_limit_bytes=32 * 1024 * 1024),
    )(visible)


def find_kernel(request_ref, keys_ref, centre_ref, slots_ref):
    table = jnp.transpose(request_ref[...])
    keys = keys_ref[...]
    owner = (keys >> 12) & 127
    local = keys & (G_DEV - 1)
    rank = jnp.zeros((64, 128), jnp.int32)
    for place in range(63, -1, -1):
        row = jnp.broadcast_to(table[place : place + 1], (64, 128))
        found = jnp.take_along_axis(row, owner, axis=1, mode="promise_in_bounds")
        rank = jnp.where(found == local, place, rank)
    tile = jnp.where(
        iota((64, 128), 0) < 32,
        jnp.broadcast_to(centre_ref[0:1, :], (64, 128)),
        jnp.broadcast_to(centre_ref[1:2, :], (64, 128)),
    )
    slots_ref[0:64, :] = (rank >> 5) * 128 + owner
    slots_ref[64:128, :] = rank & 31
    slots_ref[128:192, :] = jnp.where(keys < SENTINEL, tile, -1)


def find(request, keys, centre):
    return pl.pallas_call(
        find_kernel,
        out_shape=jax.ShapeDtypeStruct((192, 128), jnp.int32),
        in_specs=[VMEM] * 3,
        out_specs=VMEM,
        compiler_params=pltpu.CompilerParams(vmem_limit_bytes=32 * 1024 * 1024),
    )(request, keys, centre)


def gather_one(table_ref, high_ref, low_ref, out_ref, size, index):
    lanes = one_hot(pair(high_ref, index), 256)
    match = pair(low_ref, index) == iota((size, 256), 0)
    found = dot_nn(table_ref[...], lanes)
    for feature in range(9):
        parts = [
            found[part_row(part, feature) * size : (part_row(part, feature) + 1) * size]
            for part in range(parts_of(feature))
        ]
        total = parts[0] + parts[1]
        if len(parts) == 3:
            total = total + parts[2]
        picked = jnp.where(match, total, 0.0)
        line = jnp.sum(picked, axis=0, keepdims=True)
        out_ref[pl.ds(64 * feature + 2 * index, 1), :] = line[:, 0:128]
        out_ref[pl.ds(64 * feature + 2 * index + 1, 1), :] = line[:, 128:256]


def parts_of(feature):
    return 3


def part_row(part, feature):
    return part * 9 + feature


def put_parts(value, table_ref, feature, size):
    rest = value
    for part in range(parts_of(feature)):
        piece = rest.astype(BF16)
        base = part_row(part, feature) * size
        table_ref[base : base + size, :] = piece
        rest = rest - piece.astype(F32)


def project_kernel(params_ref, feats_ref, rows_s):
    rows_first(params_ref, rows_s)

    def row(index):
        return rows_s[index * 32 : (index + 1) * 32, :]

    rows = [row(index) for index in range(10)]
    feats = list(geometry(rows))
    feats.append(1.0 / (1.0 + jnp.exp(-row(10))))
    basis = directions(rows[0], rows[1], rows[2])
    for channel in range(3):
        total = 0.5 + SH_ZERO * row(11 + channel)
        for degree in range(1, 16):
            total = total + basis[degree - 1] * row(11 + 3 * degree + channel)
        feats.append(total)
    for index in range(9):
        rows = feats[index]
        put_parts(jnp.concatenate([rows[0:16], rows[16:32]], axis=1), feats_ref, index, 16)


def project(params):
    return pl.pallas_call(
        project_kernel,
        out_shape=jax.ShapeDtypeStruct((TABLE_ROWS * 16, 256), BF16),
        in_specs=[VMEM],
        out_specs=VMEM,
        scratch_shapes=[pltpu.VMEM((59 * 32, 128), F32)],
        compiler_params=pltpu.CompilerParams(vmem_limit_bytes=32 * 1024 * 1024),
    )(params)


def serve_kernel(table_ref, wanted_ref, out_ref, place_s, high_s, low_s):
    wanted = jnp.transpose(wanted_ref[...])[0:64]
    high_s[...] = (wanted >> 11) * 128 + (wanted & 127)
    low_s[...] = (wanted >> 7) & 15

    def step(index, carry):
        gather_one(table_ref, high_s, low_s, place_s, 16, index)
        return carry

    lax.fori_loop(0, 32, step, 0, unroll=GU)
    place_s[576:640, :] = jnp.zeros((64, 128), F32)
    for part in range(5):
        out_ref[pl.ds(part, 128, stride=5), :] = jnp.transpose(
            place_s[part * 128 : (part + 1) * 128, :]
        )


def serve(feats, wanted):
    return pl.pallas_call(
        serve_kernel,
        out_shape=jax.ShapeDtypeStruct((640, 128), F32),
        in_specs=[VMEM, VMEM],
        out_specs=VMEM,
        scratch_shapes=[
            pltpu.VMEM((640, 128), F32),
            pltpu.VMEM((64, 128), jnp.int32),
            pltpu.VMEM((64, 128), jnp.int32),
        ],
        compiler_params=pltpu.CompilerParams(vmem_limit_bytes=32 * 1024 * 1024),
    )(feats, wanted)


def pixel_basis():
    pixel = iota((24, 256), 1)
    across = (pixel & 15).astype(F32) - 7.5
    down = (pixel >> 4).astype(F32) - 7.5
    kind = iota((24, 256), 0)
    kind = jnp.where(kind >= 12, kind - 12, jnp.where(kind >= 6, kind - 6, kind))
    return select_monomial(kind, across, down)


def select_monomial(kind, across, down):
    value = jnp.where(kind == 0, across * across, 0.0)
    value = jnp.where(kind == 1, across * down, value)
    value = jnp.where(kind == 2, down * down, value)
    value = jnp.where(kind == 3, across, value)
    value = jnp.where(kind == 4, down, value)
    return jnp.where(kind == 5, 1.0, value).astype(BF16)


def render_kernel(
    arrived_hbm,
    slots_hbm,
    target_hbm,
    out_ref,
    loss_ref,
    places_s,
    table_s,
    coef_s,
    alpha_s,
    weight_s,
    sums_s,
    feats_s,
    weights_s,
    parts_s,
    slots_ref,
    target_ref,
    arrived_ref,
    sems,
):
    slots_copy = pltpu.make_async_copy(slots_hbm, slots_ref, sems.at[0])
    target_copy = pltpu.make_async_copy(target_hbm, target_ref, sems.at[1])
    arrived_copy = pltpu.make_async_copy(arrived_hbm, arrived_ref, sems.at[2])
    arrived_copy.start()
    slots_copy.start()
    target_copy.start()
    arrived_copy.wait()
    for part in range(5):
        table_s[part * 128 : (part + 1) * 128, :] = jnp.transpose(
            arrived_ref[pl.ds(part, 128, stride=5), :]
        )
    for feature in range(9):
        base = feature * 64
        put_parts(
            jnp.concatenate(
                [table_s[base : base + 32, :], table_s[base + 32 : base + 64, :]], axis=1
            ),
            places_s,
            feature,
            32,
        )
    slots_copy.wait()
    target_copy.wait()
    def gather(stage):
        for group in range(2):
            for step in range(4):
                gather_one(
                    places_s,
                    slots_ref.at[pl.ds(0, 64), :],
                    slots_ref.at[pl.ds(64, 64), :],
                    feats_s,
                    32,
                    group * 16 + stage * 4 + step,
                )

    def slot_values(first):
        feats = [feats_s[64 * f + first : 64 * f + first + 8, :] for f in range(9)]
        tile = slots_ref[128 + first : 136 + first, :]
        rel_u = feats[0] - ((tile & (TILES_X - 1)).astype(F32) * 16.0 + 7.5)
        rel_v = feats[1] - ((tile >> 6).astype(F32) * 16.0 + 7.5)
        return (feats, rel_u, rel_v, tile >= 0)

    def prepare(first):
        feats, rel_u, rel_v, live = slot_values(first)
        conic_1, conic_2, conic_3 = (feats[2], feats[3], feats[4])
        pull_u = conic_1 * rel_u + conic_2 * rel_v
        pull_v = conic_3 * rel_v + conic_2 * rel_u
        centre_e = (
            0.5 * (conic_1 * rel_u * rel_u + conic_3 * rel_v * rel_v) + conic_2 * rel_u * rel_v
        )
        level = jnp.log2(0.99 * feats[5])
        coefs = [
            -0.5 * LOG2_E * conic_1,
            -LOG2_E * conic_2,
            -0.5 * LOG2_E * conic_3,
            LOG2_E * pull_u,
            LOG2_E * pull_v,
            level - LOG2_E * centre_e,
        ]
        for index in range(6):
            value = jnp.where(live, coefs[index], -1024.0 if index == 5 else 0.0)
            high = value.astype(BF16).astype(F32)
            rest = value - high
            middle = rest.astype(BF16).astype(F32)
            coef_s[pl.ds(first * 24 + index, 8, stride=24), :] = high
            coef_s[pl.ds(first * 24 + index + 6, 8, stride=24), :] = middle
            coef_s[pl.ds(first * 24 + index + 12, 8, stride=24), :] = rest - middle
        for channel in range(3):
            value = feats[6 + channel]
            high = value.astype(BF16).astype(F32)
            coef_s[pl.ds(first * 24 + 18 + channel, 8, stride=24), :] = high
            coef_s[pl.ds(first * 24 + 21 + channel, 8, stride=24), :] = value - high

    def chunk_of(number, size):
        base = number * size
        return pl.ds(base if isinstance(base, int) else pl.multiple_of(base, 8), size)

    def chunk_rows(group, index):
        base = group * 4096 + index * 256
        return pl.ds(base if isinstance(base, int) else pl.multiple_of(base, 256), 256)

    def coef_of(group, index):
        base = group * 32 + index * 2
        return jnp.concatenate(
            [
                coef_s[chunk_of(base + half, 24), :]
                for half in range(2)
            ],
            axis=1,
        )

    basis = pixel_basis()
    pixel = iota((256, 128), 0)
    moments = select_monomial(
        iota((256, 128), 1), (pixel & 15).astype(F32) - 7.5, (pixel >> 4).astype(F32) - 7.5
    )

    diagonal = (iota((8, 256), 1) & 7) == iota((8, 256), 0)

    def spread(coef, base):
        return jnp.concatenate(
            [
                jnp.where(
                    diagonal,
                    jnp.broadcast_to(coef[base + channel : base + channel + 1], (8, 256)),
                    0.0,
                )
                for channel in range(3)
            ],
            axis=0,
        )

    def forward(index, state):
        results = []
        for group in range(2):
            left, colors = state[2 * group : 2 * group + 2]
            coef = coef_of(group, index)
            turned = jnp.transpose(coef)
            alpha = jnp.exp2(dot_nn(turned.astype(BF16), basis))
            tones = [
                turned[:, 18 + ch : 19 + ch] + turned[:, 21 + ch : 22 + ch] for ch in range(3)
            ]
            rows = chunk_rows(group, index)
            alpha_s[rows, :] = alpha
            parts = []
            sums = [colors[ch * 8 : (ch + 1) * 8] for ch in range(3)]
            for slot in range(32):
                cut = slice(slot * 8, (slot + 1) * 8)
                weight = alpha[cut] * left
                left = left - weight
                parts.append(weight)
                sums = [sums[ch] + weight * tones[ch][cut] for ch in range(3)]
            colors = jnp.concatenate(sums, axis=0)
            weights = jnp.concatenate(parts, axis=0)
            weight_s[rows, :] = weights
            high, low = split(weights)
            parts_s[rows, 512:768] = high
            parts_s[rows, 768:1024] = low
            results += [left, colors]
        return tuple(results)

    start = (jnp.ones((8, 256), F32), jnp.zeros((24, 256), F32))
    state = start + start
    gather(0)
    for stage in range(4):
        if stage < 3:
            gather(stage + 1)
        for group in range(2):
            prepare(group * 32 + stage * 8)
        for step in range(4):
            state = forward(4 * stage + step, state)
    err_all = []
    for group in range(2):
        errors = state[2 * group + 1] - target_ref[group * 24 : (group + 1) * 24, :]
        squares = errors * errors
        total = jnp.sum(squares[0:8] + squares[8:16] + squares[16:24], axis=1, keepdims=True)
        loss_ref[group * 8 : (group + 1) * 8, :] = jnp.broadcast_to(total / 16.0, (8, 128))
        err_high, err_low = split(errors * 0.125)
        err_all.append(jnp.concatenate([err_high, err_low, err_high], axis=0))
        turned = jnp.transpose(
            jnp.concatenate(
                [jnp.zeros((8, 256), F32), err_high.astype(F32), err_low.astype(F32)]
                + [jnp.zeros((72, 256), F32)],
                axis=0,
            )
        )
        lane = iota((256, 128), 1)
        weights_s[group, 0:256, :] = moments
        weights_s[group, 256:512, :] = moments
        weights_s[group, 512:768, :] = turned.astype(BF16)
        weights_s[group, 768:1024, :] = jnp.where(lane < 32, turned, 0.0).astype(BF16)

    def backward(step, state):
        index = 15 - step
        results = []
        for group in range(2):
            behind = state[group]
            err_three = err_all[group]
            coef = coef_of(group, index)
            col_high = spread(coef, 18)
            col_low = spread(coef, 21)
            col_three = jnp.concatenate([col_high, col_high, col_low], axis=0)
            shades = dot_nn(jnp.transpose(col_three).astype(BF16), err_three)
            rows = chunk_rows(group, index)
            alpha = alpha_s[rows, :]
            weights = weight_s[rows, :]
            parts = []
            for slot in range(31, -1, -1):
                cut = slice(slot * 8, (slot + 1) * 8)
                gap = shades[cut] - behind
                parts.append(weights[cut] * gap)
                behind = behind + alpha[cut] * gap
            pulls = jnp.concatenate(parts[::-1], axis=0)
            pull_high, pull_low = split(pulls)
            parts_s[rows, 0:256] = pull_high
            parts_s[rows, 256:512] = pull_low
            results.append(behind)
        return tuple(results)

    zero = jnp.zeros((8, 256), F32)
    def reduce_pixels(stage):
        for group in range(2):
            first = group * 4096 + (3 - stage) * 1024
            sums = dot_nn(parts_s[first : first + 1024, :], weights_s[group])
            for part in range(8):
                turned = jnp.transpose(sums[part * 128 : (part + 1) * 128])
                base = (first // 128 + part) * 16
                tints = turned[8:32] + turned[32:56]
                sums_s[base : base + 8, :] = turned[0:8]
                for channel in range(3):
                    own = jnp.where(
                        diagonal[:, 0:128], tints[channel * 8 : (channel + 1) * 8], 0.0
                    )
                    sums_s[base + 8 + channel : base + 9 + channel, :] = jnp.sum(
                        own, axis=0, keepdims=True
                    )

    def scatter(stage, total):
        steps = []
        for group in range(2):
            first = group * 32 + (3 - stage) * 8
            feats, rel_u, rel_v, live = slot_values(first)
            conic_1, conic_2, conic_3 = (feats[2], feats[3], feats[4])

            def sums_of(index):
                return sums_s[pl.ds(first * 16 + index, 8, stride=16), :]

            m_xx, m_xy, m_yy, m_x, m_y, m_0 = [sums_of(index) for index in range(6)]
            s_x = m_x - rel_u * m_0
            s_y = m_y - rel_v * m_0
            s_xx = m_xx - 2.0 * rel_u * m_x + rel_u * rel_u * m_0
            s_yy = m_yy - 2.0 * rel_v * m_y + rel_v * rel_v * m_0
            s_xy = m_xy - rel_u * m_y - rel_v * m_x + rel_u * rel_v * m_0
            slot_grads = [
                conic_1 * s_x + conic_2 * s_y,
                conic_3 * s_y + conic_2 * s_x,
                -0.5 * s_xx,
                -s_xy,
                -0.5 * s_yy,
                m_0,
                sums_of(8),
                sums_of(9),
                sums_of(10),
            ]
            slot_grads = [jnp.where(live, grad, 0.0) for grad in slot_grads]
            steps.append(
                (
                    slot_grads,
                    slots_ref[first : first + 8, :],
                    slots_ref[64 + first : 72 + first, :],
                )
            )
        return total + scatter_rows(steps, 32)

    state = (zero, zero)
    collected = jnp.zeros((288, 256), F32)
    for stage in range(6):
        if stage >= 2:
            collected = scatter(stage - 2, collected)
        if 1 <= stage < 5:
            reduce_pixels(stage - 1)
        if stage < 4:
            for step in range(4):
                state = backward(4 * stage + step, state)
    for feature in range(9):
        piece = collected[feature * 32 : (feature + 1) * 32]
        table_s[feature * 64 : feature * 64 + 32, :] = piece[:, 0:128]
        table_s[feature * 64 + 32 : feature * 64 + 64, :] = piece[:, 128:256]
    table_s[576:640, :] = jnp.zeros((64, 128), F32)
    for part in range(5):
        out_ref[pl.ds(part, 128, stride=5), :] = jnp.transpose(
            table_s[part * 128 : (part + 1) * 128, :]
        )


def scatter_rows(steps, size):
    lanes, masked_high, masked_low = [], [], []
    for values, high, low in steps:
        tops = [value.astype(BF16).astype(F32) for value in values]
        rests = [value - top for value, top in zip(values, tops)]
        for row in range(8):
            cut = slice(row, row + 1)
            lanes.append(one_hot(high[cut], 256))
            match = low[cut] == iota((size, 128), 0)
            for parts, found in ((tops, masked_high), (rests, masked_low)):
                found.append(
                    jnp.concatenate(
                        [
                            jnp.where(match, jnp.broadcast_to(part[cut], (size, 128)), 0.0)
                            for part in parts
                        ],
                        axis=0,
                    ).astype(BF16)
                )
    masked = jnp.concatenate(
        [jnp.concatenate(masked_high, axis=1), jnp.concatenate(masked_low, axis=1)], axis=0
    )
    found = dot_nt(masked, jnp.concatenate(lanes, axis=1))
    return found[0 : 9 * size] + found[9 * size : 18 * size]


def render(arrived, slots, target):
    return pl.pallas_call(
        render_kernel,
        out_shape=(
            jax.ShapeDtypeStruct((640, 128), F32),
            jax.ShapeDtypeStruct((16, 128), F32),
        ),
        in_specs=[HBM, HBM, HBM],
        out_specs=(VMEM, VMEM),
        scratch_shapes=[
            pltpu.VMEM((TABLE_ROWS * 32, 256), BF16),
            pltpu.VMEM((640, 128), F32),
            pltpu.VMEM((64 * 24, 128), F32),
            pltpu.VMEM((8192, 256), F32),
            pltpu.VMEM((8192, 256), F32),
            pltpu.VMEM((64 * 16, 128), F32),
            pltpu.VMEM((576, 128), F32),
            pltpu.VMEM((2, 1024, 128), BF16),
            pltpu.VMEM((8192, 1024), BF16),
            pltpu.VMEM((192, 128), jnp.int32),
            pltpu.VMEM((48, 256), F32),
            pltpu.VMEM((640, 128), F32),
            pltpu.SemaphoreType.DMA((3,)),
        ],
        compiler_params=pltpu.CompilerParams(vmem_limit_bytes=56 * 1024 * 1024),
    )(arrived, slots, target)


def learn_rate(index):
    if index < 3:
        return 0.0016
    if index < 6:
        return 0.005
    if index < 10:
        return 0.001
    if index < 11:
        return 0.05
    return 0.0025 if index < 14 else 0.000125


def update_kernel(
    received_ref,
    wanted_ref,
    params_ref,
    one_ref,
    two_ref,
    new_params_ref,
    new_one_ref,
    new_two_ref,
    rows_s,
    grads_s,
    table_s,
):
    wanted = jnp.transpose(wanted_ref[...])[0:64]
    piece = wanted >> 7
    for part in range(5):
        turned = jnp.transpose(received_ref[pl.ds(part, 128, stride=5), :])
        table_s[part * 128 : (part + 1) * 128, :] = turned
    high = (piece >> 4) * 128 + (wanted & 127)
    low = piece & 15
    collected = jnp.zeros((144, 256), F32)
    for group in range(4):
        steps = []
        for first in (group * 16, group * 16 + 8):
            rows = slice(first, first + 8)
            values = [table_s[f * 64 + first : f * 64 + first + 8, :] for f in range(9)]
            steps.append((values, high[rows], low[rows]))
        collected = collected + scatter_rows(steps, 16)

    def grad_of(feature):
        part = collected[feature * 16 : (feature + 1) * 16]
        return jnp.concatenate([part[:, 0:128], part[:, 128:256]], axis=0)

    rows_first(params_ref, rows_s)

    def row(index):
        return rows_s[index * 32 : (index + 1) * 32, :]

    def put(index, value):
        grads_s[index * 32 : (index + 1) * 32, :] = value

    rows = [row(index) for index in range(10)]
    unused, pull_geometry = jax.vjp(geometry, rows)
    (geo_grads,) = pull_geometry(tuple(grad_of(feature) for feature in range(5)))
    put(10, grad_of(5) * (1.0 / (1.0 + jnp.exp(row(10)))))
    basis, pull_basis = jax.vjp(directions, rows[0], rows[1], rows[2])
    tints = [grad_of(6 + channel) for channel in range(3)]
    basis_grads = []
    for channel in range(3):
        put(11 + channel, SH_ZERO * tints[channel])
    for degree in range(1, 16):
        total = None
        for channel in range(3):
            index = 11 + 3 * degree + channel
            put(index, basis[degree - 1] * tints[channel])
            term = row(index) * tints[channel]
            total = term if total is None else total + term
        basis_grads.append(total)
    mean_grads = pull_basis(basis_grads)
    for index in range(10):
        put(index, geo_grads[index] + mean_grads[index] if index < 3 else geo_grads[index])

    fix_one = 1.0 / (1.0 - BETA_ONE**ADAM_STEP)
    fix_two = 1.0 / (1.0 - BETA_TWO**ADAM_STEP)
    for base in range(0, 59, 8):
        size = min(8, 59 - base)
        rate = jnp.zeros((size, 128), F32)
        for index in range(size):
            rate = jnp.where(iota((size, 128), 0) == index, learn_rate(base + index), rate)
        for piece in range(32):
            cut = (slice(base, base + size), slice(piece * 128, (piece + 1) * 128))
            grad = grads_s[pl.ds(base * 32 + piece, size, stride=32), :]
            one = BETA_ONE * one_ref[cut] + (1.0 - BETA_ONE) * grad
            two = BETA_TWO * two_ref[cut] + (1.0 - BETA_TWO) * grad * grad
            new_one_ref[cut] = one
            new_two_ref[cut] = two
            step = one * fix_one / (jnp.sqrt(two * fix_two) + ADAM_EPS)
            new_params_ref[cut] = params_ref[cut] - rate * step


def update(received, wanted, params, moment_one, moment_two):
    whole = jax.ShapeDtypeStruct((59, G_DEV), F32)
    return pl.pallas_call(
        update_kernel,
        out_shape=(whole, whole, whole),
        in_specs=[VMEM] * 5,
        out_specs=(VMEM, VMEM, VMEM),
        scratch_shapes=[
            pltpu.VMEM((59 * 32, 128), F32),
            pltpu.VMEM((59 * 32, 128), F32),
            pltpu.VMEM((640, 128), F32),
        ],
        compiler_params=pltpu.CompilerParams(vmem_limit_bytes=48 * 1024 * 1024),
    )(received, wanted, params, moment_one, moment_two)


def slot_keys(visible):
    keys = jnp.where(visible < 0, SENTINEL, visible)
    return jnp.transpose(keys.reshape(2, 8, 512), (0, 2, 1)).reshape(64, 128)


def exchange(array):
    flat = array.reshape(N_DEV, 1, -1)
    flat = lax.all_to_all(flat, "dev", split_axis=0, concat_axis=0, tiled=True)
    return flat.reshape(array.shape)


def shards(params, moment_one, moment_two, visible, counts, tile_pos, target):
    keys = slot_keys(visible)
    request = plan(visible)
    wanted = exchange(request)
    feats = project(params)
    centre = jnp.tile(tile_pos.reshape(2, 8), (1, 16))
    slots = find(request, keys, centre)
    colours = target.astype(F32).reshape(2, 8, 3, 256)
    colours = jnp.transpose(colours, (0, 2, 1, 3)).reshape(48, 256)
    arrived = exchange(serve(feats, wanted))
    grads, loss = render(arrived, slots, colours)
    received = exchange(grads)
    outs = update(received, wanted, params, moment_one, moment_two)
    return (loss[:, 0], *outs)


def solution(mesh):
    placed = (
        P(None, "dev"),
        P(None, "dev"),
        P(None, "dev"),
        P("dev", None),
        P("dev", None),
        P("dev"),
        P("dev", None, None),
    )
    return jax.shard_map(
        shards,
        mesh=mesh,
        in_specs=placed,
        out_specs=(P("dev"), P(None, "dev"), P(None, "dev"), P(None, "dev")),
        check_vma=False,
    )
```
